512 devices in a mesh: gx: 16 (over x, z_hi), gy: 32 (over y, z_lo, core).
Axes of the slice: x: 4, y: 8, z: 8 (z_hi: 4, z_lo: 2; z = z_hi * 2 + z_lo), core: 2. Of those that a mesh axis runs over, the one named last changes fastest.
Arguments:
- velocity: bfloat16 [3, 16, 64, 256, 128], P(None, 'gx', 'gy'), may hold values from -6 to 6
- position_code: int32 [16, 64, 256, 128], P('gx', 'gy'), may hold values from 0 to 511
- occupancy: int32 [16, 64, 256], P('gx', 'gy'), may hold values from 1 to 128
- shifts: int32 [4, 3], replicated, may hold values from 0 to 7
- axis_ids: int32 [4, 16, 64, 256], P(None, 'gx', 'gy'), may hold values from 0 to 31
Outputs:
- velocity_out: bfloat16 [3, 16, 64, 256, 128], P(None, 'gx', 'gy')
- cell_means: float32 [3, 16, 64, 256], P(None, 'gx', 'gy')
The draws below stay inside these ranges and needn't reach their ends.
All inputs are finite; a program needn't handle non-finite values.
Results may differ from the reference program's by a relative error of at most 0.001.
Values sent between devices are 32-bit elements; how exact they have to be, the bound alone decides.
No kernel may reach another device: no remote copies, remote signals or barrier semaphores. Data moves between devices by JAX's collectives and lax.ppermute only.
A program may use at most 64 MiB of HBM per device.

```python
import math
import jax
import jax.numpy as jnp
from jax import lax

SLOTS = 128
SUBDIV = 8
NAXES = 32
ITERS = 4
NX = 16
NY = 64
NZ = 256


def place_ends(result, rng, low, largest):
    place = [jax.random.randint(jax.random.fold_in(rng, axis), (), 0, length) for axis, length in enumerate(result.shape)]
    main_axis = result.shape.index(max(result.shape))
    neighbour = place[:main_axis] + [(place[main_axis] + 1) % result.shape[main_axis]] + place[main_axis + 1:]
    return result.at[tuple(place)].set(low).at[tuple(neighbour)].set(largest)


def steps_of(key, extent, shards, low, largest):
    gain, own = 1.0, jax.random.fold_in(key, 6)
    for position, parts in shards:
        draws = jnp.exp(jax.random.uniform(jax.random.fold_in(own, position), (parts,), jnp.float32, low / len(shards), largest / len(shards)))
        gain = gain * jnp.repeat(draws, extent[position] // parts).reshape([-1 if axis == position else 1 for axis in range(len(extent))])
    return gain


def noise(stream_key, dims, deviation, bound, cuts=(), kind=jnp.bfloat16):
    level = steps_of(stream_key, dims, cuts, -0.22, 0.18) if cuts else 1.0
    values = jax.random.normal(stream_key, dims, jnp.float32) * deviation * level
    return jnp.minimum(jnp.maximum(values, -bound), bound).astype(kind)


def setup_inputs(seed: int = 0) -> dict:
    streams_of = jax.random.split(jax.random.key(seed), 6)
    return {
        "velocity": noise(streams_of[0], (3, NX, NY, NZ, SLOTS), 1.0, 6.0, ((1, 16), (2, 32))),
        "position_code": place_ends(jax.random.randint(streams_of[1], (NX, NY, NZ, SLOTS), 0, SUBDIV * SUBDIV * SUBDIV), jax.random.fold_in(streams_of[1], 1), 0, (SUBDIV * SUBDIV * SUBDIV) - 1).astype(jnp.int32),
        "occupancy": place_ends(jax.random.randint(streams_of[2], (NX, NY, NZ), 1, SLOTS + 1), jax.random.fold_in(streams_of[2], 1), 1, SLOTS).astype(jnp.int32),
        "shifts": place_ends(jax.random.randint(streams_of[3], (ITERS, 3), 0, SUBDIV), jax.random.fold_in(streams_of[3], 1), 0, SUBDIV - 1).astype(jnp.int32),
        "axis_ids": place_ends(jax.random.randint(streams_of[4], (ITERS, NX, NY, NZ), 0, NAXES), jax.random.fold_in(streams_of[4], 1), 0, NAXES - 1).astype(jnp.int32),
    }


GOLDEN = 2.399963229728653
TURN_COS = math.cos(130.0 * math.pi / 180.0)
TURN_SIN = math.sin(130.0 * math.pi / 180.0)

def axis_table():
    ordinal = jnp.arange(NAXES).astype(jnp.float32)
    height = 1.0 - (2.0 * ordinal + 1.0) / NAXES
    radius = jnp.sqrt(1.0 - height * height)
    phases = ordinal * GOLDEN
    return jnp.stack([radius * jnp.cos(phases), radius * jnp.sin(phases), height])

def corner_steps(corner):
    return (corner // 4, corner // 2 % 2, corner % 2)

def corner_of(code_plane, shift_now):
    sub_x = code_plane // (SUBDIV * SUBDIV)
    sub_y = code_plane // SUBDIV % SUBDIV
    sub_z = code_plane % SUBDIV
    hop_x = (sub_x + shift_now[0] >= SUBDIV).astype(jnp.int32)
    hop_y = (sub_y + shift_now[1] >= SUBDIV).astype(jnp.int32)
    hop_z = (sub_z + shift_now[2] >= SUBDIV).astype(jnp.int32)
    return hop_x * 4 + hop_y * 2 + hop_z

def rotate_relative(velocity_in, mean_vec, normal):
    relative = velocity_in - mean_vec
    crossed = jnp.stack([normal[1] * relative[2] - normal[2] * relative[1], normal[2] * relative[0] - normal[0] * relative[2], normal[0] * relative[1] - normal[1] * relative[0]])
    along_axis = lax.optimization_barrier(jnp.sum(normal * relative, axis=0))
    return mean_vec + TURN_COS * relative + TURN_SIN * crossed + (1.0 - TURN_COS) * along_axis[None] * normal

def reference(velocity, position_code, occupancy, shifts, axis_ids):
    slot_index = jnp.arange(SLOTS, dtype=jnp.int32)

    def filled_of(occ_plane):
        return (slot_index < occ_plane[..., None]).astype(jnp.float32)

    def prepare(operands):
        x_plane, occ_plane = operands
        return x_plane.astype(jnp.float32) * filled_of(occ_plane)[None]
    velocities = lax.map(prepare, (jnp.transpose(velocity, (1, 0, 2, 3, 4)), occupancy))
    directions = axis_table()
    means_now = None
    for iteration in range(ITERS):
        shift_now = shifts[iteration]

        def deposit(operands):
            x_plane, code_plane, occ_plane = operands
            filled = filled_of(occ_plane)
            corner_idx = corner_of(code_plane, shift_now)
            pieces = []
            for corner in range(8):
                chosen = filled * (corner_idx == corner).astype(jnp.float32)
                pieces.append(jnp.concatenate([lax.optimization_barrier(jnp.sum(x_plane * chosen[None], axis=-1)), lax.optimization_barrier(jnp.sum(chosen, axis=-1))[None]], axis=0))
            return jnp.stack(pieces)
        deposits = lax.map(deposit, (velocities, position_code, occupancy))
        totals = jnp.zeros((NX, 4, NY, NZ), jnp.float32)
        for corner in range(8):
            step_x, step_y, step_z = corner_steps(corner)
            totals = totals + jnp.roll(deposits[:, corner], (step_x, step_y, step_z), axis=(0, 2, 3))
        means_now = totals[:, :3] / jnp.maximum(totals[:, 3:4], 1.0)
        normal = jnp.transpose(directions[:, axis_ids[iteration]], (1, 0, 2, 3))
        packed = jnp.concatenate([means_now, normal], axis=1)
        looked = jnp.stack([jnp.roll(packed, tuple((-s for s in corner_steps(corner))), axis=(0, 2, 3)) for corner in range(8)], axis=1)

        def collide(operands):
            x_plane, code_plane, occ_plane, look_plane = operands
            filled = filled_of(occ_plane)
            corner_idx = corner_of(code_plane, shift_now)
            gathered = jnp.zeros((6,) + code_plane.shape, jnp.float32)
            for corner in range(8):
                gathered = gathered + (corner_idx == corner).astype(jnp.float32)[None] * look_plane[corner][..., None]
            return rotate_relative(x_plane, gathered[:3], gathered[3:]) * filled[None]
        velocities = lax.map(collide, (velocities, position_code, occupancy, looked))
    return (jnp.transpose(velocities, (1, 0, 2, 3, 4)).astype(jnp.bfloat16), jnp.transpose(means_now, (1, 0, 2, 3)))
```

```python
import functools
import math

import jax
import jax.numpy as jnp
import numpy as np
from jax import lax
from jax.experimental import pallas as pl
from jax.experimental.pallas import tpu as pltpu
from jax.sharding import PartitionSpec as P

SUBDIV = 8
NAXES = 32
ITERS = 4
GOLDEN = 2.399963229728653
TURN_COS = math.cos(130.0 * math.pi / 180.0)
TURN_SIN = math.sin(130.0 * math.pi / 180.0)
ALONG = (1.0 - TURN_COS) / (TURN_SIN * TURN_SIN)

F32 = jnp.float32
CHUNK = 32


def axis_table():
    ordinal = np.arange(NAXES, dtype=np.float64)
    height = 1.0 - (2.0 * ordinal + 1.0) / NAXES
    radius = np.sqrt(1.0 - height * height)
    phases = ordinal * GOLDEN
    return TURN_SIN * np.stack([radius * np.cos(phases), radius * np.sin(phases), height])


AXES = axis_table()


def is_odd(axis):
    return lax.rem(lax.axis_index(axis), 2) == 1


def hop_masks(code, shifts_ref, step):
    hop_x = code >= (SUBDIV - shifts_ref[step, 0]) * (SUBDIV * SUBDIV)
    hop_y = (code & (SUBDIV * SUBDIV - 1)) >= (SUBDIV - shifts_ref[step, 1]) * SUBDIV
    hop_z = (code & (SUBDIV - 1)) >= SUBDIV - shifts_ref[step, 2]
    return hop_x, hop_y, hop_z


def deposit(vel_ref, code_ref, shifts_ref, step, mom_ref, sums_ref):
    for col in range(2):
        for half in range(2):
            lanes = slice(half * 128, half * 128 + 128)

            def body(i, acc):
                rows = pl.ds(pl.multiple_of(i * 8, 8), 8)
                code = code_ref[col, rows, lanes]
                hop_x, hop_y, hop_z = hop_masks(code, shifts_ref, step)
                parts = [vel_ref[comp * 2 + col, rows, lanes] for comp in range(3)]
                parts.append(jnp.where(code >= 0, 1.0, 0.0))
                out = list(acc)
                for comp, value in enumerate(parts):
                    with_x = jnp.where(hop_x, value, 0.0)
                    with_y = jnp.where(hop_y, value, 0.0)
                    with_xy = jnp.where(hop_y, with_x, 0.0)
                    for pair, base in ((0, value), (2, with_y), (4, with_x), (6, with_xy)):
                        at = comp * 8 + pair
                        out[at] = out[at] + base
                        out[at + 1] = out[at + 1] + jnp.where(hop_z, base, 0.0)
                return tuple(out)

            zero = jnp.zeros((8, 128), F32)
            acc = lax.fori_loop(0, 16, body, (zero,) * 32, unroll=2)
            for comp in range(4):
                for moment in range(8):
                    row = (col * 8 + moment) * 8 + comp
                    mom_ref[row : row + 1, lanes] = jnp.sum(acc[comp * 8 + moment], axis=0, keepdims=True)
    pieces = {}
    for col in range(2):
        def moment_of(moment):
            row = (col * 8 + moment) * 8
            return mom_ref[row : row + 8, :]

        quads = {}
        for moment in (0, 2, 4, 6):
            up = moment_of(moment + 1)
            quads[moment] = moment_of(moment) - up + pltpu.roll(up, 1, 1)
        pieces[col, 1, 1] = quads[6]
        pieces[col, 1, 0] = quads[4] - quads[6]
        pieces[col, 0, 1] = quads[2] - quads[6]
        pieces[col, 0, 0] = quads[0] - quads[2] - quads[4] + quads[6]
    for hop in range(2):
        columns = (pieces[0, hop, 0], pieces[0, hop, 1] + pieces[1, hop, 0], pieces[1, hop, 1])
        for at, piece in enumerate(columns):
            row = (hop * 3 + at) * 4
            sums_ref[row : row + 4, :] = piece[0:4, :]


def fill_messages_y(sums_ref, odd_ref, even_ref):
    odd = is_odd("gy")
    for hop in range(2):
        left = sums_ref[hop * 12 : hop * 12 + 4, :]
        right = sums_ref[hop * 12 + 8 : hop * 12 + 12, :]
        odd_ref[hop * 4 : hop * 4 + 4, :] = jnp.where(odd, right, left)
        even_ref[hop * 4 : hop * 4 + 4, :] = jnp.where(odd, left, right)


def start_kernel(shifts_ref, vel_in_ref, code_in_ref, occ_ref, ids_ref, vel_ref, code_ref, sums_ref, odd_ref, even_ref, mom_ref):
    slot = lax.broadcasted_iota(jnp.int32, (128, 256), 0)
    for col in range(2):
        filled = slot < occ_ref[col : col + 1, :]
        code_ref[col] = jnp.where(filled, code_in_ref[col].T, -1)
        for comp in range(3):
            vel_ref[comp * 2 + col] = jnp.where(filled, vel_in_ref[comp * 2 + col].astype(F32).T, 0.0)
    mom_ref[...] = jnp.zeros_like(mom_ref)
    deposit(vel_ref, code_ref, shifts_ref, 0, mom_ref, sums_ref)
    fill_messages_y(sums_ref, odd_ref, even_ref)
    for step in range(ITERS):
        ids = ids_ref[step * 2 : step * 2 + 1, :].astype(F32)
        odd_ref[8 + step : 9 + step, :] = ids
        even_ref[8 + step : 9 + step, :] = ids


def middle_kernel(first, *refs):
    if first:
        sums_ref, from_odd_ref, from_even_ref, ids_ref, out_ref, odd_ref, even_ref = refs
    else:
        sums_ref, from_odd_ref, from_even_ref, out_ref, odd_ref, even_ref = refs
    odd_y, odd_x = is_odd("gy"), is_odd("gx")
    out_ref[0:24, :] = sums_ref[...]
    for hop in range(2):
        rows = slice(hop * 4, hop * 4 + 4)
        by_odd, by_even = from_odd_ref[rows, :], from_even_ref[rows, :]
        left = slice(hop * 12, hop * 12 + 4)
        right = slice(hop * 12 + 8, hop * 12 + 12)
        out_ref[left, :] = out_ref[left, :] + jnp.where(odd_y, by_even, by_odd)
        out_ref[right, :] = out_ref[right, :] + jnp.where(odd_y, by_odd, by_even)
    low, high = out_ref[0:12, :], out_ref[12:24, :]
    odd_ref[0:12, :] = jnp.where(odd_x, high, low)
    even_ref[0:12, :] = jnp.where(odd_x, low, high)
    if first:
        for step in range(ITERS):
            row = 24 + step * 3
            out_ref[row : row + 2, :] = ids_ref[step * 2 : step * 2 + 2, :].astype(F32)
            by_odd, by_even = from_odd_ref[8 + step : 9 + step, :], from_even_ref[8 + step : 9 + step, :]
            out_ref[row + 2 : row + 3, :] = jnp.where(odd_y, by_odd, by_even)
        own = out_ref[24:36, :]
        odd_ref[12:24, :] = own
        even_ref[12:24, :] = own


def totals_and_axes(step, sums_ref, from_odd_ref, from_even_ref, ids, mean_ref, axis_ref):
    odd_x = is_odd("gx")
    by_odd, by_even = from_odd_ref[0:12, :], from_even_ref[0:12, :]
    mean_ref[0, 0:12, :] = sums_ref[0:12, :] + jnp.where(odd_x, by_even, by_odd)
    mean_ref[0, 12:24, :] = sums_ref[12:24, :] + jnp.where(odd_x, by_odd, by_even)
    for cell in range(6):
        count = jnp.maximum(mean_ref[0, cell * 4 + 3 : cell * 4 + 4, :], 1.0)
        mean_ref[0, cell * 4 : cell * 4 + 3, :] = mean_ref[0, cell * 4 : cell * 4 + 3, :] / count
    mean_ref[1] = pltpu.roll(mean_ref[0], 255, 1)
    axes = [jnp.zeros((8, 256), F32) for _ in range(3)]
    for k in range(NAXES):
        match = ids == float(k)
        axes = [jnp.where(match, float(AXES[comp, k]), axes[comp]) for comp in range(3)]
    for comp in range(3):
        axis_ref[0, comp] = axes[comp]
        axis_ref[1, comp] = pltpu.roll(axes[comp], 255, 1)


def rotate(step, vel_ref, code_ref, shifts_ref, mean_ref, axis_ref, out_ref):
    for col in range(2):
        for half in range(2):
            lanes = slice(half * 128, half * 128 + 128)

            def body(i, carry):
                rows = pl.ds(pl.multiple_of(i * CHUNK, CHUNK), CHUNK)
                code = code_ref[col, rows, lanes]
                hop_x, hop_y, hop_z = hop_masks(code, shifts_ref, step)

                def pick(row_of):
                    by_x = []
                    for step_x in range(2):
                        by_y = []
                        for step_y in range(2):
                            cell = step_x * 3 + col + step_y
                            by_y.append(jnp.where(hop_z, row_of(1, cell), row_of(0, cell)))
                        by_x.append(jnp.where(hop_y, by_y[1], by_y[0]))
                    return jnp.where(hop_x, by_x[1], by_x[0])

                mean, rel, axis = [], [], []
                for comp in range(3):
                    mean.append(pick(lambda z, cell: mean_ref[z, cell * 4 + comp : cell * 4 + comp + 1, lanes]))
                    axis.append(pick(lambda z, cell: axis_ref[z, comp, cell : cell + 1, lanes]))
                    rel.append(vel_ref[comp * 2 + col, rows, lanes] - mean[comp])
                along = (axis[0] * rel[0] + axis[1] * rel[1] + axis[2] * rel[2]) * ALONG
                filled = code >= 0
                for comp in range(3):
                    b, c = (comp + 1) % 3, (comp + 2) % 3
                    value = mean[comp] + TURN_COS * rel[comp] + (axis[b] * rel[c] - axis[c] * rel[b]) + along * axis[comp]
                    out_ref[comp * 2 + col, rows, lanes] = jnp.where(filled, value, 0.0)
                return carry

            lax.fori_loop(0, 128 // CHUNK, body, 0)


def step_kernel(step, *refs):
    if step == 0:
        shifts_ref, vel_ref, code_ref, sums_ref, from_odd_ref, from_even_ref, *refs = refs
        out_ref, ids_ref, new_ref, odd_ref, even_ref, mom_ref, mean_ref, axis_ref = refs
        odd_x = is_odd("gx")
        ids_ref[...] = jnp.zeros_like(ids_ref)
        for t in range(ITERS):
            ids_ref[t * 8 : t * 8 + 3, :] = sums_ref[24 + t * 3 : 27 + t * 3, :]
            rows = slice(12 + t * 3, 15 + t * 3)
            ids_ref[t * 8 + 3 : t * 8 + 6, :] = jnp.where(odd_x, from_odd_ref[rows, :], from_even_ref[rows, :])
    else:
        shifts_ref, vel_ref, code_ref, sums_ref, from_odd_ref, from_even_ref, ids_ref, *refs = refs
        if step < ITERS - 1:
            out_ref, new_ref, odd_ref, even_ref, mom_ref, mean_ref, axis_ref = refs
        else:
            final_ref, final_means_ref, out_ref, mean_ref, axis_ref = refs
    ids = ids_ref[step * 8 : step * 8 + 8, :]
    totals_and_axes(step, sums_ref, from_odd_ref, from_even_ref, ids, mean_ref, axis_ref)
    rotate(step, vel_ref, code_ref, shifts_ref, mean_ref, axis_ref, out_ref)
    if step < ITERS - 1:
        mom_ref[...] = jnp.zeros_like(mom_ref)
        deposit(out_ref, code_ref, shifts_ref, step + 1, mom_ref, new_ref)
        fill_messages_y(new_ref, odd_ref, even_ref)
    else:
        for at in range(6):
            final_ref[at] = out_ref[at].T.astype(jnp.bfloat16)
        for comp in range(3):
            for col in range(2):
                final_means_ref[comp * 2 + col : comp * 2 + col + 1, :] = mean_ref[0, col * 4 + comp : col * 4 + comp + 1, :]


VMEM = pl.BlockSpec(memory_space=pltpu.VMEM)
SMEM = pl.BlockSpec(memory_space=pltpu.SMEM)


def call(kernel, name, n_in, shapes, scratch, smem=True):
    return pl.pallas_call(
        kernel,
        out_shape=[jax.ShapeDtypeStruct(s, d) for s, d in shapes],
        in_specs=([SMEM] if smem else []) + [VMEM] * n_in,
        out_specs=[VMEM] * len(shapes),
        scratch_shapes=scratch,
        compiler_params=pltpu.CompilerParams(vmem_limit_bytes=16 * 1024 * 1024),
        name=name,
    )


def swap(odd, even, axis):
    count = lax.axis_size(axis)
    evens = [(s, s ^ 1) for s in range(count)]
    odds = [(s, (((s - 1) % count ^ 1) + 1) % count) for s in range(count)]
    from_even = lax.ppermute(even, axis, evens)
    from_odd = lax.ppermute(odd, axis, odds)
    return from_odd, from_even


def on_device(velocity, position_code, occupancy, shifts, axis_ids):
    vel_in = velocity.reshape(6, 256, 128)
    code_in = position_code.reshape(2, 256, 128)
    occ = occupancy.reshape(2, 256)
    ids_in = axis_ids.reshape(8, 256)
    vel_shape, code_shape = ((6, 128, 256), F32), ((2, 128, 256), jnp.int32)
    moments = pltpu.VMEM((128, 256), F32)
    means = pltpu.VMEM((2, 24, 256), F32)
    axes = pltpu.VMEM((2, 3, 8, 256), F32)

    vel, code, sums, odd, even = call(
        start_kernel, "start", 4,
        [vel_shape, code_shape, ((24, 256), F32), ((12, 256), F32), ((12, 256), F32)], [moments],
    )(shifts, vel_in, code_in, occ, ids_in)
    ids = None
    for step in range(ITERS):
        first = step == 0
        from_odd, from_even = swap(odd, even, "gy")
        rows = 24 if first else 12
        middle = call(
            functools.partial(middle_kernel, first), f"middle{step}", 4 if first else 3,
            [((40 if first else 24, 256), F32), ((rows, 256), F32), ((rows, 256), F32)], [], smem=False,
        )
        sums, odd, even = middle(sums, from_odd, from_even, *((ids_in,) if first else ()))
        from_odd, from_even = swap(odd, even, "gx")
        body = functools.partial(step_kernel, step)
        args = [shifts, vel, code, sums, from_odd, from_even] + ([] if first else [ids])
        message = ((8, 256), F32)
        if step < ITERS - 1:
            shapes = [vel_shape] + ([((32, 256), F32)] if first else []) + [((24, 256), F32), message, message]
            vel, *rest = call(body, f"step{step}", len(args) - 1, shapes, [moments, means, axes])(*args)
            if first:
                ids, *rest = rest
            sums, odd, even = rest
        else:
            shapes = [((6, 256, 128), jnp.bfloat16), ((6, 256), F32)]
            scratch = [pltpu.VMEM((6, 128, 256), F32), means, axes]
            out, out_means = call(body, f"step{step}", len(args) - 1, shapes, scratch)(*args)
    return out.reshape(velocity.shape), out_means.reshape(3, *occupancy.shape)


def solution(mesh):
    in_specs = (
        P(None, "gx", "gy", None, None),
        P("gx", "gy", None, None),
        P("gx", "gy", None),
        P(),
        P(None, "gx", "gy", None),
    )
    out_specs = (P(None, "gx", "gy", None, None), P(None, "gx", "gy", None))
    return jax.shard_map(
        on_device, mesh=mesh, in_specs=in_specs, out_specs=out_specs, check_vma=False
    )
```

```python
import functools
import math

import jax
import jax.numpy as jnp
import numpy as np
from jax import lax
from jax.experimental import pallas as pl
from jax.experimental.pallas import tpu as pltpu
from jax.sharding import PartitionSpec as P

SUBDIV = 8
NAXES = 32
ITERS = 4
GOLDEN = 2.399963229728653
TURN_COS = math.cos(130.0 * math.pi / 180.0)
TURN_SIN = math.sin(130.0 * math.pi / 180.0)
ALONG = (1.0 - TURN_COS) / (TURN_SIN * TURN_SIN)

F32 = jnp.float32
CHUNK = 32
WIDE = 48


def axis_table():
    ordinal = np.arange(NAXES, dtype=np.float64)
    height = 1.0 - (2.0 * ordinal + 1.0) / NAXES
    radius = np.sqrt(1.0 - height * height)
    phases = ordinal * GOLDEN
    return TURN_SIN * np.stack([radius * np.cos(phases), radius * np.sin(phases), height])


AXES = axis_table()


def is_odd(axis):
    return lax.rem(lax.axis_index(axis), 2) == 1


def hop_masks(code, shifts_ref, step):
    hop_x = code >= (SUBDIV - shifts_ref[step, 0]) * (SUBDIV * SUBDIV)
    hop_y = (code & (SUBDIV * SUBDIV - 1)) >= (SUBDIV - shifts_ref[step, 1]) * SUBDIV
    hop_z = (code & (SUBDIV - 1)) >= SUBDIV - shifts_ref[step, 2]
    return hop_x, hop_y, hop_z


def slot_sums(values, count, col, lanes, code_ref, shifts_ref, step, mom_ref):
    def body(i, acc):
        rows = pl.ds(pl.multiple_of(i * 8, 8), 8)
        code = code_ref[col, rows, lanes]
        hop_x, hop_y, hop_z = hop_masks(code, shifts_ref, step)
        out = list(acc)
        for comp, value in enumerate(values(rows, code)):
            with_x = jnp.where(hop_x, value, 0.0)
            with_y = jnp.where(hop_y, value, 0.0)
            with_xy = jnp.where(hop_y, with_x, 0.0)
            for pair, base in ((0, value), (2, with_y), (4, with_x), (6, with_xy)):
                at = comp * 8 + pair
                out[at] = out[at] + base
                out[at + 1] = out[at + 1] + jnp.where(hop_z, base, 0.0)
        return tuple(out)

    zero = jnp.zeros((8, 128), F32)
    acc = lax.fori_loop(0, 16, body, (zero,) * (8 * count), unroll=2)
    for comp in range(count):
        for moment in range(8):
            row = (col * 8 + moment) * 8 + comp
            mom_ref[row : row + 1, lanes] = jnp.sum(acc[comp * 8 + moment], axis=0, keepdims=True)


def blocks():
    for col in range(2):
        for half in range(2):
            yield col, slice(half * 128, half * 128 + 128)


def deposit(vel_ref, code_ref, shifts_ref, step, mom_ref, counted):
    for col, lanes in blocks():

        def values(rows, code):
            parts = [vel_ref[comp * 2 + col, rows, lanes] for comp in range(3)]
            return parts + ([jnp.where(code >= 0, 1.0, 0.0)] if counted else [])

        slot_sums(values, 4 if counted else 3, col, lanes, code_ref, shifts_ref, step, mom_ref)


def cell_sums(moment_of, sums_ref):
    pieces = {}
    for col in range(2):
        quads = {}
        for moment in (0, 2, 4, 6):
            up = moment_of(col, moment + 1)
            quads[moment] = moment_of(col, moment) - up + pltpu.roll(up, 1, 1)
        pieces[col, 1, 1] = quads[6]
        pieces[col, 1, 0] = quads[4] - quads[6]
        pieces[col, 0, 1] = quads[2] - quads[6]
        pieces[col, 0, 0] = quads[0] - quads[2] - quads[4] + quads[6]
    for hop in range(2):
        columns = (pieces[0, hop, 0], pieces[0, hop, 1] + pieces[1, hop, 0], pieces[1, hop, 1])
        for at, piece in enumerate(columns):
            row = (hop * 3 + at) * 4
            sums_ref[row : row + 4, :] = piece[0:4, :]


def stored_moment(mom_ref):
    def moment_of(col, moment):
        row = (col * 8 + moment) * 8
        return mom_ref[row : row + 8, :]

    return moment_of


def fill_messages_y(sums_ref, odd_ref, even_ref):
    odd = is_odd("gy")
    for hop in range(2):
        left = sums_ref[hop * 12 : hop * 12 + 4, :]
        right = sums_ref[hop * 12 + 8 : hop * 12 + 12, :]
        odd_ref[hop * 4 : hop * 4 + 4, :] = jnp.where(odd, right, left)
        even_ref[hop * 4 : hop * 4 + 4, :] = jnp.where(odd, left, right)


def start_kernel(shifts_hbm, vel_hbm, code_hbm, occ_hbm, ids_hbm, vel_ref, code_ref, sums_ref, odd_ref, even_ref, mom_ref, vel_in_ref, code_in_ref, occ_ref, ids_ref, shifts_ref, sems):
    fetch_shifts = pltpu.make_async_copy(shifts_hbm, shifts_ref, sems.at[10])
    fetch_occ = pltpu.make_async_copy(occ_hbm, occ_ref, sems.at[8])
    fetch_ids = pltpu.make_async_copy(ids_hbm, ids_ref, sems.at[9])
    copies = []
    for col in range(2):
        copies.append(pltpu.make_async_copy(code_hbm.at[col], code_in_ref.at[col], sems.at[col]))
    for at in range(6):
        copies.append(pltpu.make_async_copy(vel_hbm.at[at], vel_in_ref.at[at], sems.at[2 + at]))
    fetch_occ.start()
    for copy in copies:
        copy.start()
    fetch_ids.start()
    fetch_shifts.start()
    mom_ref[...] = jnp.zeros_like(mom_ref)
    slot = lax.broadcasted_iota(jnp.int32, (128, 256), 0)
    fetch_occ.wait()
    for col in range(2):
        filled = slot < occ_ref[col : col + 1, :]
        copies[col].wait()
        code_ref[col] = jnp.where(filled, code_in_ref[col].T, -1)
    for comp in range(3):
        for col in range(2):
            at = comp * 2 + col
            copies[2 + at].wait()
            filled = code_ref[col] >= 0
            vel_ref[at] = jnp.where(filled, vel_in_ref[at].astype(F32).T, 0.0)
    fetch_ids.wait()
    fetch_shifts.wait()
    for step in range(ITERS):
        ids = ids_ref[step, 0:1, :].astype(F32)
        odd_ref[8 + step : 9 + step, :] = ids
        even_ref[8 + step : 9 + step, :] = ids
    deposit(vel_ref, code_ref, shifts_ref, 0, mom_ref, True)
    cell_sums(stored_moment(mom_ref), sums_ref)
    fill_messages_y(sums_ref, odd_ref, even_ref)


def middle_kernel(first, *refs):
    if first:
        sums_ref, from_odd_ref, from_even_ref, ids_ref, out_ref, odd_ref, even_ref = refs
    else:
        sums_ref, from_odd_ref, from_even_ref, out_ref, odd_ref, even_ref = refs
    odd_y, odd_x = is_odd("gy"), is_odd("gx")
    out_ref[0:24, :] = sums_ref[...]
    for hop in range(2):
        rows = slice(hop * 4, hop * 4 + 4)
        by_odd, by_even = from_odd_ref[rows, :], from_even_ref[rows, :]
        left = slice(hop * 12, hop * 12 + 4)
        right = slice(hop * 12 + 8, hop * 12 + 12)
        out_ref[left, :] = out_ref[left, :] + jnp.where(odd_y, by_even, by_odd)
        out_ref[right, :] = out_ref[right, :] + jnp.where(odd_y, by_odd, by_even)
    low, high = out_ref[0:12, :], out_ref[12:24, :]
    odd_ref[0:12, :] = jnp.where(odd_x, high, low)
    even_ref[0:12, :] = jnp.where(odd_x, low, high)
    if first:
        for step in range(ITERS):
            row = 24 + step * 3
            out_ref[row : row + 2, :] = ids_ref[step].astype(F32)
            by_odd, by_even = from_odd_ref[8 + step : 9 + step, :], from_even_ref[8 + step : 9 + step, :]
            out_ref[row + 2 : row + 3, :] = jnp.where(odd_y, by_odd, by_even)
        own = out_ref[24:36, :]
        odd_ref[12:24, :] = own
        even_ref[12:24, :] = own


def cell_means(sums_ref, from_odd_ref, from_even_ref, work_ref, tot_ref):
    odd_x = is_odd("gx")
    by_odd, by_even = from_odd_ref[0:12, :], from_even_ref[0:12, :]
    work_ref[0:12, :] = sums_ref[0:12, :] + jnp.where(odd_x, by_even, by_odd)
    work_ref[12:24, :] = sums_ref[12:24, :] + jnp.where(odd_x, by_odd, by_even)
    tot_ref[...] = jnp.zeros_like(tot_ref)
    for cell in range(6):
        for comp in range(4):
            tot_ref[comp, cell : cell + 1, :] = work_ref[cell * 4 + comp : cell * 4 + comp + 1, :]
    count = jnp.maximum(tot_ref[3], 1.0)
    return [tot_ref[comp] / count for comp in range(3)]


def cell_axes(ids):
    axes = [jnp.zeros((8, 256), F32) for _ in range(3)]
    for k in range(NAXES):
        match = ids == float(k)
        axes = [jnp.where(match, float(AXES[comp, k]), axes[comp]) for comp in range(3)]
    return axes


def turned(axis, vec):
    along = (axis[0] * vec[0] + axis[1] * vec[1] + axis[2] * vec[2]) * ALONG
    out = []
    for comp in range(3):
        b, c = (comp + 1) % 3, (comp + 2) % 3
        out.append(TURN_COS * vec[comp] + (axis[b] * vec[c] - axis[c] * vec[b]) + along * axis[comp])
    return out


def next_z(value):
    return pltpu.roll(value, 255, 1)


def store_cells(table_ref, parts):
    for cell in range(6):
        for comp, part in enumerate(parts):
            table_ref[0, cell * 8 + comp : cell * 8 + comp + 1, :] = part[cell : cell + 1, :]
    table_ref[1] = next_z(table_ref[0])


def pick(table_ref, comp, col, lanes, masks):
    hop_x, hop_y, hop_z = masks
    by_x = []
    for step_x in range(2):
        by_y = []
        for step_y in range(2):
            row = (step_x * 3 + col + step_y) * 8 + comp
            by_y.append(jnp.where(hop_z, table_ref[1, row : row + 1, lanes], table_ref[0, row : row + 1, lanes]))
        by_x.append(jnp.where(hop_y, by_y[1], by_y[0]))
    return jnp.where(hop_x, by_x[1], by_x[0])


def over_slots(body):
    def run(i, carry):
        body(pl.ds(pl.multiple_of(i * CHUNK, CHUNK), CHUNK))
        return carry

    lax.fori_loop(0, 128 // CHUNK, run, 0)


def first_kernel(shifts_ref, vel_ref, code_ref, sums_ref, from_odd_ref, from_even_ref, joint_ref, out_ref, ids_ref, new_ref, odd_ref, even_ref, mom_ref, work_ref, tot_ref, table_ref):
    odd_x = is_odd("gx")
    ids_ref[...] = jnp.zeros_like(ids_ref)
    for t in range(ITERS):
        ids_ref[t * 8 : t * 8 + 3, :] = sums_ref[24 + t * 3 : 27 + t * 3, :]
        rows = slice(12 + t * 3, 15 + t * 3)
        ids_ref[t * 8 + 3 : t * 8 + 6, :] = jnp.where(odd_x, from_odd_ref[rows, :], from_even_ref[rows, :])
    means = cell_means(sums_ref, from_odd_ref, from_even_ref, work_ref, tot_ref)
    axes = cell_axes(ids_ref[0:8, :])
    turn = turned(axes, means)
    table_ref[...] = jnp.zeros_like(table_ref)
    store_cells(table_ref, axes + [means[comp] - turn[comp] for comp in range(3)])
    for col, lanes in blocks():

        def body(rows):
            code = code_ref[col, rows, lanes]
            masks = hop_masks(code, shifts_ref, 0)
            vel = [vel_ref[comp * 2 + col, rows, lanes] for comp in range(3)]
            turn = turned([pick(table_ref, comp, col, lanes, masks) for comp in range(3)], vel)
            filled = code >= 0
            for comp in range(3):
                value = turn[comp] + pick(table_ref, 3 + comp, col, lanes, masks)
                out_ref[comp * 2 + col, rows, lanes] = jnp.where(filled, value, 0.0)

        over_slots(body)
    mom_ref[...] = jnp.zeros_like(mom_ref)
    deposit(out_ref, code_ref, shifts_ref, 1, mom_ref, True)
    cell_sums(stored_moment(mom_ref), new_ref)
    fill_messages_y(new_ref, odd_ref, even_ref)


def joint_kernel(shifts_ref, code_ref, *out_refs):
    for t, out_ref in zip((1, 2), out_refs):
        out_ref[...] = jnp.zeros_like(out_ref)
        for col, lanes in blocks():

            def body(i, acc):
                rows = pl.ds(pl.multiple_of(i * 8, 8), 8)
                code = code_ref[col, rows, lanes]
                now, later = hop_masks(code, shifts_ref, t), hop_masks(code, shifts_ref, t + 1)
                out, at = list(acc), 0
                one = jnp.where(code >= 0, 1.0, 0.0)
                for by_x in (one, jnp.where(now[0], one, 0.0), jnp.where(later[0], one, 0.0)):
                    for by_y in (by_x, jnp.where(now[1], by_x, 0.0), jnp.where(later[1], by_x, 0.0)):
                        for by_z in (by_y, jnp.where(now[2], by_y, 0.0), jnp.where(later[2], by_y, 0.0)):
                            out[at] = out[at] + by_z
                            at += 1
                return tuple(out)

            acc = lax.fori_loop(0, 16, body, (jnp.zeros((8, 128), F32),) * 27, unroll=2)
            for at in range(27):
                out_ref[col * 27 + at : col * 27 + at + 1, lanes] = jnp.sum(acc[at], axis=0, keepdims=True)


def turn_kernel(step, *refs):
    sums = step < ITERS - 1
    if step == 1:
        shifts_ref, code_ref, ids_ref, vel_ref, *refs = refs
    else:
        shifts_ref, code_ref, ids_ref, vel_ref, last_ref, *refs = refs
    if sums:
        out_ref, axes_ref, mom_ref, table_ref = refs
    else:
        out_ref, axes_ref, table_ref = refs
    axes = cell_axes(ids_ref[step * 8 : step * 8 + 8, :])
    for comp in range(3):
        axes_ref[comp] = axes[comp]
    table_ref[...] = jnp.zeros_like(table_ref)
    store_cells(table_ref, axes)
    for col, lanes in blocks():

        def body(rows):
            code = code_ref[col, rows, lanes]
            vel = [vel_ref[comp * 2 + col, rows, lanes] for comp in range(3)]
            if step > 1:
                masks = hop_masks(code, shifts_ref, step - 1)
                filled = code >= 0
                vel = [jnp.where(filled, vel[comp] + pick(last_ref, comp, col, lanes, masks), 0.0) for comp in range(3)]
            masks = hop_masks(code, shifts_ref, step)
            turn = turned([pick(table_ref, comp, col, lanes, masks) for comp in range(3)], vel)
            for comp in range(3):
                out_ref[comp * 2 + col, rows, lanes] = turn[comp]

        over_slots(body)
    if sums:
        mom_ref[...] = jnp.zeros_like(mom_ref)
        deposit(out_ref, code_ref, shifts_ref, step + 1, mom_ref, False)


def shift_kernel(step, shifts_ref, sums_ref, from_odd_ref, from_even_ref, axes_ref, mom_ref, joint_ref, shift_ref, new_ref, odd_ref, even_ref, work_ref, tot_ref, next_ref):
    means = cell_means(sums_ref, from_odd_ref, from_even_ref, work_ref, tot_ref)
    turn = turned([axes_ref[comp] for comp in range(3)], means)
    shift_ref[...] = jnp.zeros_like(shift_ref)
    ones = jnp.ones((8, 256), F32)
    store_cells(shift_ref, [means[comp] - turn[comp] for comp in range(3)] + [ones])
    nested = []
    for dim in range(3):
        nested.append(jnp.where(shifts_ref[step, dim] <= shifts_ref[step + 1, dim], 1, 2))
    for col in range(2):
        parts = {}
        for corner in range(8):
            cell = (corner >> 2) * 3 + col + (corner >> 1 & 1)
            parts[corner] = shift_ref[corner & 1, cell * 8 : cell * 8 + 8, :]
        for bit in (1, 2, 4):
            for corner in range(8):
                if corner & bit:
                    parts[corner] = parts[corner] - parts[corner ^ bit]
        for later in range(8):
            row = (col * 8 + later) * 8
            total = mom_ref[row : row + 8, :]
            for now in range(8):
                at = col * 27
                for dim, (bit, weight) in enumerate(((4, 9), (2, 3), (1, 1))):
                    if now & bit and later & bit:
                        at = at + nested[dim] * weight
                    elif now & bit:
                        at = at + weight
                    elif later & bit:
                        at = at + 2 * weight
                total = total + joint_ref[pl.ds(at, 1), :] * parts[now]
            next_ref[row : row + 8, :] = total
    cell_sums(stored_moment(next_ref), new_ref)
    fill_messages_y(new_ref, odd_ref, even_ref)


def last_kernel(shifts_ref, code_ref, vel_ref, sums_ref, from_odd_ref, from_even_ref, axes_ref, out_ref, means_ref, work_ref, tot_ref, table_ref, end_ref):
    means = cell_means(sums_ref, from_odd_ref, from_even_ref, work_ref, tot_ref)
    turn = turned([axes_ref[comp] for comp in range(3)], means)
    table_ref[...] = jnp.zeros_like(table_ref)
    store_cells(table_ref, [means[comp] - turn[comp] for comp in range(3)])
    for comp in range(3):
        means_ref[comp] = means[comp][0:2, :]
    for col, lanes in blocks():

        def body(rows):
            code = code_ref[col, rows, lanes]
            masks = hop_masks(code, shifts_ref, ITERS - 1)
            filled = code >= 0
            for comp in range(3):
                value = vel_ref[comp * 2 + col, rows, lanes] + pick(table_ref, comp, col, lanes, masks)
                end_ref[comp * 2 + col, rows, lanes] = jnp.where(filled, value, 0.0)

        over_slots(body)
    for at in range(6):
        out_ref[at] = end_ref[at].T.astype(jnp.bfloat16)


VMEM = pl.BlockSpec(memory_space=pltpu.VMEM)
SMEM = pl.BlockSpec(memory_space=pltpu.SMEM)
HBM = pl.BlockSpec(memory_space=pltpu.HBM)
BYTES = 8_000_000


def call(kernel, name, in_specs, shapes, scratch, cost=0):
    return pl.pallas_call(
        kernel,
        out_shape=[jax.ShapeDtypeStruct(s, d) for s, d in shapes],
        in_specs=in_specs,
        out_specs=[VMEM] * len(shapes),
        scratch_shapes=scratch,
        compiler_params=pltpu.CompilerParams(vmem_limit_bytes=16 * 1024 * 1024),
        cost_estimate=pl.CostEstimate(flops=0, bytes_accessed=cost, transcendentals=0) if cost else None,
        name=name,
    )


def swap(odd, even, axis):
    count = lax.axis_size(axis)
    evens = [(s, s ^ 1) for s in range(count)]
    odds = [(s, (((s - 1) % count ^ 1) + 1) % count) for s in range(count)]
    from_even = lax.ppermute(even, axis, evens)
    from_odd = lax.ppermute(odd, axis, odds)
    return from_odd, from_even


def on_device(velocity, position_code, occupancy, shifts, axis_ids):
    vel_in = velocity.reshape(6, 256, 128)
    code_in = position_code.reshape(2, 256, 128)
    occ = occupancy.reshape(2, 256)
    ids_in = axis_ids.reshape(ITERS, 2, 256)

    def rows(count):
        return ((count, 256), F32)

    def room(*shape):
        return pltpu.VMEM(shape, F32)

    vel_shape, code_shape = ((6, 128, 256), F32), ((2, 128, 256), jnp.int32)
    table_shape, axes_shape = ((2, WIDE, 256), F32), ((3, 8, 256), F32)
    moments, table = room(128, 256), room(2, WIDE, 256)
    small = [room(24, 256), room(4, 8, 256)]

    vel, code, sums, odd, even = call(
        start_kernel, "start", [HBM] * 5, [vel_shape, code_shape, rows(24), rows(12), rows(12)],
        [moments, pltpu.VMEM((6, 256, 128), jnp.bfloat16), pltpu.VMEM((2, 256, 128), jnp.int32), pltpu.VMEM((2, 256), jnp.int32), pltpu.VMEM((ITERS, 2, 256), jnp.int32), pltpu.SMEM((ITERS, 3), jnp.int32), pltpu.SemaphoreType.DMA((11,))],
    )(*(pltpu.with_memory_space_constraint(x, pltpu.HBM) for x in (shifts, vel_in, code_in, occ, ids_in)))

    from_odd, from_even = swap(odd, even, "gy")
    sums, odd, even = call(
        functools.partial(middle_kernel, True), "middle0", [VMEM] * 4, [rows(36), rows(24), rows(24)], [],
    )(sums, from_odd, from_even, ids_in)
    from_odd, from_even = swap(odd, even, "gx")
    joints = call(joint_kernel, "joint", [SMEM, VMEM], [rows(56), rows(56)], [], BYTES)(shifts, code)
    vel, ids, sums, odd, even = call(
        first_kernel, "first", [SMEM] + [VMEM] * 6, [vel_shape, rows(32), rows(24), rows(8), rows(8)], [moments, *small, table],
    )(shifts, vel, code, sums, from_odd, from_even, joints[0])

    shift = None
    for step in range(1, ITERS):
        last = step == ITERS - 1
        from_odd, from_even = swap(odd, even, "gy")
        sums, odd, even = call(
            functools.partial(middle_kernel, False), f"middle{step}", [VMEM] * 3, [rows(24), rows(12), rows(12)], [],
        )(sums, from_odd, from_even)
        from_odd, from_even = swap(odd, even, "gx")
        args = [shifts, code, ids, vel] + ([] if step == 1 else [shift])
        vel, axes, *moms = call(
            functools.partial(turn_kernel, step), f"turn{step}", [SMEM] + [VMEM] * (len(args) - 1),
            [vel_shape, axes_shape] + ([] if last else [rows(128)]), [table], BYTES,
        )(*args)
        if last:
            out, out_means = call(
                last_kernel, "last", [SMEM] + [VMEM] * 6, [((6, 256, 128), jnp.bfloat16), ((3, 2, 256), F32)],
                [*small, table, room(6, 128, 256)],
            )(shifts, code, vel, sums, from_odd, from_even, axes)
        else:
            shift, sums, odd, even = call(
                functools.partial(shift_kernel, step), f"shift{step}", [SMEM] + [VMEM] * 6,
                [table_shape, rows(24), rows(8), rows(8)], [*small, moments],
            )(shifts, sums, from_odd, from_even, axes, moms[0], joints[step - 1])
    return out.reshape(velocity.shape), out_means.reshape(3, *occupancy.shape)


def solution(mesh):
    in_specs = (
        P(None, "gx", "gy", None, None),
        P("gx", "gy", None, None),
        P("gx", "gy", None),
        P(),
        P(None, "gx", "gy", None),
    )
    out_specs = (P(None, "gx", "gy", None, None), P(None, "gx", "gy", None))
    return jax.shard_map(
        on_device, mesh=mesh, in_specs=in_specs, out_specs=out_specs, check_vma=False
    )
```

```python
import functools
import math

import jax
import jax.numpy as jnp
import numpy as np
from jax import lax
from jax.experimental import pallas as pl
from jax.experimental.pallas import tpu as pltpu
from jax.sharding import PartitionSpec as P

SUBDIV = 8
NAXES = 32
ITERS = 4
GOLDEN = 2.399963229728653
TURN_COS = math.cos(130.0 * math.pi / 180.0)
TURN_SIN = math.sin(130.0 * math.pi / 180.0)
ALONG = (1.0 - TURN_COS) / (TURN_SIN * TURN_SIN)

F32 = jnp.float32
CHUNK = 32
WIDE = 48
WIDE_STEP = 2


def axis_table():
    ordinal = np.arange(NAXES, dtype=np.float64)
    height = 1.0 - (2.0 * ordinal + 1.0) / NAXES
    radius = np.sqrt(1.0 - height * height)
    phases = ordinal * GOLDEN
    return TURN_SIN * np.stack([radius * np.cos(phases), radius * np.sin(phases), height])


AXES = axis_table()


def is_odd(axis):
    return lax.rem(lax.axis_index(axis), 2) == 1


def hop_masks(code, shifts_ref, step):
    hop_x = code >= (SUBDIV - shifts_ref[step, 0]) * (SUBDIV * SUBDIV)
    hop_y = (code & (SUBDIV * SUBDIV - 1)) >= (SUBDIV - shifts_ref[step, 1]) * SUBDIV
    hop_z = (code & (SUBDIV - 1)) >= SUBDIV - shifts_ref[step, 2]
    return hop_x, hop_y, hop_z


def slot_sums(values, count, col, lanes, code_ref, shifts_ref, step, mom_ref):
    def body(i, acc):
        rows = pl.ds(pl.multiple_of(i * 8, 8), 8)
        code = code_ref[col, rows, lanes]
        hop_x, hop_y, hop_z = hop_masks(code, shifts_ref, step)
        out = list(acc)
        for comp, value in enumerate(values(rows, code)):
            with_x = jnp.where(hop_x, value, 0.0)
            with_y = jnp.where(hop_y, value, 0.0)
            with_xy = jnp.where(hop_y, with_x, 0.0)
            for pair, base in ((0, value), (2, with_y), (4, with_x), (6, with_xy)):
                at = comp * 8 + pair
                out[at] = out[at] + base
                out[at + 1] = out[at + 1] + jnp.where(hop_z, base, 0.0)
        return tuple(out)

    zero = jnp.zeros((8, 128), F32)
    acc = lax.fori_loop(0, 16, body, (zero,) * (8 * count), unroll=16)
    for comp in range(count):
        for moment in range(8):
            row = (col * 8 + moment) * 8 + comp
            mom_ref[row : row + 1, lanes] = jnp.sum(acc[comp * 8 + moment], axis=0, keepdims=True)


def blocks():
    for col in range(2):
        for half in range(2):
            yield col, slice(half * 128, half * 128 + 128)


def deposit(vel_ref, code_ref, shifts_ref, step, mom_ref, counted):
    for col, lanes in blocks():

        def values(rows, code):
            parts = [vel_ref[comp * 2 + col, rows, lanes] for comp in range(3)]
            return parts + ([jnp.where(code >= 0, 1.0, 0.0)] if counted else [])

        slot_sums(values, 4 if counted else 3, col, lanes, code_ref, shifts_ref, step, mom_ref)


def cell_sums(moment_of, sums_ref):
    pieces = {}
    for col in range(2):
        quads = {}
        for moment in (0, 2, 4, 6):
            up = moment_of(col, moment + 1)
            quads[moment] = moment_of(col, moment) - up + pltpu.roll(up, 1, 1)
        pieces[col, 1, 1] = quads[6]
        pieces[col, 1, 0] = quads[4] - quads[6]
        pieces[col, 0, 1] = quads[2] - quads[6]
        pieces[col, 0, 0] = quads[0] - quads[2] - quads[4] + quads[6]
    for hop in range(2):
        columns = (pieces[0, hop, 0], pieces[0, hop, 1] + pieces[1, hop, 0], pieces[1, hop, 1])
        for at, piece in enumerate(columns):
            row = (hop * 3 + at) * 4
            sums_ref[row : row + 4, :] = piece[0:4, :]


def stored_moment(mom_ref):
    def moment_of(col, moment):
        row = (col * 8 + moment) * 8
        return mom_ref[row : row + 8, :]

    return moment_of


def fill_messages_y(sums_ref, odd_ref, even_ref, columns=1, first=0):
    odd = is_odd("gy")
    size = columns * 4
    for hop in range(2):
        left = sums_ref[hop * 12 : hop * 12 + size, :]
        right = sums_ref[hop * 12 + 12 - size : hop * 12 + 12, :]
        rows = slice(first + hop * size, first + hop * size + size)
        odd_ref[rows, :] = jnp.where(odd, right, left)
        even_ref[rows, :] = jnp.where(odd, left, right)


def fill_messages_x(out_ref, size, odd_ref, even_ref):
    odd = is_odd("gx")
    low, high = out_ref[0:size, :], out_ref[size : 2 * size, :]
    odd_ref[0:size, :] = jnp.where(odd, high, low)
    even_ref[0:size, :] = jnp.where(odd, low, high)


def from_sides(axis, from_odd, from_even):
    odd = is_odd(axis)
    return jnp.where(odd, from_even, from_odd), jnp.where(odd, from_odd, from_even)


def start_kernel(shifts_hbm, vel_hbm, code_hbm, occ_hbm, ids_hbm, vel_ref, code_ref, sums_ref, odd_ref, even_ref, mom_ref, vel_in_ref, code_in_ref, occ_ref, ids_ref, shifts_ref, sems):
    fetch_shifts = pltpu.make_async_copy(shifts_hbm, shifts_ref, sems.at[10])
    fetch_occ = pltpu.make_async_copy(occ_hbm, occ_ref, sems.at[8])
    fetch_ids = pltpu.make_async_copy(ids_hbm, ids_ref, sems.at[9])
    copies = []
    for col in range(2):
        copies.append(pltpu.make_async_copy(code_hbm.at[col], code_in_ref.at[col], sems.at[col]))
    for at in range(6):
        copies.append(pltpu.make_async_copy(vel_hbm.at[at], vel_in_ref.at[at], sems.at[2 + at]))
    fetch_occ.start()
    for copy in copies:
        copy.start()
    fetch_ids.start()
    fetch_shifts.start()
    mom_ref[...] = jnp.zeros_like(mom_ref)
    slot = lax.broadcasted_iota(jnp.int32, (128, 256), 0)
    fetch_occ.wait()
    for col in range(2):
        filled = slot < occ_ref[col : col + 1, :]
        copies[col].wait()
        code_ref[col] = jnp.where(filled, code_in_ref[col].T, -1)
    for comp in range(3):
        for col in range(2):
            at = comp * 2 + col
            copies[2 + at].wait()
            filled = code_ref[col] >= 0
            vel_ref[at] = jnp.where(filled, vel_in_ref[at].astype(F32).T, 0.0)
    fetch_ids.wait()
    fetch_shifts.wait()
    for step in range(ITERS):
        ids = ids_ref[step, 0:1, :].astype(F32)
        odd_ref[8 + step : 9 + step, :] = ids
        even_ref[8 + step : 9 + step, :] = ids
    far = ids_ref[WIDE_STEP, 1:2, :].astype(F32)
    odd_ref[12:13, :] = far
    even_ref[12:13, :] = far
    deposit(vel_ref, code_ref, shifts_ref, 0, mom_ref, True)
    cell_sums(stored_moment(mom_ref), sums_ref)
    fill_messages_y(sums_ref, odd_ref, even_ref)


def middle_kernel(first, *refs):
    if first:
        sums_ref, from_odd_ref, from_even_ref, ids_ref, out_ref, odd_ref, even_ref = refs
    else:
        sums_ref, from_odd_ref, from_even_ref, out_ref, odd_ref, even_ref = refs
    out_ref[0:24, :] = sums_ref[...]
    for hop in range(2):
        rows = slice(hop * 4, hop * 4 + 4)
        by_left, by_right = from_sides("gy", from_odd_ref[rows, :], from_even_ref[rows, :])
        left = slice(hop * 12, hop * 12 + 4)
        right = slice(hop * 12 + 8, hop * 12 + 12)
        out_ref[left, :] = out_ref[left, :] + by_left
        out_ref[right, :] = out_ref[right, :] + by_right
    fill_messages_x(out_ref, 12, odd_ref, even_ref)
    if first:
        for step in range(ITERS):
            row = 24 + step * 3
            out_ref[row : row + 2, :] = ids_ref[step].astype(F32)
            _, by_right = from_sides("gy", from_odd_ref[8 + step : 9 + step, :], from_even_ref[8 + step : 9 + step, :])
            out_ref[row + 2 : row + 3, :] = by_right
        by_left, by_right = from_sides("gy", from_odd_ref[12:13, :], from_even_ref[12:13, :])
        out_ref[36:37, :] = by_left
        out_ref[37:38, :] = by_right
        own = out_ref[24:38, :]
        odd_ref[12:26, :] = own
        even_ref[12:26, :] = own


def wide_middle_kernel(sums_ref, from_odd_ref, from_even_ref, out_ref, odd_ref, even_ref):
    for hop in range(2):
        at, own = hop * 20, hop * 12
        rows = slice(hop * 8, hop * 8 + 8)
        by_left, by_right = from_sides("gy", from_odd_ref[rows, :], from_even_ref[rows, :])
        out_ref[at : at + 8, :] = by_left
        out_ref[at + 12 : at + 20, :] = by_right
        out_ref[at + 8 : at + 12, :] = sums_ref[own + 4 : own + 8, :]
        out_ref[at + 4 : at + 8, :] = out_ref[at + 4 : at + 8, :] + sums_ref[own : own + 4, :]
        out_ref[at + 12 : at + 16, :] = out_ref[at + 12 : at + 16, :] + sums_ref[own + 8 : own + 12, :]
    fill_messages_x(out_ref, 20, odd_ref, even_ref)


def cell_means(sums_ref, from_odd_ref, from_even_ref, work_ref, tot_ref, width=3):
    size = width * 4
    by_low, by_high = from_sides("gx", from_odd_ref[0:size, :], from_even_ref[0:size, :])
    work_ref[0:size, :] = sums_ref[0:size, :] + by_low
    work_ref[size : 2 * size, :] = sums_ref[size : 2 * size, :] + by_high
    tot_ref[...] = jnp.zeros_like(tot_ref)
    for cell in range(2 * width):
        for comp in range(4):
            tot_ref[comp, cell : cell + 1, :] = work_ref[cell * 4 + comp : cell * 4 + comp + 1, :]
    count = jnp.maximum(tot_ref[3], 1.0)
    return [tot_ref[comp] / count for comp in range(3)]


def cell_axes(ids):
    axes = [jnp.zeros(ids.shape, F32) for _ in range(3)]
    for k in range(NAXES):
        match = ids == float(k)
        axes = [jnp.where(match, float(AXES[comp, k]), axes[comp]) for comp in range(3)]
    return axes


def turned(axis, vec):
    along = (axis[0] * vec[0] + axis[1] * vec[1] + axis[2] * vec[2]) * ALONG
    out = []
    for comp in range(3):
        b, c = (comp + 1) % 3, (comp + 2) % 3
        out.append(TURN_COS * vec[comp] + (axis[b] * vec[c] - axis[c] * vec[b]) + along * axis[comp])
    return out


def next_z(value):
    return pltpu.roll(value, 255, 1)


def store_cells(table_ref, parts, cells=6):
    for cell in range(cells):
        for comp, part in enumerate(parts):
            table_ref[0, cell * 8 + comp : cell * 8 + comp + 1, :] = part[cell : cell + 1, :]
    table_ref[1] = next_z(table_ref[0])


def pick(table_ref, comp, col, lanes, masks):
    hop_x, hop_y, hop_z = masks
    by_x = []
    for step_x in range(2):
        by_y = []
        for step_y in range(2):
            row = (step_x * 3 + col + step_y) * 8 + comp
            by_y.append(jnp.where(hop_z, table_ref[1, row : row + 1, lanes], table_ref[0, row : row + 1, lanes]))
        by_x.append(jnp.where(hop_y, by_y[1], by_y[0]))
    return jnp.where(hop_x, by_x[1], by_x[0])


def over_slots(body):
    def run(i, carry):
        body(pl.ds(pl.multiple_of(i * CHUNK, CHUNK), CHUNK))
        return carry

    lax.fori_loop(0, 128 // CHUNK, run, 0, unroll=128 // CHUNK)


def first_kernel(shifts_ref, vel_ref, code_ref, sums_ref, from_odd_ref, from_even_ref, joint_ref, out_ref, ids_ref, far_ids_ref, new_ref, odd_ref, even_ref, mom_ref, work_ref, tot_ref, table_ref):
    ids_ref[...] = jnp.zeros_like(ids_ref)
    far_ids_ref[...] = jnp.zeros_like(far_ids_ref)
    _, by_high = from_sides("gx", from_odd_ref[12:26, :], from_even_ref[12:26, :])
    work_ref[0:14, :] = by_high
    for t in range(ITERS):
        ids_ref[t * 8 : t * 8 + 3, :] = sums_ref[24 + t * 3 : 27 + t * 3, :]
        ids_ref[t * 8 + 3 : t * 8 + 6, :] = work_ref[t * 3 : t * 3 + 3, :]
    far_ids_ref[0:1, :] = sums_ref[36:37, :]
    far_ids_ref[1:4, :] = sums_ref[24 + WIDE_STEP * 3 : 27 + WIDE_STEP * 3, :]
    far_ids_ref[4:5, :] = sums_ref[37:38, :]
    far_ids_ref[5:6, :] = work_ref[12:13, :]
    far_ids_ref[6:9, :] = work_ref[WIDE_STEP * 3 : WIDE_STEP * 3 + 3, :]
    far_ids_ref[9:10, :] = work_ref[13:14, :]
    means = cell_means(sums_ref, from_odd_ref, from_even_ref, work_ref, tot_ref)
    axes = cell_axes(ids_ref[0:8, :])
    turn = turned(axes, means)
    table_ref[...] = jnp.zeros_like(table_ref)
    store_cells(table_ref, axes + [means[comp] - turn[comp] for comp in range(3)])
    for col, lanes in blocks():

        def body(rows):
            code = code_ref[col, rows, lanes]
            masks = hop_masks(code, shifts_ref, 0)
            vel = [vel_ref[comp * 2 + col, rows, lanes] for comp in range(3)]
            turn = turned([pick(table_ref, comp, col, lanes, masks) for comp in range(3)], vel)
            filled = code >= 0
            for comp in range(3):
                value = turn[comp] + pick(table_ref, 3 + comp, col, lanes, masks)
                out_ref[comp * 2 + col, rows, lanes] = jnp.where(filled, value, 0.0)

        over_slots(body)
    mom_ref[...] = jnp.zeros_like(mom_ref)
    deposit(out_ref, code_ref, shifts_ref, 1, mom_ref, True)
    cell_sums(stored_moment(mom_ref), new_ref)
    fill_messages_y(new_ref, odd_ref, even_ref)


def joint_kernel(shifts_ref, code_ref, first_ref, second_ref, odd_ref, even_ref):
    for t, out_ref in ((1, first_ref), (2, second_ref)):
        out_ref[...] = jnp.zeros_like(out_ref)
        for col, lanes in blocks():

            def body(i, acc):
                rows = pl.ds(pl.multiple_of(i * 8, 8), 8)
                code = code_ref[col, rows, lanes]
                now, later = hop_masks(code, shifts_ref, t), hop_masks(code, shifts_ref, t + 1)
                out, at = list(acc), 0
                one = jnp.where(code >= 0, 1.0, 0.0)
                for by_x in (one, jnp.where(now[0], one, 0.0), jnp.where(later[0], one, 0.0)):
                    for by_y in (by_x, jnp.where(now[1], by_x, 0.0), jnp.where(later[1], by_x, 0.0)):
                        for by_z in (by_y, jnp.where(now[2], by_y, 0.0), jnp.where(later[2], by_y, 0.0)):
                            out[at] = out[at] + by_z
                            at += 1
                return tuple(out)

            acc = lax.fori_loop(0, 16, body, (jnp.zeros((8, 128), F32),) * 27, unroll=2)
            for at in range(27):
                out_ref[col * 27 + at : col * 27 + at + 1, lanes] = jnp.sum(acc[at], axis=0, keepdims=True)
    odd = is_odd("gy")
    nested = nested_hops(WIDE_STEP, shifts_ref)
    for x in range(3):
        for y in range(2):
            for z in range(3):
                hopped = nested[1] if y else 2
                left = second_ref[x * 9 + y * 3 + z : x * 9 + y * 3 + z + 1, :] - second_ref[pl.ds(x * 9 + hopped * 3 + z, 1), :]
                right = second_ref[pl.ds(27 + x * 9 + hopped * 3 + z, 1), :]
                row = x * 6 + y * 3 + z
                odd_ref[row : row + 1, :] = jnp.where(odd, right, left)
                even_ref[row : row + 1, :] = jnp.where(odd, left, right)


def turn_kernel(step, *refs):
    if step == 1:
        shifts_ref, code_ref, ids_ref, vel_ref, *refs = refs
    else:
        shifts_ref, code_ref, ids_ref, vel_ref, last_ref, *refs = refs
    if step == WIDE_STEP:
        far_ids_ref, joint_odd_ref, joint_even_ref, now_ref, out_ref, axes_ref, sums_ref, odd_ref, even_ref, table_ref, mom_ref = refs
        for comp, axis in enumerate(cell_axes(far_ids_ref[...])):
            axes_ref[comp] = axis
    elif step < ITERS - 1:
        out_ref, axes_ref, mom_ref, table_ref = refs
    else:
        out_ref, axes_ref, table_ref = refs
    axes = cell_axes(ids_ref[step * 8 : step * 8 + 8, :])
    if step != WIDE_STEP:
        for comp in range(3):
            axes_ref[comp] = axes[comp]
    table_ref[...] = jnp.zeros_like(table_ref)
    store_cells(table_ref, axes)
    for col, lanes in blocks():

        def body(rows):
            code = code_ref[col, rows, lanes]
            vel = [vel_ref[comp * 2 + col, rows, lanes] for comp in range(3)]
            if step > 1:
                masks = hop_masks(code, shifts_ref, step - 1)
                filled = code >= 0
                vel = [jnp.where(filled, vel[comp] + pick(last_ref, comp, col, lanes, masks), 0.0) for comp in range(3)]
            masks = hop_masks(code, shifts_ref, step)
            turn = turned([pick(table_ref, comp, col, lanes, masks) for comp in range(3)], vel)
            for comp in range(3):
                out_ref[comp * 2 + col, rows, lanes] = turn[comp]

        over_slots(body)
    if step < ITERS - 1:
        mom_ref[...] = jnp.zeros_like(mom_ref)
        deposit(out_ref, code_ref, shifts_ref, step + 1, mom_ref, False)
    if step == WIDE_STEP:
        cell_sums(stored_moment(mom_ref), sums_ref)
        fill_messages_y(now_ref, odd_ref, even_ref, 2)
        fill_messages_y(sums_ref, odd_ref, even_ref, 1, 16)
        odd_ref[24:42, :] = joint_odd_ref[...]
        even_ref[24:42, :] = joint_even_ref[...]


def nested_hops(step, shifts_ref):
    return [jnp.where(shifts_ref[step, dim] <= shifts_ref[step + 1, dim], 1, 2) for dim in range(3)]


def corner_differences(shift_ref, cells):
    parts = {}
    for corner in range(8):
        cell = cells[corner >> 2][corner >> 1 & 1]
        parts[corner] = shift_ref[corner & 1, cell * 8 : cell * 8 + 8, :]
    for bit in (1, 2, 4):
        for corner in range(8):
            if corner & bit:
                parts[corner] = parts[corner] - parts[corner ^ bit]
    return parts


def shift_moment(joint_ref, first, parts, later, nested, weights=(9, 3, 1)):
    total = None
    for now in range(8):
        at = first
        for dim, (bit, weight) in enumerate(zip((4, 2, 1), weights)):
            if now & bit and later & bit:
                at = at + nested[dim] * weight
            elif now & bit:
                at = at + weight
            elif later & bit:
                at = at + 2 * weight
        term = joint_ref[pl.ds(at, 1), :] * parts[now]
        total = term if total is None else total + term
    return total


def shifts_of(means, axes):
    turn = turned(axes, means)
    return [means[comp] - turn[comp] for comp in range(3)] + [jnp.ones_like(means[0])]


def shift_kernel(step, shifts_ref, sums_ref, from_odd_ref, from_even_ref, axes_ref, mom_ref, joint_ref, shift_ref, new_ref, *refs):
    *messages, work_ref, tot_ref, next_ref = refs
    means = cell_means(sums_ref, from_odd_ref, from_even_ref, work_ref, tot_ref)
    shift_ref[...] = jnp.zeros_like(shift_ref)
    store_cells(shift_ref, shifts_of(means, [axes_ref[comp] for comp in range(3)]))
    nested = nested_hops(step, shifts_ref)
    for col in range(2):
        parts = corner_differences(shift_ref, ((col, col + 1), (3 + col, 4 + col)))
        for later in range(8):
            row = (col * 8 + later) * 8
            next_ref[row : row + 8, :] = mom_ref[row : row + 8, :] + shift_moment(joint_ref, col * 27, parts, later, nested)
    cell_sums(stored_moment(next_ref), new_ref)
    if messages:
        fill_messages_y(new_ref, *messages)


def wide_shift_kernel(step, shifts_ref, sums_ref, from_odd_ref, from_even_ref, axes_ref, turned_ref, joint_ref, y_odd_ref, y_even_ref, shift_ref, new_ref, odd_ref, even_ref, work_ref, tot_ref, next_ref, far_ref, side_ref):
    means = cell_means(sums_ref, from_odd_ref, from_even_ref, work_ref, tot_ref, 5)
    far_ref[...] = jnp.zeros_like(far_ref)
    store_cells(far_ref, shifts_of(means, [axes_ref[comp] for comp in range(3)]), 10)
    for hop in range(2):
        for side in range(2):
            shift_ref[side, hop * 24 : hop * 24 + 24, :] = far_ref[side, hop * 40 + 8 : hop * 40 + 32, :]
    nested = nested_hops(step, shifts_ref)
    for col in range(2):
        parts = corner_differences(far_ref, ((col + 1, col + 2), (col + 6, col + 7)))
        for later in range(8):
            row = (col * 8 + later) * 8
            next_ref[row : row + 8, :] = shift_moment(joint_ref, col * 27, parts, later, nested)
    cell_sums(stored_moment(next_ref), new_ref)
    new_ref[...] = new_ref[...] + turned_ref[...]
    for side, came in enumerate(from_sides("gy", y_odd_ref[16:42, :], y_even_ref[16:42, :])):
        side_ref[...] = came
        first = side * 3
        parts = corner_differences(far_ref, ((first, first + 1), (first + 5, first + 6)))
        quads = []
        for moment in (0, 4):
            up = shift_moment(side_ref, 8, parts, moment + 1, nested, (6, 3, 1))
            quads.append(shift_moment(side_ref, 8, parts, moment, nested, (6, 3, 1)) - up + pltpu.roll(up, 1, 1))
        for hop, piece in enumerate((quads[0] - quads[1], quads[1])):
            rows = slice(hop * 12 + side * 8, hop * 12 + side * 8 + 4)
            new_ref[rows, :] = new_ref[rows, :] + piece[0:4, :] + side_ref[hop * 4 : hop * 4 + 4, :]
    fill_messages_x(new_ref, 12, odd_ref, even_ref)


def last_kernel(shifts_ref, code_ref, vel_ref, sums_ref, from_odd_ref, from_even_ref, axes_ref, out_ref, means_ref, work_ref, tot_ref, table_ref, end_ref):
    means = cell_means(sums_ref, from_odd_ref, from_even_ref, work_ref, tot_ref)
    turn = turned([axes_ref[comp] for comp in range(3)], means)
    table_ref[...] = jnp.zeros_like(table_ref)
    store_cells(table_ref, [means[comp] - turn[comp] for comp in range(3)])
    for comp in range(3):
        means_ref[comp] = means[comp][0:2, :]
    for col, lanes in blocks():

        def body(rows):
            code = code_ref[col, rows, lanes]
            masks = hop_masks(code, shifts_ref, ITERS - 1)
            filled = code >= 0
            for comp in range(3):
                value = vel_ref[comp * 2 + col, rows, lanes] + pick(table_ref, comp, col, lanes, masks)
                end_ref[comp * 2 + col, rows, lanes] = jnp.where(filled, value, 0.0)

        over_slots(body)
    for at in range(6):
        out_ref[at] = end_ref[at].T.astype(jnp.bfloat16)


VMEM = pl.BlockSpec(memory_space=pltpu.VMEM)
SMEM = pl.BlockSpec(memory_space=pltpu.SMEM)
HBM = pl.BlockSpec(memory_space=pltpu.HBM)
BYTES = 8_000_000


def call(kernel, name, in_specs, shapes, scratch, cost=0):
    return pl.pallas_call(
        kernel,
        out_shape=[jax.ShapeDtypeStruct(s, d) for s, d in shapes],
        in_specs=in_specs,
        out_specs=[VMEM] * len(shapes),
        scratch_shapes=scratch,
        compiler_params=pltpu.CompilerParams(vmem_limit_bytes=16 * 1024 * 1024),
        cost_estimate=pl.CostEstimate(flops=0, bytes_accessed=cost, transcendentals=0) if cost else None,
        name=name,
    )


def swap(odd, even, axis):
    count = lax.axis_size(axis)
    evens = [(s, s ^ 1) for s in range(count)]
    odds = [(s, (((s - 1) % count ^ 1) + 1) % count) for s in range(count)]
    from_even = lax.ppermute(even, axis, evens)
    from_odd = lax.ppermute(odd, axis, odds)
    return from_odd, from_even


def on_device(velocity, position_code, occupancy, shifts, axis_ids):
    vel_in = velocity.reshape(6, 256, 128)
    code_in = position_code.reshape(2, 256, 128)
    occ = occupancy.reshape(2, 256)
    ids_in = axis_ids.reshape(ITERS, 2, 256)

    def rows(count):
        return ((count, 256), F32)

    def room(*shape):
        return pltpu.VMEM(shape, F32)

    vel_shape, code_shape = ((6, 128, 256), F32), ((2, 128, 256), jnp.int32)
    table_shape, axes_shape = ((2, WIDE, 256), F32), ((3, 8, 256), F32)
    moments, table = room(128, 256), room(2, WIDE, 256)
    small = [room(24, 256), room(4, 8, 256)]

    vel, code, sums, odd, even = call(
        start_kernel, "start", [HBM] * 5, [vel_shape, code_shape, rows(24), rows(13), rows(13)],
        [moments, pltpu.VMEM((6, 256, 128), jnp.bfloat16), pltpu.VMEM((2, 256, 128), jnp.int32), pltpu.VMEM((2, 256), jnp.int32), pltpu.VMEM((ITERS, 2, 256), jnp.int32), pltpu.SMEM((ITERS, 3), jnp.int32), pltpu.SemaphoreType.DMA((11,))],
    )(*(pltpu.with_memory_space_constraint(x, pltpu.HBM) for x in (shifts, vel_in, code_in, occ, ids_in)))

    from_odd, from_even = swap(odd, even, "gy")
    sums, odd, even = call(
        functools.partial(middle_kernel, True), "middle0", [VMEM] * 4, [rows(38), rows(26), rows(26)], [],
    )(sums, from_odd, from_even, ids_in)
    from_odd, from_even = swap(odd, even, "gx")
    *joints, joint_odd, joint_even = call(
        joint_kernel, "joint", [SMEM, VMEM], [rows(56), rows(56), rows(18), rows(18)], [], BYTES
    )(shifts, code)
    vel, ids, far_ids, sums, odd, even = call(
        first_kernel, "first", [SMEM] + [VMEM] * 6, [vel_shape, rows(32), rows(16), rows(24), rows(8), rows(8)], [moments, *small, table],
    )(shifts, vel, code, sums, from_odd, from_even, joints[0])

    shift = None
    for step in range(1, ITERS):
        last, wide, after_wide = step == ITERS - 1, step == WIDE_STEP, step == WIDE_STEP + 1
        args = [shifts, code, ids, vel] + ([] if step == 1 else [shift])
        shapes, scratch = [vel_shape, axes_shape], [table]
        if wide:
            args += [far_ids, joint_odd, joint_even, sums]
            shapes = [vel_shape, ((3, 16, 256), F32), rows(24), rows(42), rows(42)]
            scratch = [table, moments]
        elif not last:
            shapes.append(rows(128))
        vel, axes, *more = call(
            functools.partial(turn_kernel, step), f"turn{step}", [SMEM] + [VMEM] * (len(args) - 1), shapes, scratch, BYTES,
        )(*args)
        if wide:
            own, odd, even = more
        if not after_wide:
            y_odd, y_even = swap(odd, even, "gy")
            sums, odd, even = call(
                wide_middle_kernel if wide else functools.partial(middle_kernel, False), f"middle{step}", [VMEM] * 3,
                [rows(40), rows(20), rows(20)] if wide else [rows(24), rows(12), rows(12)], [],
            )(sums, y_odd, y_even)
        from_odd, from_even = swap(odd, even, "gx")
        if last:
            out, out_means = call(
                last_kernel, "last", [SMEM] + [VMEM] * 6, [((6, 256, 128), jnp.bfloat16), ((3, 2, 256), F32)],
                [*small, table, room(6, 128, 256)],
            )(shifts, code, vel, sums, from_odd, from_even, axes)
        elif wide:
            shift, sums, odd, even = call(
                functools.partial(wide_shift_kernel, step), f"shift{step}", [SMEM] + [VMEM] * 8,
                [table_shape, rows(24), rows(12), rows(12)],
                [room(40, 256), room(4, 16, 256), moments, room(2, 80, 256), room(26, 256)],
            )(shifts, sums, from_odd, from_even, axes, own, joints[step - 1], y_odd, y_even)
        else:
            messages = [] if step + 1 == WIDE_STEP else [rows(8), rows(8)]
            shift, sums, *pair = call(
                functools.partial(shift_kernel, step), f"shift{step}", [SMEM] + [VMEM] * 6,
                [table_shape, rows(24), *messages], [*small, moments],
            )(shifts, sums, from_odd, from_even, axes, more[0], joints[step - 1])
            if pair:
                odd, even = pair
    return out.reshape(velocity.shape), out_means.reshape(3, *occupancy.shape)


def solution(mesh):
    in_specs = (
        P(None, "gx", "gy", None, None),
        P("gx", "gy", None, None),
        P("gx", "gy", None),
        P(),
        P(None, "gx", "gy", None),
    )
    out_specs = (P(None, "gx", "gy", None, None), P(None, "gx", "gy", None))
    return jax.shard_map(
        on_device, mesh=mesh, in_specs=in_specs, out_specs=out_specs, check_vma=False
    )
```

```python
import functools
import math

import jax
import jax.numpy as jnp
import numpy as np
from jax import lax
from jax.experimental import pallas as pl
from jax.experimental.pallas import tpu as pltpu
from jax.sharding import PartitionSpec as P

SUBDIV = 8
NAXES = 32
ITERS = 4
GOLDEN = 2.399963229728653
TURN_COS = math.cos(130.0 * math.pi / 180.0)
TURN_SIN = math.sin(130.0 * math.pi / 180.0)
ALONG = (1.0 - TURN_COS) / (TURN_SIN * TURN_SIN)

F32 = jnp.float32
CHUNK = 32
WIDE = 48
WIDE_STEP = 2


def axis_table():
    ordinal = np.arange(NAXES, dtype=np.float64)
    height = 1.0 - (2.0 * ordinal + 1.0) / NAXES
    radius = np.sqrt(1.0 - height * height)
    phases = ordinal * GOLDEN
    return TURN_SIN * np.stack([radius * np.cos(phases), radius * np.sin(phases), height])


AXES = axis_table()


def is_odd(axis):
    return lax.rem(lax.axis_index(axis), 2) == 1


def hop_masks(code, shifts_ref, step):
    hop_x = code >= (SUBDIV - shifts_ref[step, 0]) * (SUBDIV * SUBDIV)
    hop_y = (code & (SUBDIV * SUBDIV - 1)) >= (SUBDIV - shifts_ref[step, 1]) * SUBDIV
    hop_z = (code & (SUBDIV - 1)) >= SUBDIV - shifts_ref[step, 2]
    return hop_x, hop_y, hop_z


def slot_sums(values, count, col, lanes, code_ref, shifts_ref, step, mom_ref):
    def body(i, acc):
        rows = pl.ds(pl.multiple_of(i * 8, 8), 8)
        code = code_ref[col, rows, lanes]
        hop_x, hop_y, hop_z = hop_masks(code, shifts_ref, step)
        out = list(acc)
        for comp, value in enumerate(values(rows, code)):
            with_x = jnp.where(hop_x, value, 0.0)
            with_y = jnp.where(hop_y, value, 0.0)
            with_xy = jnp.where(hop_y, with_x, 0.0)
            for pair, base in ((0, value), (2, with_y), (4, with_x), (6, with_xy)):
                at = comp * 8 + pair
                out[at] = out[at] + base
                out[at + 1] = out[at + 1] + jnp.where(hop_z, base, 0.0)
        return tuple(out)

    zero = jnp.zeros((8, 128), F32)
    acc = lax.fori_loop(0, 16, body, (zero,) * (8 * count), unroll=16)
    for comp in range(count):
        for moment in range(8):
            row = (col * 8 + moment) * 8 + comp
            mom_ref[row : row + 1, lanes] = jnp.sum(acc[comp * 8 + moment], axis=0, keepdims=True)


def blocks(cols=(0, 1)):
    for col in cols:
        for half in range(2):
            yield col, slice(half * 128, half * 128 + 128)


def deposit(vel_ref, code_ref, shifts_ref, step, mom_ref, counted, cols=(0, 1)):
    for col, lanes in blocks(cols):

        def values(rows, code):
            parts = [vel_ref[comp * 2 + col, rows, lanes] for comp in range(3)]
            return parts + ([jnp.where(code >= 0, 1.0, 0.0)] if counted else [])

        slot_sums(values, 4 if counted else 3, col, lanes, code_ref, shifts_ref, step, mom_ref)


def cell_sums(moment_of, sums_ref):
    pieces = {}
    for col in range(2):
        quads = {}
        for moment in (0, 2, 4, 6):
            up = moment_of(col, moment + 1)
            quads[moment] = moment_of(col, moment) - up + pltpu.roll(up, 1, 1)
        pieces[col, 1, 1] = quads[6]
        pieces[col, 1, 0] = quads[4] - quads[6]
        pieces[col, 0, 1] = quads[2] - quads[6]
        pieces[col, 0, 0] = quads[0] - quads[2] - quads[4] + quads[6]
    for hop in range(2):
        columns = (pieces[0, hop, 0], pieces[0, hop, 1] + pieces[1, hop, 0], pieces[1, hop, 1])
        for at, piece in enumerate(columns):
            row = (hop * 3 + at) * 4
            sums_ref[row : row + 4, :] = piece[0:4, :]


def stored_moment(mom_ref):
    def moment_of(col, moment):
        row = (col * 8 + moment) * 8
        return mom_ref[row : row + 8, :]

    return moment_of


def fill_messages_y(sums_ref, odd_ref, even_ref, columns=1, first=0):
    odd = is_odd("gy")
    size = columns * 4
    for hop in range(2):
        left = sums_ref[hop * 12 : hop * 12 + size, :]
        right = sums_ref[hop * 12 + 12 - size : hop * 12 + 12, :]
        rows = slice(first + hop * size, first + hop * size + size)
        odd_ref[rows, :] = jnp.where(odd, right, left)
        even_ref[rows, :] = jnp.where(odd, left, right)


def fill_messages_x(out_ref, size, odd_ref, even_ref):
    odd = is_odd("gx")
    low, high = out_ref[0:size, :], out_ref[size : 2 * size, :]
    odd_ref[0:size, :] = jnp.where(odd, high, low)
    even_ref[0:size, :] = jnp.where(odd, low, high)


def from_sides(axis, from_odd, from_even):
    odd = is_odd(axis)
    return jnp.where(odd, from_even, from_odd), jnp.where(odd, from_odd, from_even)


def start_kernel(shifts_hbm, vel_hbm, code_hbm, occ_hbm, ids_hbm, vel_ref, code_ref, sums_ref, odd_ref, even_ref, mom_ref, vel_in_ref, code_in_ref, occ_ref, ids_ref, shifts_ref, sems):
    fetch_shifts = pltpu.make_async_copy(shifts_hbm, shifts_ref, sems.at[10])
    fetch_occ = pltpu.make_async_copy(occ_hbm, occ_ref, sems.at[8])
    fetch_ids = pltpu.make_async_copy(ids_hbm, ids_ref, sems.at[9])
    copies = []
    for col in range(2):
        copies.append(pltpu.make_async_copy(code_hbm.at[col], code_in_ref.at[col], sems.at[col]))
    for at in range(6):
        copies.append(pltpu.make_async_copy(vel_hbm.at[at], vel_in_ref.at[at], sems.at[2 + at]))
    fetch_occ.start()
    for at in (0, 2, 4, 6, 1, 3, 5, 7):
        copies[at].start()
    fetch_ids.start()
    fetch_shifts.start()
    mom_ref[...] = jnp.zeros_like(mom_ref)
    slot = lax.broadcasted_iota(jnp.int32, (128, 256), 0)
    fetch_occ.wait()
    fetch_shifts.wait()
    for col in range(2):
        filled = slot < occ_ref[col : col + 1, :]
        copies[col].wait()
        code_ref[col] = jnp.where(filled, code_in_ref[col].T, -1)
        for comp in range(3):
            at = comp * 2 + col
            copies[2 + at].wait()
            vel_ref[at] = jnp.where(filled, vel_in_ref[at].astype(F32).T, 0.0)
        deposit(vel_ref, code_ref, shifts_ref, 0, mom_ref, True, (col,))
    fetch_ids.wait()
    for step in range(ITERS):
        ids = ids_ref[step].astype(F32)
        rows = slice(12 + step * 2, 14 + step * 2)
        odd_ref[rows, :] = ids
        even_ref[rows, :] = ids
    cell_sums(stored_moment(mom_ref), sums_ref)
    fill_messages_x(sums_ref, 12, odd_ref, even_ref)


def add_x(sums_ref, from_odd_ref, from_even_ref, out_ref):
    by_low, by_high = from_sides("gx", from_odd_ref[0:12, :], from_even_ref[0:12, :])
    out_ref[0:12, :] = sums_ref[0:12, :] + by_low
    out_ref[12:24, :] = sums_ref[12:24, :] + by_high


def add_y(sums_ref, by_left_ref, by_right_ref, out_ref):
    for hop in range(2):
        at, own, rows = hop * 20, hop * 12, slice(hop * 8, hop * 8 + 8)
        out_ref[at : at + 8, :] = by_left_ref[rows, :]
        out_ref[at + 12 : at + 20, :] = by_right_ref[rows, :]
        out_ref[at + 8 : at + 12, :] = sums_ref[own + 4 : own + 8, :]
        out_ref[at + 4 : at + 8, :] = out_ref[at + 4 : at + 8, :] + sums_ref[own : own + 4, :]
        out_ref[at + 12 : at + 16, :] = out_ref[at + 12 : at + 16, :] + sums_ref[own + 8 : own + 12, :]


def first_middle_kernel(sums_ref, from_odd_ref, from_even_ref, ids_ref, ghost_odd_ref, ghost_even_ref, out_ref, both_ref, odd_ref, even_ref):
    add_x(sums_ref, from_odd_ref, from_even_ref, out_ref)
    fill_messages_y(out_ref, odd_ref, even_ref, 2)
    for step in range(ITERS):
        both_ref[step * 2 : step * 2 + 2, :] = ids_ref[step].astype(F32)
    _, by_high = from_sides("gx", from_odd_ref[12:20, :], from_even_ref[12:20, :])
    both_ref[8:16, :] = by_high
    for ref in (odd_ref, even_ref):
        for x in range(2):
            for step in range(ITERS):
                ref[16 + x * 4 + step : 17 + x * 4 + step, :] = both_ref[x * 8 + step * 2 : x * 8 + step * 2 + 1, :]
            for k, step in enumerate((0, WIDE_STEP)):
                ref[24 + x * 2 + k : 25 + x * 2 + k, :] = both_ref[x * 8 + step * 2 + 1 : x * 8 + step * 2 + 2, :]
    odd_ref[28:100, :] = ghost_odd_ref[...]
    even_ref[28:100, :] = ghost_even_ref[...]


def wide_middle_kernel(sums_ref, from_odd_ref, from_even_ref, turned_ref, joint_odd_ref, joint_even_ref, out_ref, odd_ref, even_ref):
    add_x(sums_ref, from_odd_ref, from_even_ref, out_ref)
    fill_messages_y(out_ref, odd_ref, even_ref, 2)
    fill_messages_y(turned_ref, odd_ref, even_ref, 1, 16)
    odd_ref[24:42, :] = joint_odd_ref[...]
    even_ref[24:42, :] = joint_even_ref[...]


def cell_means(work_ref, tot_ref, cells=6):
    tot_ref[...] = jnp.zeros_like(tot_ref)
    for cell in range(cells):
        for comp in range(4):
            tot_ref[comp, cell : cell + 1, :] = work_ref[cell * 4 + comp : cell * 4 + comp + 1, :]
    count = jnp.maximum(tot_ref[3], 1.0)
    return [tot_ref[comp] / count for comp in range(3)]


def cell_axes(ids):
    axes = [jnp.zeros(ids.shape, F32) for _ in range(3)]
    for k in range(NAXES):
        match = ids == float(k)
        axes = [jnp.where(match, float(AXES[comp, k]), axes[comp]) for comp in range(3)]
    return axes


def turned(axis, vec):
    along = (axis[0] * vec[0] + axis[1] * vec[1] + axis[2] * vec[2]) * ALONG
    out = []
    for comp in range(3):
        b, c = (comp + 1) % 3, (comp + 2) % 3
        out.append(TURN_COS * vec[comp] + (axis[b] * vec[c] - axis[c] * vec[b]) + along * axis[comp])
    return out


def next_z(value):
    return pltpu.roll(value, 255, 1)


def store_cells(table_ref, parts, cells=6):
    for cell in range(cells):
        for comp, part in enumerate(parts):
            table_ref[0, cell * 8 + comp : cell * 8 + comp + 1, :] = part[cell : cell + 1, :]
    table_ref[1] = next_z(table_ref[0])


def pick(table_ref, comp, col, lanes, masks):
    hop_x, hop_y, hop_z = masks
    by_x = []
    for step_x in range(2):
        by_y = []
        for step_y in range(2):
            row = (step_x * 3 + col + step_y) * 8 + comp
            by_y.append(jnp.where(hop_z, table_ref[1, row : row + 1, lanes], table_ref[0, row : row + 1, lanes]))
        by_x.append(jnp.where(hop_y, by_y[1], by_y[0]))
    return jnp.where(hop_x, by_x[1], by_x[0])


def over_slots(body):
    def run(i, carry):
        body(pl.ds(pl.multiple_of(i * CHUNK, CHUNK), CHUNK))
        return carry

    lax.fori_loop(0, 128 // CHUNK, run, 0, unroll=128 // CHUNK)


def first_kernel(shifts_ref, vel_ref, code_ref, sums_ref, from_odd_ref, from_even_ref, both_ref, out_ref, ids_ref, far_ids_ref, new_ref, odd_ref, even_ref, mom_ref, work_ref, tot_ref, axis_ref, shift_ref, far_ref, turn_ref, left_ref, right_ref):
    by_left, by_right = from_sides("gy", from_odd_ref[...], from_even_ref[...])
    left_ref[...] = by_left
    right_ref[...] = by_right
    ids_ref[...] = jnp.zeros_like(ids_ref)
    for x in range(2):
        for t in range(ITERS):
            row = t * 8 + x * 3
            ids_ref[row : row + 2, :] = both_ref[x * 8 + t * 2 : x * 8 + t * 2 + 2, :]
            ids_ref[row + 2 : row + 3, :] = right_ref[16 + x * 4 + t : 17 + x * 4 + t, :]
    far_ids_ref[...] = jnp.zeros_like(far_ids_ref)
    for k, t in enumerate((0, WIDE_STEP)):
        for x in range(2):
            row, outer = k * 16 + x * 5, slice(24 + x * 2 + k, 25 + x * 2 + k)
            far_ids_ref[row : row + 1, :] = left_ref[outer, :]
            far_ids_ref[row + 1 : row + 4, :] = ids_ref[t * 8 + x * 3 : t * 8 + x * 3 + 3, :]
            far_ids_ref[row + 4 : row + 5, :] = right_ref[outer, :]
    add_y(sums_ref, left_ref, right_ref, work_ref)
    means = cell_means(work_ref, tot_ref, 10)
    axes = cell_axes(far_ids_ref[0:16, :])
    far_ref[...] = jnp.zeros_like(far_ref)
    store_cells(far_ref, shifts_of(means, axes), 10)
    for table_ref in (shift_ref, axis_ref, turn_ref):
        table_ref[...] = jnp.zeros_like(table_ref)
    own_cells(far_ref, shift_ref)
    store_cells(axis_ref, cell_axes(ids_ref[0:8, :]))
    for col, lanes in blocks():

        def body(rows):
            code = code_ref[col, rows, lanes]
            masks = hop_masks(code, shifts_ref, 0)
            vel = [vel_ref[comp * 2 + col, rows, lanes] for comp in range(3)]
            turn = turned([pick(axis_ref, comp, col, lanes, masks) for comp in range(3)], vel)
            filled = code >= 0
            for comp in range(3):
                value = turn[comp] + pick(shift_ref, comp, col, lanes, masks)
                out_ref[comp * 2 + col, rows, lanes] = jnp.where(filled, value, 0.0)

        over_slots(body)
    mom_ref[...] = jnp.zeros_like(mom_ref)
    deposit(out_ref, code_ref, shifts_ref, 1, mom_ref, True)
    cell_sums(stored_moment(mom_ref), new_ref)
    zero = jnp.zeros((16, 256), F32)
    for k in range(3):
        unit = [zero + (1.0 if comp == k else 0.0) for comp in range(3)]
        store_cells(turn_ref.at[k], turned(axes, unit), 10)
    nested = nested_hops(0, shifts_ref)
    for side, came_ref in enumerate((left_ref, right_ref)):
        cells = side_cells(side)
        sources = [(28, corner_differences(far_ref, cells))]
        sources += [(46 + k * 18, corner_differences(turn_ref.at[k], cells)) for k in range(3)]
        add_side(new_ref, side, came_ref, sources, nested)
    fill_messages_x(new_ref, 12, odd_ref, even_ref)


def ghost_kernel(shifts_ref, vel_ref, code_ref, odd_ref, even_ref, left_ref, right_ref):
    for col, lanes in blocks():
        side_ref = right_ref if col else left_ref

        def classes(value, now, later):
            out = []
            for by_x in (value, jnp.where(now[0], value, 0), jnp.where(later[0], value, 0)):
                for by_y in (by_x, jnp.where(now[1], by_x, 0)):
                    out.append(by_y)
            return out

        def body(comps, counts, i, acc):
            rows = pl.ds(pl.multiple_of(i * 8, 8), 8)
            code = code_ref[col, rows, lanes]
            now, later = hop_masks(code, shifts_ref, 0), hop_masks(code, shifts_ref, 1)
            kept = later[1] if col else jnp.logical_not(later[1])
            out = []
            for comp in comps:
                for value in classes(jnp.where(kept, vel_ref[comp * 2 + col, rows, lanes], 0.0), now, later):
                    out += [value, jnp.where(now[2], value, 0.0), jnp.where(later[2], value, 0.0)]
            if counts:
                word = jnp.where(now[2], 1 + 256, 1) + jnp.where(later[2], 65536, 0)
                out += classes(jnp.where(jnp.logical_and(kept, code >= 0), word, 0), now, later)
            return tuple(a + b for a, b in zip(acc, out))

        zero, none = jnp.zeros((8, 128), F32), jnp.zeros((8, 128), jnp.int32)
        for comps, counts in (((0, 1), False), ((2,), True)):
            start = (zero,) * (18 * len(comps)) + ((none,) * 6 if counts else ())
            acc = lax.fori_loop(0, 16, functools.partial(body, comps, counts), start, unroll=8)
            for n, comp in enumerate(comps):
                for at in range(18):
                    row = 18 + comp * 18 + at
                    side_ref[row : row + 1, lanes] = jnp.sum(acc[n * 18 + at], axis=0, keepdims=True)
            if counts:
                for at in range(6):
                    word = acc[18 * len(comps) + at]
                    for z in range(3):
                        part = lax.shift_right_logical(word, 8 * z) & 255
                        row = at * 3 + z
                        side_ref[row : row + 1, lanes] = jnp.sum(part.astype(F32), axis=0, keepdims=True)
    odd = is_odd("gy")
    odd_ref[...] = jnp.where(odd, right_ref[...], left_ref[...])
    even_ref[...] = jnp.where(odd, left_ref[...], right_ref[...])


def joint_kernel(shifts_ref, code_ref, first_ref, second_ref, odd_ref, even_ref):
    for t, out_ref in ((1, first_ref), (2, second_ref)):
        out_ref[...] = jnp.zeros_like(out_ref)
        for col, lanes in blocks():

            def body(i, acc):
                rows = pl.ds(pl.multiple_of(i * 8, 8), 8)
                code = code_ref[col, rows, lanes]
                now, later = hop_masks(code, shifts_ref, t), hop_masks(code, shifts_ref, t + 1)
                out, at = list(acc), 0
                one = jnp.where(code >= 0, 1.0, 0.0)
                for by_x in (one, jnp.where(now[0], one, 0.0), jnp.where(later[0], one, 0.0)):
                    for by_y in (by_x, jnp.where(now[1], by_x, 0.0), jnp.where(later[1], by_x, 0.0)):
                        for by_z in (by_y, jnp.where(now[2], by_y, 0.0), jnp.where(later[2], by_y, 0.0)):
                            out[at] = out[at] + by_z
                            at += 1
                return tuple(out)

            acc = lax.fori_loop(0, 16, body, (jnp.zeros((8, 128), F32),) * 27, unroll=2)
            for at in range(27):
                out_ref[col * 27 + at : col * 27 + at + 1, lanes] = jnp.sum(acc[at], axis=0, keepdims=True)
    odd = is_odd("gy")
    nested = nested_hops(WIDE_STEP, shifts_ref)
    for x in range(3):
        for y in range(2):
            for z in range(3):
                hopped = nested[1] if y else 2
                left = second_ref[x * 9 + y * 3 + z : x * 9 + y * 3 + z + 1, :] - second_ref[pl.ds(x * 9 + hopped * 3 + z, 1), :]
                right = second_ref[pl.ds(27 + x * 9 + hopped * 3 + z, 1), :]
                row = x * 6 + y * 3 + z
                odd_ref[row : row + 1, :] = jnp.where(odd, right, left)
                even_ref[row : row + 1, :] = jnp.where(odd, left, right)


def turn_kernel(step, *refs):
    if step == 1:
        shifts_ref, code_ref, ids_ref, vel_ref, *refs = refs
    else:
        shifts_ref, code_ref, ids_ref, vel_ref, last_ref, *refs = refs
    if step == WIDE_STEP:
        far_ids_ref, out_ref, axes_ref, sums_ref, table_ref, mom_ref = refs
        for comp, axis in enumerate(cell_axes(far_ids_ref[16:32, :])):
            axes_ref[comp] = axis
    elif step < ITERS - 1:
        out_ref, axes_ref, mom_ref, table_ref = refs
    else:
        out_ref, axes_ref, table_ref = refs
    axes = cell_axes(ids_ref[step * 8 : step * 8 + 8, :])
    if step != WIDE_STEP:
        for comp in range(3):
            axes_ref[comp] = axes[comp]
    table_ref[...] = jnp.zeros_like(table_ref)
    store_cells(table_ref, axes)
    for col, lanes in blocks():

        def body(rows):
            code = code_ref[col, rows, lanes]
            vel = [vel_ref[comp * 2 + col, rows, lanes] for comp in range(3)]
            if step > 1:
                masks = hop_masks(code, shifts_ref, step - 1)
                filled = code >= 0
                vel = [jnp.where(filled, vel[comp] + pick(last_ref, comp, col, lanes, masks), 0.0) for comp in range(3)]
            masks = hop_masks(code, shifts_ref, step)
            turn = turned([pick(table_ref, comp, col, lanes, masks) for comp in range(3)], vel)
            for comp in range(3):
                out_ref[comp * 2 + col, rows, lanes] = turn[comp]

        over_slots(body)
    if step < ITERS - 1:
        mom_ref[...] = jnp.zeros_like(mom_ref)
        deposit(out_ref, code_ref, shifts_ref, step + 1, mom_ref, False)
    if step == WIDE_STEP:
        cell_sums(stored_moment(mom_ref), sums_ref)


def nested_hops(step, shifts_ref):
    return [jnp.where(shifts_ref[step, dim] <= shifts_ref[step + 1, dim], 1, 2) for dim in range(3)]


def corner_differences(shift_ref, cells):
    parts = {}
    for corner in range(8):
        cell = cells[corner >> 2][corner >> 1 & 1]
        parts[corner] = shift_ref[corner & 1, cell * 8 : cell * 8 + 8, :]
    for bit in (1, 2, 4):
        for corner in range(8):
            if corner & bit:
                parts[corner] = parts[corner] - parts[corner ^ bit]
    return parts


def shift_moment(joint_ref, first, parts, later, nested, weights=(9, 3, 1)):
    total = None
    for now in range(8):
        at = first
        for dim, (bit, weight) in enumerate(zip((4, 2, 1), weights)):
            if now & bit and later & bit:
                at = at + nested[dim] * weight
            elif now & bit:
                at = at + weight
            elif later & bit:
                at = at + 2 * weight
        term = joint_ref[pl.ds(at, 1), :] * parts[now]
        total = term if total is None else total + term
    return total


def shifts_of(means, axes):
    turn = turned(axes, means)
    return [means[comp] - turn[comp] for comp in range(3)] + [jnp.ones_like(means[0])]


def own_cells(far_ref, out_ref):
    for hop in range(2):
        for side in range(2):
            out_ref[side, hop * 24 : hop * 24 + 24, :] = far_ref[side, hop * 40 + 8 : hop * 40 + 32, :]


def side_cells(side):
    first = side * 3
    return ((first, first + 1), (first + 5, first + 6))


def add_side(new_ref, side, came_ref, sources, nested):
    def moment_of(later):
        total = None
        for row, parts in sources:
            term = shift_moment(came_ref, row, parts, later, nested, (6, 3, 1))
            total = term if total is None else total + term
        return total

    quads = []
    for moment in (0, 4):
        up = moment_of(moment + 1)
        quads.append(moment_of(moment) - up + pltpu.roll(up, 1, 1))
    for hop, piece in enumerate((quads[0] - quads[1], quads[1])):
        rows = slice(hop * 12 + side * 8, hop * 12 + side * 8 + 4)
        new_ref[rows, :] = new_ref[rows, :] + piece[0:4, :]


def shift_kernel(step, shifts_ref, sums_ref, from_odd_ref, from_even_ref, axes_ref, mom_ref, joint_ref, shift_ref, new_ref, odd_ref, even_ref, work_ref, tot_ref, next_ref):
    add_x(sums_ref, from_odd_ref, from_even_ref, work_ref)
    means = cell_means(work_ref, tot_ref)
    shift_ref[...] = jnp.zeros_like(shift_ref)
    store_cells(shift_ref, shifts_of(means, [axes_ref[comp] for comp in range(3)]))
    nested = nested_hops(step, shifts_ref)
    for col in range(2):
        parts = corner_differences(shift_ref, ((col, col + 1), (3 + col, 4 + col)))
        for later in range(8):
            row = (col * 8 + later) * 8
            next_ref[row : row + 8, :] = mom_ref[row : row + 8, :] + shift_moment(joint_ref, col * 27, parts, later, nested)
    cell_sums(stored_moment(next_ref), new_ref)
    fill_messages_x(new_ref, 12, odd_ref, even_ref)


def wide_shift_kernel(step, shifts_ref, sums_ref, from_odd_ref, from_even_ref, axes_ref, turned_ref, joint_ref, shift_ref, new_ref, odd_ref, even_ref, work_ref, tot_ref, next_ref, far_ref, left_ref, right_ref):
    by_left, by_right = from_sides("gy", from_odd_ref[...], from_even_ref[...])
    left_ref[...] = by_left
    right_ref[...] = by_right
    add_y(sums_ref, left_ref, right_ref, work_ref)
    means = cell_means(work_ref, tot_ref, 10)
    far_ref[...] = jnp.zeros_like(far_ref)
    store_cells(far_ref, shifts_of(means, [axes_ref[comp] for comp in range(3)]), 10)
    own_cells(far_ref, shift_ref)
    nested = nested_hops(step, shifts_ref)
    for col in range(2):
        parts = corner_differences(far_ref, ((col + 1, col + 2), (col + 6, col + 7)))
        for later in range(8):
            row = (col * 8 + later) * 8
            next_ref[row : row + 8, :] = shift_moment(joint_ref, col * 27, parts, later, nested)
    cell_sums(stored_moment(next_ref), new_ref)
    new_ref[...] = new_ref[...] + turned_ref[...]
    for side, came_ref in enumerate((left_ref, right_ref)):
        for hop in range(2):
            rows = slice(hop * 12 + side * 8, hop * 12 + side * 8 + 4)
            new_ref[rows, :] = new_ref[rows, :] + came_ref[16 + hop * 4 : 20 + hop * 4, :]
        add_side(new_ref, side, came_ref, [(24, corner_differences(far_ref, side_cells(side)))], nested)
    fill_messages_x(new_ref, 12, odd_ref, even_ref)


def last_kernel(shifts_ref, code_ref, vel_ref, sums_ref, from_odd_ref, from_even_ref, axes_ref, out_hbm, means_hbm, work_ref, tot_ref, table_ref, end_ref, out_ref, means_ref, sems):
    add_x(sums_ref, from_odd_ref, from_even_ref, work_ref)
    means = cell_means(work_ref, tot_ref)
    turn = turned([axes_ref[comp] for comp in range(3)], means)
    table_ref[...] = jnp.zeros_like(table_ref)
    store_cells(table_ref, [means[comp] - turn[comp] for comp in range(3)])
    for comp in range(3):
        means_ref[comp] = means[comp][0:2, :]
    saves = [pltpu.make_async_copy(means_ref, means_hbm, sems.at[6])]
    saves[0].start()
    for col in range(2):
        for _, lanes in blocks((col,)):

            def body(rows):
                code = code_ref[col, rows, lanes]
                masks = hop_masks(code, shifts_ref, ITERS - 1)
                filled = code >= 0
                for comp in range(3):
                    value = vel_ref[comp * 2 + col, rows, lanes] + pick(table_ref, comp, col, lanes, masks)
                    end_ref[comp * 2 + col, rows, lanes] = jnp.where(filled, value, 0.0)

            over_slots(body)
        for comp in range(3):
            at = comp * 2 + col
            out_ref[at] = end_ref[at].T.astype(jnp.bfloat16)
            saves.append(pltpu.make_async_copy(out_ref.at[at], out_hbm.at[at], sems.at[at]))
            saves[-1].start()
    for save in saves:
        save.wait()


VMEM = pl.BlockSpec(memory_space=pltpu.VMEM)
SMEM = pl.BlockSpec(memory_space=pltpu.SMEM)
HBM = pl.BlockSpec(memory_space=pltpu.HBM)
BYTES = 8_000_000


def call(kernel, name, in_specs, shapes, scratch, cost=0, out_specs=None):
    return pl.pallas_call(
        kernel,
        out_shape=[jax.ShapeDtypeStruct(s, d) for s, d in shapes],
        in_specs=in_specs,
        out_specs=out_specs or [VMEM] * len(shapes),
        scratch_shapes=scratch,
        compiler_params=pltpu.CompilerParams(vmem_limit_bytes=16 * 1024 * 1024),
        cost_estimate=pl.CostEstimate(flops=0, bytes_accessed=cost, transcendentals=0) if cost else None,
        name=name,
    )


def swap(odd, even, axis):
    count = lax.axis_size(axis)
    evens = [(s, s ^ 1) for s in range(count)]
    odds = [(s, (((s - 1) % count ^ 1) + 1) % count) for s in range(count)]
    from_even = lax.ppermute(even, axis, evens)
    from_odd = lax.ppermute(odd, axis, odds)
    return from_odd, from_even


def on_device(velocity, position_code, occupancy, shifts, axis_ids):
    vel_in = velocity.reshape(6, 256, 128)
    code_in = position_code.reshape(2, 256, 128)
    occ = occupancy.reshape(2, 256)
    ids_in = axis_ids.reshape(ITERS, 2, 256)

    def rows(count):
        return ((count, 256), F32)

    def room(*shape):
        return pltpu.VMEM(shape, F32)

    vel_shape, code_shape = ((6, 128, 256), F32), ((2, 128, 256), jnp.int32)
    table_shape, axes_shape = ((2, WIDE, 256), F32), ((3, 8, 256), F32)
    moments, table = room(128, 256), room(2, WIDE, 256)
    small = [room(24, 256), room(4, 8, 256)]
    wide_small, far = [room(40, 256), room(4, 16, 256)], room(2, 80, 256)

    vel, code, sums, odd, even = call(
        start_kernel, "start", [HBM] * 5, [vel_shape, code_shape, rows(24), rows(20), rows(20)],
        [moments, pltpu.VMEM((6, 256, 128), jnp.bfloat16), pltpu.VMEM((2, 256, 128), jnp.int32), pltpu.VMEM((2, 256), jnp.int32), pltpu.VMEM((ITERS, 2, 256), jnp.int32), pltpu.SMEM((ITERS, 3), jnp.int32), pltpu.SemaphoreType.DMA((11,))],
    )(*(pltpu.with_memory_space_constraint(x, pltpu.HBM) for x in (shifts, vel_in, code_in, occ, ids_in)))

    from_odd, from_even = swap(odd, even, "gx")
    ghost_odd, ghost_even = call(
        ghost_kernel, "ghost", [SMEM, VMEM, VMEM], [rows(72), rows(72)], [room(72, 256), room(72, 256)], BYTES
    )(shifts, vel, code)
    sums, both, odd, even = call(
        first_middle_kernel, "middle0", [VMEM] * 6, [rows(24), rows(16), rows(100), rows(100)], [],
    )(sums, from_odd, from_even, ids_in, ghost_odd, ghost_even)
    from_odd, from_even = swap(odd, even, "gy")
    vel, ids, far_ids, sums, odd, even = call(
        first_kernel, "first", [SMEM] + [VMEM] * 6, [vel_shape, rows(32), rows(32), rows(24), rows(12), rows(12)],
        [moments, *wide_small, table, table, far, room(3, 2, 80, 256), room(100, 256), room(100, 256)],
    )(shifts, vel, code, sums, from_odd, from_even, both)

    shift = None
    for step in range(1, ITERS):
        last, wide = step == ITERS - 1, step == WIDE_STEP
        from_odd, from_even = swap(odd, even, "gx")
        args = [shifts, code, ids, vel] + ([] if step == 1 else [shift])
        shapes, scratch = [vel_shape, axes_shape], [table]
        if wide:
            args.append(far_ids)
            shapes = [vel_shape, ((3, 16, 256), F32), rows(24)]
            scratch = [table, moments]
        elif not last:
            shapes.append(rows(128))
        vel, axes, *more = call(
            functools.partial(turn_kernel, step), f"turn{step}", [SMEM] + [VMEM] * (len(args) - 1), shapes, scratch, BYTES,
        )(*args)
        if step == 1:
            *joints, joint_odd, joint_even = call(
                joint_kernel, "joint", [SMEM, VMEM], [rows(56), rows(56), rows(18), rows(18)], [], BYTES
            )(shifts, code)
        if last:
            out, out_means = call(
                last_kernel, "last", [SMEM] + [VMEM] * 6, [((6, 256, 128), jnp.bfloat16), ((3, 2, 256), F32)],
                [*small, table, room(6, 128, 256), pltpu.VMEM((6, 256, 128), jnp.bfloat16), room(3, 2, 256), pltpu.SemaphoreType.DMA((7,))],
                out_specs=[HBM, HBM],
            )(shifts, code, vel, sums, from_odd, from_even, axes)
        elif wide:
            sums, odd, even = call(
                wide_middle_kernel, f"middle{step}", [VMEM] * 6, [rows(24), rows(42), rows(42)], [],
            )(sums, from_odd, from_even, more[0], joint_odd, joint_even)
            from_odd, from_even = swap(odd, even, "gy")
            shift, sums, odd, even = call(
                functools.partial(wide_shift_kernel, step), f"shift{step}", [SMEM] + [VMEM] * 6,
                [table_shape, rows(24), rows(12), rows(12)], [*wide_small, moments, far, room(42, 256), room(42, 256)],
            )(shifts, sums, from_odd, from_even, axes, more[0], joints[step - 1])
        else:
            shift, sums, odd, even = call(
                functools.partial(shift_kernel, step), f"shift{step}", [SMEM] + [VMEM] * 6,
                [table_shape, rows(24), rows(12), rows(12)], [*small, moments],
            )(shifts, sums, from_odd, from_even, axes, more[0], joints[step - 1])
    return out.reshape(velocity.shape), out_means.reshape(3, *occupancy.shape)


def solution(mesh):
    in_specs = (
        P(None, "gx", "gy", None, None),
        P("gx", "gy", None, None),
        P("gx", "gy", None),
        P(),
        P(None, "gx", "gy", None),
    )
    out_specs = (P(None, "gx", "gy", None, None), P(None, "gx", "gy", None))
    return jax.shard_map(
        on_device, mesh=mesh, in_specs=in_specs, out_specs=out_specs, check_vma=False
    )
```

```python
import functools
import math

import jax
import jax.numpy as jnp
import numpy as np
from jax import lax
from jax.experimental import pallas as pl
from jax.experimental.pallas import tpu as pltpu
from jax.sharding import PartitionSpec as P

SUBDIV = 8
NAXES = 32
ITERS = 4
GOLDEN = 2.399963229728653
TURN_COS = math.cos(130.0 * math.pi / 180.0)
TURN_SIN = math.sin(130.0 * math.pi / 180.0)
ALONG = (1.0 - TURN_COS) / (TURN_SIN * TURN_SIN)

F32 = jnp.float32
CHUNK = 32
WIDE = 48
WIDE_STEP = 2


def axis_table():
    ordinal = np.arange(NAXES, dtype=np.float64)
    height = 1.0 - (2.0 * ordinal + 1.0) / NAXES
    radius = np.sqrt(1.0 - height * height)
    phases = ordinal * GOLDEN
    return TURN_SIN * np.stack([radius * np.cos(phases), radius * np.sin(phases), height])


AXES = axis_table()


def is_odd(axis):
    return lax.rem(lax.axis_index(axis), 2) == 1


def hop_masks(code, shifts_ref, step):
    hop_x = code >= (SUBDIV - shifts_ref[step, 0]) * (SUBDIV * SUBDIV)
    hop_y = (code & (SUBDIV * SUBDIV - 1)) >= (SUBDIV - shifts_ref[step, 1]) * SUBDIV
    hop_z = (code & (SUBDIV - 1)) >= SUBDIV - shifts_ref[step, 2]
    return hop_x, hop_y, hop_z


def slot_sums(values, count, col, lanes, code_ref, shifts_ref, step, mom_ref):
    def body(i, acc):
        rows = pl.ds(pl.multiple_of(i * 8, 8), 8)
        code = code_ref[col, rows, lanes]
        hop_x, hop_y, hop_z = hop_masks(code, shifts_ref, step)
        out = list(acc)
        for comp, value in enumerate(values(rows, code)):
            with_x = jnp.where(hop_x, value, 0.0)
            with_y = jnp.where(hop_y, value, 0.0)
            with_xy = jnp.where(hop_y, with_x, 0.0)
            for pair, base in ((0, value), (2, with_y), (4, with_x), (6, with_xy)):
                at = comp * 8 + pair
                out[at] = out[at] + base
                out[at + 1] = out[at + 1] + jnp.where(hop_z, base, 0.0)
        return tuple(out)

    zero = jnp.zeros((8, 128), F32)
    acc = lax.fori_loop(0, 16, body, (zero,) * (8 * count), unroll=16)
    for comp in range(count):
        for moment in range(8):
            row = (col * 8 + moment) * 8 + comp
            mom_ref[row : row + 1, lanes] = jnp.sum(acc[comp * 8 + moment], axis=0, keepdims=True)


def blocks(cols=(0, 1)):
    for col in cols:
        for half in range(2):
            yield col, slice(half * 128, half * 128 + 128)


def deposit(vel_ref, code_ref, shifts_ref, step, mom_ref, counted, cols=(0, 1)):
    for col, lanes in blocks(cols):

        def values(rows, code):
            parts = [vel_ref[comp * 2 + col, rows, lanes] for comp in range(3)]
            return parts + ([jnp.where(code >= 0, 1.0, 0.0)] if counted else [])

        slot_sums(values, 4 if counted else 3, col, lanes, code_ref, shifts_ref, step, mom_ref)


def cell_sums(moment_of, sums_ref):
    pieces = {}
    for col in range(2):
        quads = {}
        for moment in (0, 2, 4, 6):
            up = moment_of(col, moment + 1)
            quads[moment] = moment_of(col, moment) - up + pltpu.roll(up, 1, 1)
        pieces[col, 1, 1] = quads[6]
        pieces[col, 1, 0] = quads[4] - quads[6]
        pieces[col, 0, 1] = quads[2] - quads[6]
        pieces[col, 0, 0] = quads[0] - quads[2] - quads[4] + quads[6]
    for hop in range(2):
        columns = (pieces[0, hop, 0], pieces[0, hop, 1] + pieces[1, hop, 0], pieces[1, hop, 1])
        for at, piece in enumerate(columns):
            row = (hop * 3 + at) * 4
            sums_ref[row : row + 4, :] = piece[0:4, :]


def stored_moment(mom_ref):
    def moment_of(col, moment):
        row = (col * 8 + moment) * 8
        return mom_ref[row : row + 8, :]

    return moment_of


def fill_messages_y(sums_ref, odd_ref, even_ref, columns=1, first=0):
    odd = is_odd("gy")
    size = columns * 4
    for hop in range(2):
        left = sums_ref[hop * 12 : hop * 12 + size, :]
        right = sums_ref[hop * 12 + 12 - size : hop * 12 + 12, :]
        rows = slice(first + hop * size, first + hop * size + size)
        odd_ref[rows, :] = jnp.where(odd, right, left)
        even_ref[rows, :] = jnp.where(odd, left, right)


def fill_messages_x(out_ref, size, odd_ref, even_ref):
    odd = is_odd("gx")
    low, high = out_ref[0:size, :], out_ref[size : 2 * size, :]
    odd_ref[0:size, :] = jnp.where(odd, high, low)
    even_ref[0:size, :] = jnp.where(odd, low, high)


def from_sides(axis, from_odd, from_even):
    odd = is_odd(axis)
    return jnp.where(odd, from_even, from_odd), jnp.where(odd, from_odd, from_even)


def start_kernel(shifts_hbm, vel_hbm, code_hbm, occ_hbm, ids_hbm, vel_ref, code_ref, sums_ref, odd_ref, even_ref, mom_ref, vel_in_ref, code_in_ref, occ_ref, ids_ref, shifts_ref, sems):
    fetch_shifts = pltpu.make_async_copy(shifts_hbm, shifts_ref, sems.at[10])
    fetch_occ = pltpu.make_async_copy(occ_hbm, occ_ref, sems.at[8])
    fetch_ids = pltpu.make_async_copy(ids_hbm, ids_ref, sems.at[9])
    copies = []
    for col in range(2):
        copies.append(pltpu.make_async_copy(code_hbm.at[col], code_in_ref.at[col], sems.at[col]))
    for at in range(6):
        copies.append(pltpu.make_async_copy(vel_hbm.at[at], vel_in_ref.at[at], sems.at[2 + at]))
    fetch_occ.start()
    for at in (0, 2, 4, 6, 1, 3, 5, 7):
        copies[at].start()
    fetch_ids.start()
    fetch_shifts.start()
    mom_ref[...] = jnp.zeros_like(mom_ref)
    slot = lax.broadcasted_iota(jnp.int32, (128, 256), 0)
    fetch_occ.wait()
    fetch_shifts.wait()
    for col in range(2):
        filled = slot < occ_ref[col : col + 1, :]
        copies[col].wait()
        code_ref[col] = jnp.where(filled, code_in_ref[col].T, -1)
        for comp in range(3):
            at = comp * 2 + col
            copies[2 + at].wait()
            vel_ref[at] = jnp.where(filled, vel_in_ref[at].astype(F32).T, 0.0)
        deposit(vel_ref, code_ref, shifts_ref, 0, mom_ref, True, (col,))
    fetch_ids.wait()
    for step in range(ITERS):
        ids = ids_ref[step].astype(F32)
        rows = slice(12 + step * 2, 14 + step * 2)
        odd_ref[rows, :] = ids
        even_ref[rows, :] = ids
    cell_sums(stored_moment(mom_ref), sums_ref)
    fill_messages_x(sums_ref, 12, odd_ref, even_ref)


def add_x(sums_ref, from_odd_ref, from_even_ref, out_ref):
    by_low, by_high = from_sides("gx", from_odd_ref[0:12, :], from_even_ref[0:12, :])
    out_ref[0:12, :] = sums_ref[0:12, :] + by_low
    out_ref[12:24, :] = sums_ref[12:24, :] + by_high


def add_y(sums_ref, by_left_ref, by_right_ref, out_ref):
    for hop in range(2):
        at, own, rows = hop * 20, hop * 12, slice(hop * 8, hop * 8 + 8)
        out_ref[at : at + 8, :] = by_left_ref[rows, :]
        out_ref[at + 12 : at + 20, :] = by_right_ref[rows, :]
        out_ref[at + 8 : at + 12, :] = sums_ref[own + 4 : own + 8, :]
        out_ref[at + 4 : at + 8, :] = out_ref[at + 4 : at + 8, :] + sums_ref[own : own + 4, :]
        out_ref[at + 12 : at + 16, :] = out_ref[at + 12 : at + 16, :] + sums_ref[own + 8 : own + 12, :]


def first_middle_kernel(sums_ref, from_odd_ref, from_even_ref, ids_ref, ghost_odd_ref, ghost_even_ref, out_ref, both_ref, odd_ref, even_ref):
    add_x(sums_ref, from_odd_ref, from_even_ref, out_ref)
    fill_messages_y(out_ref, odd_ref, even_ref, 2)
    for step in range(ITERS):
        both_ref[step * 2 : step * 2 + 2, :] = ids_ref[step].astype(F32)
    _, by_high = from_sides("gx", from_odd_ref[12:20, :], from_even_ref[12:20, :])
    both_ref[8:16, :] = by_high
    for ref in (odd_ref, even_ref):
        for x in range(2):
            for step in range(ITERS):
                ref[16 + x * 4 + step : 17 + x * 4 + step, :] = both_ref[x * 8 + step * 2 : x * 8 + step * 2 + 1, :]
            for k, step in enumerate((0, WIDE_STEP)):
                ref[24 + x * 2 + k : 25 + x * 2 + k, :] = both_ref[x * 8 + step * 2 + 1 : x * 8 + step * 2 + 2, :]
    odd_ref[28:100, :] = ghost_odd_ref[...]
    even_ref[28:100, :] = ghost_even_ref[...]


def wide_middle_kernel(sums_ref, from_odd_ref, from_even_ref, turned_ref, joint_odd_ref, joint_even_ref, out_ref, odd_ref, even_ref):
    add_x(sums_ref, from_odd_ref, from_even_ref, out_ref)
    fill_messages_y(out_ref, odd_ref, even_ref, 2)
    fill_messages_y(turned_ref, odd_ref, even_ref, 1, 16)
    odd_ref[24:42, :] = joint_odd_ref[...]
    even_ref[24:42, :] = joint_even_ref[...]


def cell_means(work_ref, tot_ref, cells=6):
    tot_ref[...] = jnp.zeros_like(tot_ref)
    for cell in range(cells):
        for comp in range(4):
            tot_ref[comp, cell : cell + 1, :] = work_ref[cell * 4 + comp : cell * 4 + comp + 1, :]
    count = jnp.maximum(tot_ref[3], 1.0)
    return [tot_ref[comp] / count for comp in range(3)]


def cell_axes(ids):
    axes = [jnp.zeros(ids.shape, F32) for _ in range(3)]
    for k in range(NAXES):
        match = ids == float(k)
        axes = [jnp.where(match, float(AXES[comp, k]), axes[comp]) for comp in range(3)]
    return axes


def turned(axis, vec):
    along = (axis[0] * vec[0] + axis[1] * vec[1] + axis[2] * vec[2]) * ALONG
    out = []
    for comp in range(3):
        b, c = (comp + 1) % 3, (comp + 2) % 3
        out.append(TURN_COS * vec[comp] + (axis[b] * vec[c] - axis[c] * vec[b]) + along * axis[comp])
    return out


def next_z(value):
    return pltpu.roll(value, 255, 1)


def store_cells(table_ref, parts, cells=6):
    for cell in range(cells):
        for comp, part in enumerate(parts):
            table_ref[0, cell * 8 + comp : cell * 8 + comp + 1, :] = part[cell : cell + 1, :]
    table_ref[1] = next_z(table_ref[0])


def pick(table_ref, comp, col, lanes, masks):
    hop_x, hop_y, hop_z = masks
    by_x = []
    for step_x in range(2):
        by_y = []
        for step_y in range(2):
            row = (step_x * 3 + col + step_y) * 8 + comp
            by_y.append(jnp.where(hop_z, table_ref[1, row : row + 1, lanes], table_ref[0, row : row + 1, lanes]))
        by_x.append(jnp.where(hop_y, by_y[1], by_y[0]))
    return jnp.where(hop_x, by_x[1], by_x[0])


def over_slots(body):
    def run(i, carry):
        body(pl.ds(pl.multiple_of(i * CHUNK, CHUNK), CHUNK))
        return carry

    lax.fori_loop(0, 128 // CHUNK, run, 0, unroll=128 // CHUNK)


def first_kernel(shifts_ref, sums_ref, from_odd_ref, from_even_ref, both_ref, joint_ref, _, ids_ref, far_ids_ref, shift_ref, new_ref, odd_ref, even_ref, next_ref, work_ref, tot_ref, far_ref, turn_ref, left_ref, right_ref):
    by_left, by_right = from_sides("gy", from_odd_ref[...], from_even_ref[...])
    left_ref[...] = by_left
    right_ref[...] = by_right
    ids_ref[...] = jnp.zeros_like(ids_ref)
    for x in range(2):
        for t in range(ITERS):
            row = t * 8 + x * 3
            ids_ref[row : row + 2, :] = both_ref[x * 8 + t * 2 : x * 8 + t * 2 + 2, :]
            ids_ref[row + 2 : row + 3, :] = right_ref[16 + x * 4 + t : 17 + x * 4 + t, :]
    far_ids_ref[...] = jnp.zeros_like(far_ids_ref)
    for k, t in enumerate((0, WIDE_STEP)):
        for x in range(2):
            row, outer = k * 16 + x * 5, slice(24 + x * 2 + k, 25 + x * 2 + k)
            far_ids_ref[row : row + 1, :] = left_ref[outer, :]
            far_ids_ref[row + 1 : row + 4, :] = ids_ref[t * 8 + x * 3 : t * 8 + x * 3 + 3, :]
            far_ids_ref[row + 4 : row + 5, :] = right_ref[outer, :]
    add_y(sums_ref, left_ref, right_ref, work_ref)
    means = cell_means(work_ref, tot_ref, 10)
    axes = cell_axes(far_ids_ref[0:16, :])
    far_ref[...] = jnp.zeros_like(far_ref)
    store_cells(far_ref, shifts_of(means, axes), 10)
    own_cells(far_ref, shift_ref)
    turn_ref[...] = jnp.zeros_like(turn_ref)
    zero = jnp.zeros((16, 256), F32)
    for k in range(3):
        unit = [zero + (1.0 if comp == k else 0.0) for comp in range(3)]
        store_cells(turn_ref.at[k], turned(axes, unit), 10)
    nested = nested_hops(0, shifts_ref)

    def sources_of(cells, first, size):
        tables = [far_ref] + [turn_ref.at[k] for k in range(3)]
        return [(first + at * size, corner_differences(table, cells)) for at, table in enumerate(tables)]

    for col in range(2):
        sources = sources_of(((col + 1, col + 2), (col + 6, col + 7)), col * 27, 54)
        for later in range(8):
            row = (col * 8 + later) * 8
            next_ref[row : row + 8, :] = joint_moment(joint_ref, sources, later, nested, (9, 3, 1))
    cell_sums(stored_moment(next_ref), new_ref)
    for side, came_ref in enumerate((left_ref, right_ref)):
        add_side(new_ref, side, came_ref, sources_of(side_cells(side), 28, 18), nested)
    fill_messages_x(new_ref, 12, odd_ref, even_ref)


def joint_sums(vel_ref, code_ref, shifts_ref, t, out_ref):
    def classes(value, now, later):
        out = []
        for by_x in (value, jnp.where(now[0], value, 0), jnp.where(later[0], value, 0)):
            out += [by_x, jnp.where(now[1], by_x, 0), jnp.where(later[1], by_x, 0)]
        return out

    def body(col, lanes, comp, counts, i, acc):
        rows = pl.ds(pl.multiple_of(i * 8, 8), 8)
        code = code_ref[col, rows, lanes]
        now, later = hop_masks(code, shifts_ref, t), hop_masks(code, shifts_ref, t + 1)
        out = []
        if comp is not None:
            for value in classes(vel_ref[comp * 2 + col, rows, lanes], now, later):
                out += [value, jnp.where(now[2], value, 0.0), jnp.where(later[2], value, 0.0)]
        if counts:
            word = jnp.where(now[2], 1 + 256, 1) + jnp.where(later[2], 65536, 0)
            out += classes(jnp.where(code >= 0, word, 0), now, later)
        return tuple(a + b for a, b in zip(acc, out))

    zero, none = (jnp.zeros((8, 128), F32),) * 27, (jnp.zeros((8, 128), jnp.int32),) * 9
    for col, lanes in blocks():
        for comp, counts in ((None, True),) if vel_ref is None else ((0, False), (1, False), (2, True)):
            start = (() if comp is None else zero) + (none if counts else ())
            acc = lax.fori_loop(0, 16, functools.partial(body, col, lanes, comp, counts), start, unroll=8)
            if comp is not None:
                for at in range(27):
                    row = 54 + comp * 54 + col * 27 + at
                    out_ref[row : row + 1, lanes] = jnp.sum(acc[at], axis=0, keepdims=True)
            if counts:
                for at, word in enumerate(acc[-9:]):
                    for z in range(3):
                        part = lax.shift_right_logical(word, 8 * z) & 255
                        row = col * 27 + at * 3 + z
                        out_ref[row : row + 1, lanes] = jnp.sum(part.astype(F32), axis=0, keepdims=True)


def boundary_sums(joint_ref, kinds, nested, odd_ref, even_ref):
    odd = is_odd("gy")
    for kind in range(kinds):
        for x in range(3):
            for y in range(2):
                for z in range(3):
                    first = kind * 54 + x * 9 + z
                    hopped = (nested[1] if y else 2) * 3
                    left = joint_ref[first + y * 3 : first + y * 3 + 1, :] - joint_ref[pl.ds(first + hopped, 1), :]
                    right = joint_ref[pl.ds(27 + first + hopped, 1), :]
                    row = kind * 18 + x * 6 + y * 3 + z
                    odd_ref[row : row + 1, :] = jnp.where(odd, right, left)
                    even_ref[row : row + 1, :] = jnp.where(odd, left, right)


def class_kernel(shifts_ref, vel_ref, code_ref, out_ref, odd_ref, even_ref):
    joint_sums(vel_ref, code_ref, shifts_ref, 0, out_ref)
    boundary_sums(out_ref, 4, nested_hops(0, shifts_ref), odd_ref, even_ref)


def joint_kernel(shifts_ref, code_ref, first_ref, second_ref, odd_ref, even_ref):
    joint_sums(None, code_ref, shifts_ref, 1, first_ref)
    joint_sums(None, code_ref, shifts_ref, 2, second_ref)
    boundary_sums(second_ref, 1, nested_hops(WIDE_STEP, shifts_ref), odd_ref, even_ref)


def turn_kernel(step, *refs):
    shifts_ref, code_ref, ids_ref, vel_ref, last_ref, *refs = refs
    if step == 1:
        *refs, before_ref = refs
        before_ref[...] = jnp.zeros_like(before_ref)
        store_cells(before_ref, cell_axes(ids_ref[0:8, :]))
    if step == WIDE_STEP:
        far_ids_ref, out_ref, axes_ref, sums_ref, table_ref, mom_ref = refs
        for comp, axis in enumerate(cell_axes(far_ids_ref[16:32, :])):
            axes_ref[comp] = axis
    elif step < ITERS - 1:
        out_ref, axes_ref, mom_ref, table_ref = refs
    else:
        out_ref, axes_ref, table_ref = refs
    axes = cell_axes(ids_ref[step * 8 : step * 8 + 8, :])
    if step != WIDE_STEP:
        for comp in range(3):
            axes_ref[comp] = axes[comp]
    table_ref[...] = jnp.zeros_like(table_ref)
    store_cells(table_ref, axes)
    for col, lanes in blocks():

        def body(rows):
            code = code_ref[col, rows, lanes]
            vel = [vel_ref[comp * 2 + col, rows, lanes] for comp in range(3)]
            masks = hop_masks(code, shifts_ref, step - 1)
            if step == 1:
                vel = turned([pick(before_ref, comp, col, lanes, masks) for comp in range(3)], vel)
            filled = code >= 0
            vel = [jnp.where(filled, vel[comp] + pick(last_ref, comp, col, lanes, masks), 0.0) for comp in range(3)]
            masks = hop_masks(code, shifts_ref, step)
            turn = turned([pick(table_ref, comp, col, lanes, masks) for comp in range(3)], vel)
            for comp in range(3):
                out_ref[comp * 2 + col, rows, lanes] = turn[comp]

        over_slots(body)
    if step < ITERS - 1:
        mom_ref[...] = jnp.zeros_like(mom_ref)
        deposit(out_ref, code_ref, shifts_ref, step + 1, mom_ref, False)
    if step == WIDE_STEP:
        cell_sums(stored_moment(mom_ref), sums_ref)


def nested_hops(step, shifts_ref):
    return [jnp.where(shifts_ref[step, dim] <= shifts_ref[step + 1, dim], 1, 2) for dim in range(3)]


def corner_differences(shift_ref, cells):
    parts = {}
    for corner in range(8):
        cell = cells[corner >> 2][corner >> 1 & 1]
        parts[corner] = shift_ref[corner & 1, cell * 8 : cell * 8 + 8, :]
    for bit in (1, 2, 4):
        for corner in range(8):
            if corner & bit:
                parts[corner] = parts[corner] - parts[corner ^ bit]
    return parts


def joint_moment(joint_ref, sources, later, nested, weights):
    total = None
    for now in range(8):
        at = 0
        for dim, (bit, weight) in enumerate(zip((4, 2, 1), weights)):
            if now & bit and later & bit:
                at = at + nested[dim] * weight
            elif now & bit:
                at = at + weight
            elif later & bit:
                at = at + 2 * weight
        for first, parts in sources:
            term = joint_ref[pl.ds(first + at, 1), :] * parts[now]
            total = term if total is None else total + term
    return total


def shifts_of(means, axes):
    turn = turned(axes, means)
    return [means[comp] - turn[comp] for comp in range(3)] + [jnp.ones_like(means[0])]


def own_cells(far_ref, out_ref):
    for hop in range(2):
        for side in range(2):
            out_ref[side, hop * 24 : hop * 24 + 24, :] = far_ref[side, hop * 40 + 8 : hop * 40 + 32, :]


def side_cells(side):
    first = side * 3
    return ((first, first + 1), (first + 5, first + 6))


def add_side(new_ref, side, came_ref, sources, nested):
    def moment_of(later):
        return joint_moment(came_ref, sources, later, nested, (6, 3, 1))

    quads = []
    for moment in (0, 4):
        up = moment_of(moment + 1)
        quads.append(moment_of(moment) - up + pltpu.roll(up, 1, 1))
    for hop, piece in enumerate((quads[0] - quads[1], quads[1])):
        rows = slice(hop * 12 + side * 8, hop * 12 + side * 8 + 4)
        new_ref[rows, :] = new_ref[rows, :] + piece[0:4, :]


def shift_kernel(step, shifts_ref, sums_ref, from_odd_ref, from_even_ref, axes_ref, mom_ref, joint_ref, shift_ref, new_ref, odd_ref, even_ref, work_ref, tot_ref, next_ref):
    add_x(sums_ref, from_odd_ref, from_even_ref, work_ref)
    means = cell_means(work_ref, tot_ref)
    shift_ref[...] = jnp.zeros_like(shift_ref)
    store_cells(shift_ref, shifts_of(means, [axes_ref[comp] for comp in range(3)]))
    nested = nested_hops(step, shifts_ref)
    for col in range(2):
        parts = corner_differences(shift_ref, ((col, col + 1), (3 + col, 4 + col)))
        for later in range(8):
            row = (col * 8 + later) * 8
            next_ref[row : row + 8, :] = mom_ref[row : row + 8, :] + joint_moment(joint_ref, [(col * 27, parts)], later, nested, (9, 3, 1))
    cell_sums(stored_moment(next_ref), new_ref)
    fill_messages_x(new_ref, 12, odd_ref, even_ref)


def wide_shift_kernel(step, shifts_ref, sums_ref, from_odd_ref, from_even_ref, axes_ref, turned_ref, joint_ref, shift_ref, new_ref, odd_ref, even_ref, work_ref, tot_ref, next_ref, far_ref, left_ref, right_ref):
    by_left, by_right = from_sides("gy", from_odd_ref[...], from_even_ref[...])
    left_ref[...] = by_left
    right_ref[...] = by_right
    add_y(sums_ref, left_ref, right_ref, work_ref)
    means = cell_means(work_ref, tot_ref, 10)
    far_ref[...] = jnp.zeros_like(far_ref)
    store_cells(far_ref, shifts_of(means, [axes_ref[comp] for comp in range(3)]), 10)
    own_cells(far_ref, shift_ref)
    nested = nested_hops(step, shifts_ref)
    for col in range(2):
        parts = corner_differences(far_ref, ((col + 1, col + 2), (col + 6, col + 7)))
        for later in range(8):
            row = (col * 8 + later) * 8
            next_ref[row : row + 8, :] = joint_moment(joint_ref, [(col * 27, parts)], later, nested, (9, 3, 1))
    cell_sums(stored_moment(next_ref), new_ref)
    new_ref[...] = new_ref[...] + turned_ref[...]
    for side, came_ref in enumerate((left_ref, right_ref)):
        for hop in range(2):
            rows = slice(hop * 12 + side * 8, hop * 12 + side * 8 + 4)
            new_ref[rows, :] = new_ref[rows, :] + came_ref[16 + hop * 4 : 20 + hop * 4, :]
        add_side(new_ref, side, came_ref, [(24, corner_differences(far_ref, side_cells(side)))], nested)
    fill_messages_x(new_ref, 12, odd_ref, even_ref)


def last_kernel(shifts_ref, code_ref, vel_ref, sums_ref, from_odd_ref, from_even_ref, axes_ref, out_hbm, means_hbm, work_ref, tot_ref, table_ref, end_ref, out_ref, means_ref, sems):
    add_x(sums_ref, from_odd_ref, from_even_ref, work_ref)
    means = cell_means(work_ref, tot_ref)
    turn = turned([axes_ref[comp] for comp in range(3)], means)
    table_ref[...] = jnp.zeros_like(table_ref)
    store_cells(table_ref, [means[comp] - turn[comp] for comp in range(3)])
    for comp in range(3):
        means_ref[comp] = means[comp][0:2, :]
    saves = [pltpu.make_async_copy(means_ref, means_hbm, sems.at[6])]
    saves[0].start()
    for col in range(2):
        for _, lanes in blocks((col,)):

            def body(rows):
                code = code_ref[col, rows, lanes]
                masks = hop_masks(code, shifts_ref, ITERS - 1)
                filled = code >= 0
                for comp in range(3):
                    value = vel_ref[comp * 2 + col, rows, lanes] + pick(table_ref, comp, col, lanes, masks)
                    end_ref[comp * 2 + col, rows, lanes] = jnp.where(filled, value, 0.0)

            over_slots(body)
        for comp in range(3):
            at = comp * 2 + col
            out_ref[at] = end_ref[at].T.astype(jnp.bfloat16)
            saves.append(pltpu.make_async_copy(out_ref.at[at], out_hbm.at[at], sems.at[at]))
            saves[-1].start()
    for save in saves:
        save.wait()


VMEM = pl.BlockSpec(memory_space=pltpu.VMEM)
SMEM = pl.BlockSpec(memory_space=pltpu.SMEM)
HBM = pl.BlockSpec(memory_space=pltpu.HBM)
BYTES = 8_000_000


def call(kernel, name, in_specs, shapes, scratch, cost=0, out_specs=None):
    return pl.pallas_call(
        kernel,
        out_shape=[jax.ShapeDtypeStruct(s, d) for s, d in shapes],
        in_specs=in_specs,
        out_specs=out_specs or [VMEM] * len(shapes),
        scratch_shapes=scratch,
        compiler_params=pltpu.CompilerParams(vmem_limit_bytes=16 * 1024 * 1024),
        cost_estimate=pl.CostEstimate(flops=0, bytes_accessed=cost, transcendentals=0) if cost else None,
        name=name,
    )


def swap(odd, even, axis):
    count = lax.axis_size(axis)
    evens = [(s, s ^ 1) for s in range(count)]
    odds = [(s, (((s - 1) % count ^ 1) + 1) % count) for s in range(count)]
    from_even = lax.ppermute(even, axis, evens)
    from_odd = lax.ppermute(odd, axis, odds)
    return from_odd, from_even


def on_device(velocity, position_code, occupancy, shifts, axis_ids):
    vel_in = velocity.reshape(6, 256, 128)
    code_in = position_code.reshape(2, 256, 128)
    occ = occupancy.reshape(2, 256)
    ids_in = axis_ids.reshape(ITERS, 2, 256)

    def rows(count):
        return ((count, 256), F32)

    def room(*shape):
        return pltpu.VMEM(shape, F32)

    vel_shape, code_shape = ((6, 128, 256), F32), ((2, 128, 256), jnp.int32)
    table_shape, axes_shape = ((2, WIDE, 256), F32), ((3, 8, 256), F32)
    moments, table = room(128, 256), room(2, WIDE, 256)
    small = [room(24, 256), room(4, 8, 256)]
    wide_small, far = [room(40, 256), room(4, 16, 256)], room(2, 80, 256)

    vel, code, sums, odd, even = call(
        start_kernel, "start", [HBM] * 5, [vel_shape, code_shape, rows(24), rows(20), rows(20)],
        [moments, pltpu.VMEM((6, 256, 128), jnp.bfloat16), pltpu.VMEM((2, 256, 128), jnp.int32), pltpu.VMEM((2, 256), jnp.int32), pltpu.VMEM((ITERS, 2, 256), jnp.int32), pltpu.SMEM((ITERS, 3), jnp.int32), pltpu.SemaphoreType.DMA((11,))],
    )(*(pltpu.with_memory_space_constraint(x, pltpu.HBM) for x in (shifts, vel_in, code_in, occ, ids_in)))

    from_odd, from_even = swap(odd, even, "gx")
    classes, class_odd, class_even = call(
        class_kernel, "classes", [SMEM, VMEM, VMEM], [rows(216), rows(72), rows(72)], [], BYTES
    )(shifts, vel, code)
    sums, both, odd, even = call(
        first_middle_kernel, "middle0", [VMEM] * 6, [rows(24), rows(16), rows(100), rows(100)], [],
    )(sums, from_odd, from_even, ids_in, class_odd, class_even)
    from_odd, from_even = swap(odd, even, "gy")
    *joints, joint_odd, joint_even = call(
        joint_kernel, "joint", [SMEM, VMEM], [rows(54), rows(54), rows(18), rows(18)], [], BYTES
    )(shifts, code)
    ids, far_ids, shift, sums, odd, even = call(
        first_kernel, "first", [SMEM] + [VMEM] * 6, [rows(32), rows(32), table_shape, rows(24), rows(12), rows(12)],
        [moments, *wide_small, far, room(3, 2, 80, 256), room(100, 256), room(100, 256)],
    )(shifts, sums, from_odd, from_even, both, classes, joints[0])

    for step in range(1, ITERS):
        last, wide = step == ITERS - 1, step == WIDE_STEP
        from_odd, from_even = swap(odd, even, "gx")
        args = [shifts, code, ids, vel, shift]
        shapes, scratch = [vel_shape, axes_shape], [table] * (2 if step == 1 else 1)
        if wide:
            args.append(far_ids)
            shapes = [vel_shape, ((3, 16, 256), F32), rows(24)]
            scratch = [table, moments]
        elif not last:
            shapes.append(rows(128))
        vel, axes, *more = call(
            functools.partial(turn_kernel, step), f"turn{step}", [SMEM] + [VMEM] * (len(args) - 1), shapes, scratch, BYTES,
        )(*args)
        if last:
            out, out_means = call(
                last_kernel, "last", [SMEM] + [VMEM] * 6, [((6, 256, 128), jnp.bfloat16), ((3, 2, 256), F32)],
                [*small, table, room(6, 128, 256), pltpu.VMEM((6, 256, 128), jnp.bfloat16), room(3, 2, 256), pltpu.SemaphoreType.DMA((7,))],
                out_specs=[HBM, HBM],
            )(shifts, code, vel, sums, from_odd, from_even, axes)
        elif wide:
            sums, odd, even = call(
                wide_middle_kernel, f"middle{step}", [VMEM] * 6, [rows(24), rows(42), rows(42)], [],
            )(sums, from_odd, from_even, more[0], joint_odd, joint_even)
            from_odd, from_even = swap(odd, even, "gy")
            shift, sums, odd, even = call(
                functools.partial(wide_shift_kernel, step), f"shift{step}", [SMEM] + [VMEM] * 6,
                [table_shape, rows(24), rows(12), rows(12)], [*wide_small, moments, far, room(42, 256), room(42, 256)],
            )(shifts, sums, from_odd, from_even, axes, more[0], joints[step - 1])
        else:
            shift, sums, odd, even = call(
                functools.partial(shift_kernel, step), f"shift{step}", [SMEM] + [VMEM] * 6,
                [table_shape, rows(24), rows(12), rows(12)], [*small, moments],
            )(shifts, sums, from_odd, from_even, axes, more[0], joints[step - 1])
    return out.reshape(velocity.shape), out_means.reshape(3, *occupancy.shape)


def solution(mesh):
    in_specs = (
        P(None, "gx", "gy", None, None),
        P("gx", "gy", None, None),
        P("gx", "gy", None),
        P(),
        P(None, "gx", "gy", None),
    )
    out_specs = (P(None, "gx", "gy", None, None), P(None, "gx", "gy", None))
    return jax.shard_map(
        on_device, mesh=mesh, in_specs=in_specs, out_specs=out_specs, check_vma=False
    )
```

```python
import functools
import math

import jax
import jax.numpy as jnp
import numpy as np
from jax import lax
from jax.experimental import pallas as pl
from jax.experimental.pallas import tpu as pltpu
from jax.sharding import PartitionSpec as P

SUBDIV = 8
NAXES = 32
ITERS = 4
GOLDEN = 2.399963229728653
TURN_COS = math.cos(130.0 * math.pi / 180.0)
TURN_SIN = math.sin(130.0 * math.pi / 180.0)
ALONG = (1.0 - TURN_COS) / (TURN_SIN * TURN_SIN)

F32 = jnp.float32
CHUNK = 32
WIDE = 48
WIDE_STEP = 2


def axis_table():
    ordinal = np.arange(NAXES, dtype=np.float64)
    height = 1.0 - (2.0 * ordinal + 1.0) / NAXES
    radius = np.sqrt(1.0 - height * height)
    phases = ordinal * GOLDEN
    return TURN_SIN * np.stack([radius * np.cos(phases), radius * np.sin(phases), height])


AXES = axis_table()


def is_odd(axis):
    return lax.rem(lax.axis_index(axis), 2) == 1


def hop_limits(shifts_ref, step):
    return [(SUBDIV - shifts_ref[step, dim]) * SUBDIV ** (2 - dim) for dim in range(3)]


def hop_masks(code, limits):
    hop_x = code >= limits[0]
    hop_y = (code & (SUBDIV * SUBDIV - 1)) >= limits[1]
    hop_z = (code & (SUBDIV - 1)) >= limits[2]
    return hop_x, hop_y, hop_z


def slot_sums(values, count, col, lanes, code_ref, shifts_ref, step, mom_ref):
    def body(i, acc):
        rows = pl.ds(pl.multiple_of(i * 8, 8), 8)
        code = code_ref[col, rows, lanes]
        hop_x, hop_y, hop_z = hop_masks(code, hop_limits(shifts_ref, step))
        out = list(acc)
        for comp, value in enumerate(values(rows, code)):
            with_x = jnp.where(hop_x, value, 0.0)
            with_y = jnp.where(hop_y, value, 0.0)
            with_xy = jnp.where(hop_y, with_x, 0.0)
            for pair, base in ((0, value), (2, with_y), (4, with_x), (6, with_xy)):
                at = comp * 8 + pair
                out[at] = out[at] + base
                out[at + 1] = out[at + 1] + jnp.where(hop_z, base, 0.0)
        return tuple(out)

    zero = jnp.zeros((8, 128), F32)
    acc = lax.fori_loop(0, 16, body, (zero,) * (8 * count), unroll=16)
    for comp in range(count):
        for moment in range(8):
            row = (col * 8 + moment) * 8 + comp
            mom_ref[row : row + 1, lanes] = jnp.sum(acc[comp * 8 + moment], axis=0, keepdims=True)


def blocks(cols=(0, 1)):
    for col in cols:
        for half in range(2):
            yield col, slice(half * 128, half * 128 + 128)


def deposit(vel_ref, code_ref, shifts_ref, step, mom_ref, counted, cols=(0, 1)):
    for col, lanes in blocks(cols):

        def values(rows, code):
            parts = [vel_ref[comp * 2 + col, rows, lanes] for comp in range(3)]
            return parts + ([jnp.where(code >= 0, 1.0, 0.0)] if counted else [])

        slot_sums(values, 4 if counted else 3, col, lanes, code_ref, shifts_ref, step, mom_ref)


def cell_sums(moment_of, sums_ref):
    pieces = {}
    for col in range(2):
        quads = {}
        for moment in (0, 2, 4, 6):
            up = moment_of(col, moment + 1)
            quads[moment] = moment_of(col, moment) - up + pltpu.roll(up, 1, 1)
        pieces[col, 1, 1] = quads[6]
        pieces[col, 1, 0] = quads[4] - quads[6]
        pieces[col, 0, 1] = quads[2] - quads[6]
        pieces[col, 0, 0] = quads[0] - quads[2] - quads[4] + quads[6]
    for hop in range(2):
        columns = (pieces[0, hop, 0], pieces[0, hop, 1] + pieces[1, hop, 0], pieces[1, hop, 1])
        for at, piece in enumerate(columns):
            row = (hop * 3 + at) * 4
            sums_ref[row : row + 4, :] = piece[0:4, :]


def stored_moment(mom_ref):
    def moment_of(col, moment):
        row = (col * 8 + moment) * 8
        return mom_ref[row : row + 8, :]

    return moment_of


def fill_messages_y(sums_ref, odd_ref, even_ref, columns=1, first=0):
    odd = is_odd("gy")
    size = columns * 4
    for hop in range(2):
        left = sums_ref[hop * 12 : hop * 12 + size, :]
        right = sums_ref[hop * 12 + 12 - size : hop * 12 + 12, :]
        rows = slice(first + hop * size, first + hop * size + size)
        odd_ref[rows, :] = jnp.where(odd, right, left)
        even_ref[rows, :] = jnp.where(odd, left, right)


def fill_messages_x(out_ref, size, odd_ref, even_ref):
    odd = is_odd("gx")
    low, high = out_ref[0:size, :], out_ref[size : 2 * size, :]
    odd_ref[0:size, :] = jnp.where(odd, high, low)
    even_ref[0:size, :] = jnp.where(odd, low, high)


def from_sides(axis, from_odd, from_even):
    odd = is_odd(axis)
    return jnp.where(odd, from_even, from_odd), jnp.where(odd, from_odd, from_even)


def start_kernel(shifts_hbm, vel_hbm, code_hbm, occ_hbm, ids_hbm, vel_ref, code_ref, sums_ref, odd_ref, even_ref, mom_ref, vel_in_ref, code_in_ref, occ_ref, ids_ref, shifts_ref, sems):
    fetch_shifts = pltpu.make_async_copy(shifts_hbm, shifts_ref, sems.at[10])
    fetch_occ = pltpu.make_async_copy(occ_hbm, occ_ref, sems.at[8])
    fetch_ids = pltpu.make_async_copy(ids_hbm, ids_ref, sems.at[9])
    copies = []
    for col in range(2):
        copies.append(pltpu.make_async_copy(code_hbm.at[col], code_in_ref.at[col], sems.at[col]))
    for at in range(6):
        copies.append(pltpu.make_async_copy(vel_hbm.at[at], vel_in_ref.at[at], sems.at[2 + at]))
    fetch_occ.start()
    for at in (0, 2, 4, 6, 1, 3, 5, 7):
        copies[at].start()
    fetch_ids.start()
    fetch_shifts.start()
    mom_ref[...] = jnp.zeros_like(mom_ref)
    slot = lax.broadcasted_iota(jnp.int32, (128, 256), 0)
    fetch_occ.wait()
    fetch_shifts.wait()
    for col in range(2):
        filled = slot < occ_ref[col : col + 1, :]
        copies[col].wait()
        code_ref[col] = jnp.where(filled, code_in_ref[col].T, -1)
        for comp in range(3):
            at = comp * 2 + col
            copies[2 + at].wait()
            vel_ref[at] = jnp.where(filled, vel_in_ref[at].astype(F32).T, 0.0)
        deposit(vel_ref, code_ref, shifts_ref, 0, mom_ref, True, (col,))
    fetch_ids.wait()
    for step in range(ITERS):
        ids = ids_ref[step].astype(F32)
        rows = slice(12 + step * 2, 14 + step * 2)
        odd_ref[rows, :] = ids
        even_ref[rows, :] = ids
    cell_sums(stored_moment(mom_ref), sums_ref)
    fill_messages_x(sums_ref, 12, odd_ref, even_ref)


def add_x(sums_ref, from_odd_ref, from_even_ref, out_ref):
    by_low, by_high = from_sides("gx", from_odd_ref[0:12, :], from_even_ref[0:12, :])
    out_ref[0:12, :] = sums_ref[0:12, :] + by_low
    out_ref[12:24, :] = sums_ref[12:24, :] + by_high


def add_y(sums_ref, by_left_ref, by_right_ref, out_ref):
    for hop in range(2):
        at, own, rows = hop * 20, hop * 12, slice(hop * 8, hop * 8 + 8)
        out_ref[at : at + 8, :] = by_left_ref[rows, :]
        out_ref[at + 12 : at + 20, :] = by_right_ref[rows, :]
        out_ref[at + 8 : at + 12, :] = sums_ref[own + 4 : own + 8, :]
        out_ref[at + 4 : at + 8, :] = out_ref[at + 4 : at + 8, :] + sums_ref[own : own + 4, :]
        out_ref[at + 12 : at + 16, :] = out_ref[at + 12 : at + 16, :] + sums_ref[own + 8 : own + 12, :]


def first_middle_kernel(sums_ref, from_odd_ref, from_even_ref, ids_ref, ghost_odd_ref, ghost_even_ref, out_ref, both_ref, odd_ref, even_ref):
    add_x(sums_ref, from_odd_ref, from_even_ref, out_ref)
    fill_messages_y(out_ref, odd_ref, even_ref, 2)
    for step in range(ITERS):
        both_ref[step * 2 : step * 2 + 2, :] = ids_ref[step].astype(F32)
    _, by_high = from_sides("gx", from_odd_ref[12:20, :], from_even_ref[12:20, :])
    both_ref[8:16, :] = by_high
    for ref in (odd_ref, even_ref):
        for x in range(2):
            for step in range(ITERS):
                ref[16 + x * 4 + step : 17 + x * 4 + step, :] = both_ref[x * 8 + step * 2 : x * 8 + step * 2 + 1, :]
            for k, step in enumerate((0, WIDE_STEP)):
                ref[24 + x * 2 + k : 25 + x * 2 + k, :] = both_ref[x * 8 + step * 2 + 1 : x * 8 + step * 2 + 2, :]
    odd_ref[28:100, :] = ghost_odd_ref[...]
    even_ref[28:100, :] = ghost_even_ref[...]


def wide_middle_kernel(sums_ref, from_odd_ref, from_even_ref, turned_ref, joint_odd_ref, joint_even_ref, out_ref, odd_ref, even_ref):
    add_x(sums_ref, from_odd_ref, from_even_ref, out_ref)
    fill_messages_y(out_ref, odd_ref, even_ref, 2)
    fill_messages_y(turned_ref, odd_ref, even_ref, 1, 16)
    odd_ref[24:42, :] = joint_odd_ref[...]
    even_ref[24:42, :] = joint_even_ref[...]


def cell_means(work_ref, tot_ref, cells=6):
    tot_ref[...] = jnp.zeros_like(tot_ref)
    for cell in range(cells):
        for comp in range(4):
            tot_ref[comp, cell : cell + 1, :] = work_ref[cell * 4 + comp : cell * 4 + comp + 1, :]
    count = jnp.maximum(tot_ref[3], 1.0)
    return [tot_ref[comp] / count for comp in range(3)]


def cell_axes(ids):
    axes = [jnp.zeros(ids.shape, F32) for _ in range(3)]
    for k in range(NAXES):
        match = ids == float(k)
        axes = [jnp.where(match, float(AXES[comp, k]), axes[comp]) for comp in range(3)]
    return axes


def turned(axis, vec):
    along = (axis[0] * vec[0] + axis[1] * vec[1] + axis[2] * vec[2]) * ALONG
    out = []
    for comp in range(3):
        b, c = (comp + 1) % 3, (comp + 2) % 3
        out.append(TURN_COS * vec[comp] + (axis[b] * vec[c] - axis[c] * vec[b]) + along * axis[comp])
    return out


def next_z(value):
    return pltpu.roll(value, 255, 1)


def store_cells(table_ref, parts, cells=6):
    for cell in range(cells):
        for comp, part in enumerate(parts):
            table_ref[0, cell * 8 + comp : cell * 8 + comp + 1, :] = part[cell : cell + 1, :]
    table_ref[1] = next_z(table_ref[0])


def pick(table_ref, comp, col, lanes, masks):
    hop_x, hop_y, hop_z = masks
    by_x = []
    for step_x in range(2):
        by_y = []
        for step_y in range(2):
            row = (step_x * 3 + col + step_y) * 8 + comp
            by_y.append(jnp.where(hop_z, table_ref[1, row : row + 1, lanes], table_ref[0, row : row + 1, lanes]))
        by_x.append(jnp.where(hop_y, by_y[1], by_y[0]))
    return jnp.where(hop_x, by_x[1], by_x[0])


def over_slots(body):
    def run(i, carry):
        body(pl.ds(pl.multiple_of(i * CHUNK, CHUNK), CHUNK))
        return carry

    lax.fori_loop(0, 128 // CHUNK, run, 0, unroll=128 // CHUNK)


def first_kernel(shifts_ref, sums_ref, from_odd_ref, from_even_ref, both_ref, joint_ref, _, ids_ref, far_ids_ref, shift_ref, new_ref, odd_ref, even_ref, next_ref, work_ref, tot_ref, far_ref, turn_ref, left_ref, right_ref):
    by_left, by_right = from_sides("gy", from_odd_ref[...], from_even_ref[...])
    left_ref[...] = by_left
    right_ref[...] = by_right
    ids_ref[...] = jnp.zeros_like(ids_ref)
    for x in range(2):
        for t in range(ITERS):
            row = t * 8 + x * 3
            ids_ref[row : row + 2, :] = both_ref[x * 8 + t * 2 : x * 8 + t * 2 + 2, :]
            ids_ref[row + 2 : row + 3, :] = right_ref[16 + x * 4 + t : 17 + x * 4 + t, :]
    far_ids_ref[...] = jnp.zeros_like(far_ids_ref)
    for k, t in enumerate((0, WIDE_STEP)):
        for x in range(2):
            row, outer = k * 16 + x * 5, slice(24 + x * 2 + k, 25 + x * 2 + k)
            far_ids_ref[row : row + 1, :] = left_ref[outer, :]
            far_ids_ref[row + 1 : row + 4, :] = ids_ref[t * 8 + x * 3 : t * 8 + x * 3 + 3, :]
            far_ids_ref[row + 4 : row + 5, :] = right_ref[outer, :]
    add_y(sums_ref, left_ref, right_ref, work_ref)
    means = cell_means(work_ref, tot_ref, 10)
    axes = cell_axes(far_ids_ref[0:16, :])
    far_ref[...] = jnp.zeros_like(far_ref)
    store_cells(far_ref, shifts_of(means, axes), 10)
    own_cells(far_ref, shift_ref)
    turn_ref[...] = jnp.zeros_like(turn_ref)
    zero = jnp.zeros((16, 256), F32)
    for k in range(3):
        unit = [zero + (1.0 if comp == k else 0.0) for comp in range(3)]
        store_cells(turn_ref.at[k], turned(axes, unit), 10)
    nested = nested_hops(0, shifts_ref)

    def sources_of(cells, first, size):
        tables = [far_ref] + [turn_ref.at[k] for k in range(3)]
        return [(first + at * size, corner_differences(table, cells)) for at, table in enumerate(tables)]

    for col in range(2):
        sources = sources_of(((col + 1, col + 2), (col + 6, col + 7)), col * 27, 54)
        for later in range(8):
            row = (col * 8 + later) * 8
            next_ref[row : row + 8, :] = joint_moment(joint_ref, sources, later, nested, (9, 3, 1))
    cell_sums(stored_moment(next_ref), new_ref)
    for side, came_ref in enumerate((left_ref, right_ref)):
        add_side(new_ref, side, came_ref, sources_of(side_cells(side), 28, 18), nested)
    fill_messages_x(new_ref, 12, odd_ref, even_ref)


def joint_sums(vel_ref, code_ref, shifts_ref, t, out_ref):
    def classes(value, now, later):
        out = []
        for by_x in (value, jnp.where(now[0], value, 0), jnp.where(later[0], value, 0)):
            out += [by_x, jnp.where(now[1], by_x, 0), jnp.where(later[1], by_x, 0)]
        return out

    now_limits, later_limits = hop_limits(shifts_ref, t), hop_limits(shifts_ref, t + 1)

    def body(col, lanes, comp, counts, i, acc):
        rows = pl.ds(pl.multiple_of(i * 8, 8), 8)
        code = code_ref[col, rows, lanes]
        now, later = hop_masks(code, now_limits), hop_masks(code, later_limits)
        out = []
        if comp is not None:
            for value in classes(vel_ref[comp * 2 + col, rows, lanes], now, later):
                out += [value, jnp.where(now[2], value, 0.0), jnp.where(later[2], value, 0.0)]
        if counts:
            word = jnp.where(now[2], 1 + 256, 1) + jnp.where(later[2], 65536, 0)
            out += classes(jnp.where(code >= 0, word, 0), now, later)
        return tuple(a + b for a, b in zip(acc, out))

    zero, none = (jnp.zeros((8, 128), F32),) * 27, (jnp.zeros((8, 128), jnp.int32),) * 9
    for col, lanes in blocks():
        for comp, counts in ((None, True),) if vel_ref is None else ((0, False), (1, False), (2, True)):
            start = (() if comp is None else zero) + (none if counts else ())
            acc = lax.fori_loop(0, 16, functools.partial(body, col, lanes, comp, counts), start, unroll=8)
            if comp is not None:
                for at in range(27):
                    row = 54 + comp * 54 + col * 27 + at
                    out_ref[row : row + 1, lanes] = jnp.sum(acc[at], axis=0, keepdims=True)
            if counts:
                for at, word in enumerate(acc[-9:]):
                    for z in range(3):
                        part = lax.shift_right_logical(word, 8 * z) & 255
                        row = col * 27 + at * 3 + z
                        out_ref[row : row + 1, lanes] = jnp.sum(part.astype(F32), axis=0, keepdims=True)


def boundary_sums(joint_ref, kinds, nested, odd_ref, even_ref):
    odd = is_odd("gy")
    for kind in range(kinds):
        for x in range(3):
            for y in range(2):
                for z in range(3):
                    first = kind * 54 + x * 9 + z
                    hopped = (nested[1] if y else 2) * 3
                    left = joint_ref[first + y * 3 : first + y * 3 + 1, :] - joint_ref[pl.ds(first + hopped, 1), :]
                    right = joint_ref[pl.ds(27 + first + hopped, 1), :]
                    row = kind * 18 + x * 6 + y * 3 + z
                    odd_ref[row : row + 1, :] = jnp.where(odd, right, left)
                    even_ref[row : row + 1, :] = jnp.where(odd, left, right)


def class_kernel(shifts_ref, vel_ref, code_ref, out_ref, odd_ref, even_ref):
    joint_sums(vel_ref, code_ref, shifts_ref, 0, out_ref)
    boundary_sums(out_ref, 4, nested_hops(0, shifts_ref), odd_ref, even_ref)


def joint_kernel(shifts_ref, code_ref, first_ref, second_ref, odd_ref, even_ref):
    joint_sums(None, code_ref, shifts_ref, 1, first_ref)
    joint_sums(None, code_ref, shifts_ref, 2, second_ref)
    boundary_sums(second_ref, 1, nested_hops(WIDE_STEP, shifts_ref), odd_ref, even_ref)


def turn_kernel(step, *refs):
    shifts_ref, code_ref, ids_ref, vel_ref, last_ref, *refs = refs
    if step == 1:
        *refs, before_ref = refs
        before_ref[...] = jnp.zeros_like(before_ref)
        store_cells(before_ref, cell_axes(ids_ref[0:8, :]))
    if step == WIDE_STEP:
        far_ids_ref, out_ref, axes_ref, sums_ref, table_ref, mom_ref = refs
        for comp, axis in enumerate(cell_axes(far_ids_ref[16:32, :])):
            axes_ref[comp] = axis
    elif step < ITERS - 1:
        out_ref, axes_ref, mom_ref, table_ref = refs
    else:
        out_ref, axes_ref, table_ref = refs
    axes = cell_axes(ids_ref[step * 8 : step * 8 + 8, :])
    if step != WIDE_STEP:
        for comp in range(3):
            axes_ref[comp] = axes[comp]
    table_ref[...] = jnp.zeros_like(table_ref)
    store_cells(table_ref, axes)
    for col, lanes in blocks():

        def body(rows):
            code = code_ref[col, rows, lanes]
            vel = [vel_ref[comp * 2 + col, rows, lanes] for comp in range(3)]
            masks = hop_masks(code, hop_limits(shifts_ref, step - 1))
            if step == 1:
                vel = turned([pick(before_ref, comp, col, lanes, masks) for comp in range(3)], vel)
            filled = code >= 0
            vel = [jnp.where(filled, vel[comp] + pick(last_ref, comp, col, lanes, masks), 0.0) for comp in range(3)]
            masks = hop_masks(code, hop_limits(shifts_ref, step))
            turn = turned([pick(table_ref, comp, col, lanes, masks) for comp in range(3)], vel)
            for comp in range(3):
                out_ref[comp * 2 + col, rows, lanes] = turn[comp]

        over_slots(body)
    if step < ITERS - 1:
        mom_ref[...] = jnp.zeros_like(mom_ref)
        deposit(out_ref, code_ref, shifts_ref, step + 1, mom_ref, False)
    if step == WIDE_STEP:
        cell_sums(stored_moment(mom_ref), sums_ref)


def nested_hops(step, shifts_ref):
    return [jnp.where(shifts_ref[step, dim] <= shifts_ref[step + 1, dim], 1, 2) for dim in range(3)]


def corner_differences(shift_ref, cells):
    parts = {}
    for corner in range(8):
        cell = cells[corner >> 2][corner >> 1 & 1]
        parts[corner] = shift_ref[corner & 1, cell * 8 : cell * 8 + 8, :]
    for bit in (1, 2, 4):
        for corner in range(8):
            if corner & bit:
                parts[corner] = parts[corner] - parts[corner ^ bit]
    return parts


def joint_moment(joint_ref, sources, later, nested, weights):
    total = None
    for now in range(8):
        at = 0
        for dim, (bit, weight) in enumerate(zip((4, 2, 1), weights)):
            if now & bit and later & bit:
                at = at + nested[dim] * weight
            elif now & bit:
                at = at + weight
            elif later & bit:
                at = at + 2 * weight
        for first, parts in sources:
            term = joint_ref[pl.ds(first + at, 1), :] * parts[now]
            total = term if total is None else total + term
    return total


def shifts_of(means, axes):
    turn = turned(axes, means)
    return [means[comp] - turn[comp] for comp in range(3)] + [jnp.ones_like(means[0])]


def own_cells(far_ref, out_ref):
    for hop in range(2):
        for side in range(2):
            out_ref[side, hop * 24 : hop * 24 + 24, :] = far_ref[side, hop * 40 + 8 : hop * 40 + 32, :]


def side_cells(side):
    first = side * 3
    return ((first, first + 1), (first + 5, first + 6))


def add_side(new_ref, side, came_ref, sources, nested):
    def moment_of(later):
        return joint_moment(came_ref, sources, later, nested, (6, 3, 1))

    quads = []
    for moment in (0, 4):
        up = moment_of(moment + 1)
        quads.append(moment_of(moment) - up + pltpu.roll(up, 1, 1))
    for hop, piece in enumerate((quads[0] - quads[1], quads[1])):
        rows = slice(hop * 12 + side * 8, hop * 12 + side * 8 + 4)
        new_ref[rows, :] = new_ref[rows, :] + piece[0:4, :]


def shift_kernel(step, shifts_ref, sums_ref, from_odd_ref, from_even_ref, axes_ref, mom_ref, joint_ref, shift_ref, new_ref, odd_ref, even_ref, work_ref, tot_ref, next_ref):
    add_x(sums_ref, from_odd_ref, from_even_ref, work_ref)
    means = cell_means(work_ref, tot_ref)
    shift_ref[...] = jnp.zeros_like(shift_ref)
    store_cells(shift_ref, shifts_of(means, [axes_ref[comp] for comp in range(3)]))
    nested = nested_hops(step, shifts_ref)
    for col in range(2):
        parts = corner_differences(shift_ref, ((col, col + 1), (3 + col, 4 + col)))
        for later in range(8):
            row = (col * 8 + later) * 8
            next_ref[row : row + 8, :] = mom_ref[row : row + 8, :] + joint_moment(joint_ref, [(col * 27, parts)], later, nested, (9, 3, 1))
    cell_sums(stored_moment(next_ref), new_ref)
    fill_messages_x(new_ref, 12, odd_ref, even_ref)


def wide_shift_kernel(step, shifts_ref, sums_ref, from_odd_ref, from_even_ref, axes_ref, turned_ref, joint_ref, shift_ref, new_ref, odd_ref, even_ref, work_ref, tot_ref, next_ref, far_ref, left_ref, right_ref):
    by_left, by_right = from_sides("gy", from_odd_ref[...], from_even_ref[...])
    left_ref[...] = by_left
    right_ref[...] = by_right
    add_y(sums_ref, left_ref, right_ref, work_ref)
    means = cell_means(work_ref, tot_ref, 10)
    far_ref[...] = jnp.zeros_like(far_ref)
    store_cells(far_ref, shifts_of(means, [axes_ref[comp] for comp in range(3)]), 10)
    own_cells(far_ref, shift_ref)
    nested = nested_hops(step, shifts_ref)
    for col in range(2):
        parts = corner_differences(far_ref, ((col + 1, col + 2), (col + 6, col + 7)))
        for later in range(8):
            row = (col * 8 + later) * 8
            next_ref[row : row + 8, :] = joint_moment(joint_ref, [(col * 27, parts)], later, nested, (9, 3, 1))
    cell_sums(stored_moment(next_ref), new_ref)
    new_ref[...] = new_ref[...] + turned_ref[...]
    for side, came_ref in enumerate((left_ref, right_ref)):
        for hop in range(2):
            rows = slice(hop * 12 + side * 8, hop * 12 + side * 8 + 4)
            new_ref[rows, :] = new_ref[rows, :] + came_ref[16 + hop * 4 : 20 + hop * 4, :]
        add_side(new_ref, side, came_ref, [(24, corner_differences(far_ref, side_cells(side)))], nested)
    fill_messages_x(new_ref, 12, odd_ref, even_ref)


def last_kernel(shifts_ref, code_ref, vel_ref, sums_ref, from_odd_ref, from_even_ref, axes_ref, out_hbm, means_hbm, work_ref, tot_ref, table_ref, end_ref, out_ref, means_ref, sems):
    add_x(sums_ref, from_odd_ref, from_even_ref, work_ref)
    means = cell_means(work_ref, tot_ref)
    turn = turned([axes_ref[comp] for comp in range(3)], means)
    table_ref[...] = jnp.zeros_like(table_ref)
    store_cells(table_ref, [means[comp] - turn[comp] for comp in range(3)])
    for comp in range(3):
        means_ref[comp] = means[comp][0:2, :]
    saves = [pltpu.make_async_copy(means_ref, means_hbm, sems.at[6])]
    saves[0].start()
    limits = hop_limits(shifts_ref, ITERS - 1)
    for col in range(2):
        for _, lanes in blocks((col,)):

            def body(rows):
                code = code_ref[col, rows, lanes]
                masks = hop_masks(code, limits)
                filled = code >= 0
                for comp in range(3):
                    value = vel_ref[comp * 2 + col, rows, lanes] + pick(table_ref, comp, col, lanes, masks)
                    end_ref[comp * 2 + col, rows, lanes] = jnp.where(filled, value, 0.0)

            over_slots(body)
        for comp in range(3):
            at = comp * 2 + col
            out_ref[at] = end_ref[at].T.astype(jnp.bfloat16)
            saves.append(pltpu.make_async_copy(out_ref.at[at], out_hbm.at[at], sems.at[at]))
            saves[-1].start()
    for save in saves:
        save.wait()


VMEM = pl.BlockSpec(memory_space=pltpu.VMEM)
HBM = pl.BlockSpec(memory_space=pltpu.HBM)
BYTES = 8_000_000


def call(kernel, name, in_specs, shapes, scratch, cost=0, out_specs=None):
    return pl.pallas_call(
        kernel,
        out_shape=[jax.ShapeDtypeStruct(s, d) for s, d in shapes],
        in_specs=in_specs,
        out_specs=out_specs or [VMEM] * len(shapes),
        scratch_shapes=scratch,
        compiler_params=pltpu.CompilerParams(vmem_limit_bytes=16 * 1024 * 1024),
        cost_estimate=pl.CostEstimate(flops=0, bytes_accessed=cost, transcendentals=0) if cost else None,
        name=name,
    )


def swap(odd, even, axis):
    count = lax.axis_size(axis)
    evens = [(s, s ^ 1) for s in range(count)]
    odds = [(s, (((s - 1) % count ^ 1) + 1) % count) for s in range(count)]
    from_even = lax.ppermute(even, axis, evens)
    from_odd = lax.ppermute(odd, axis, odds)
    return from_odd, from_even


def on_device(velocity, position_code, occupancy, shifts, axis_ids):
    vel_in = velocity.reshape(6, 256, 128)
    code_in = position_code.reshape(2, 256, 128)
    occ = occupancy.reshape(2, 256)
    ids_in = axis_ids.reshape(ITERS, 2, 256)

    def rows(count):
        return ((count, 256), F32)

    def room(*shape):
        return pltpu.VMEM(shape, F32)

    vel_shape, code_shape = ((6, 128, 256), F32), ((2, 128, 256), jnp.int32)
    table_shape, axes_shape = ((2, WIDE, 256), F32), ((3, 8, 256), F32)
    moments, table = room(128, 256), room(2, WIDE, 256)
    small = [room(24, 256), room(4, 8, 256)]
    wide_small, far = [room(40, 256), room(4, 16, 256)], room(2, 80, 256)

    vel, code, sums, odd, even = call(
        start_kernel, "start", [HBM] * 5, [vel_shape, code_shape, rows(24), rows(20), rows(20)],
        [moments, pltpu.VMEM((6, 256, 128), jnp.bfloat16), pltpu.VMEM((2, 256, 128), jnp.int32), pltpu.VMEM((2, 256), jnp.int32), pltpu.VMEM((ITERS, 2, 256), jnp.int32), pltpu.SMEM((ITERS, 3), jnp.int32), pltpu.SemaphoreType.DMA((11,))],
    )(*(pltpu.with_memory_space_constraint(x, pltpu.HBM) for x in (shifts, vel_in, code_in, occ, ids_in)))

    from_odd, from_even = swap(odd, even, "gx")
    classes, class_odd, class_even = call(
        class_kernel, "classes", [VMEM] * 3, [rows(216), rows(72), rows(72)], [], BYTES
    )(shifts, vel, code)
    sums, both, odd, even = call(
        first_middle_kernel, "middle0", [VMEM] * 6, [rows(24), rows(16), rows(100), rows(100)], [],
    )(sums, from_odd, from_even, ids_in, class_odd, class_even)
    from_odd, from_even = swap(odd, even, "gy")
    *joints, joint_odd, joint_even = call(
        joint_kernel, "joint", [VMEM] * 2, [rows(54), rows(54), rows(18), rows(18)], [], BYTES
    )(shifts, code)
    ids, far_ids, shift, sums, odd, even = call(
        first_kernel, "first", [VMEM] * 7, [rows(32), rows(32), table_shape, rows(24), rows(12), rows(12)],
        [moments, *wide_small, far, room(3, 2, 80, 256), room(100, 256), room(100, 256)],
    )(shifts, sums, from_odd, from_even, both, classes, joints[0])

    for step in range(1, ITERS):
        last, wide = step == ITERS - 1, step == WIDE_STEP
        from_odd, from_even = swap(odd, even, "gx")
        args = [shifts, code, ids, vel, shift]
        shapes, scratch = [vel_shape, axes_shape], [table] * (2 if step == 1 else 1)
        if wide:
            args.append(far_ids)
            shapes = [vel_shape, ((3, 16, 256), F32), rows(24)]
            scratch = [table, moments]
        elif not last:
            shapes.append(rows(128))
        vel, axes, *more = call(
            functools.partial(turn_kernel, step), f"turn{step}", [VMEM] * len(args), shapes, scratch, BYTES,
        )(*args)
        if last:
            out, out_means = call(
                last_kernel, "last", [VMEM] * 7, [((6, 256, 128), jnp.bfloat16), ((3, 2, 256), F32)],
                [*small, table, room(6, 128, 256), pltpu.VMEM((6, 256, 128), jnp.bfloat16), room(3, 2, 256), pltpu.SemaphoreType.DMA((7,))],
                out_specs=[HBM, HBM],
            )(shifts, code, vel, sums, from_odd, from_even, axes)
        elif wide:
            sums, odd, even = call(
                wide_middle_kernel, f"middle{step}", [VMEM] * 6, [rows(24), rows(42), rows(42)], [],
            )(sums, from_odd, from_even, more[0], joint_odd, joint_even)
            from_odd, from_even = swap(odd, even, "gy")
            shift, sums, odd, even = call(
                functools.partial(wide_shift_kernel, step), f"shift{step}", [VMEM] * 7,
                [table_shape, rows(24), rows(12), rows(12)], [*wide_small, moments, far, room(42, 256), room(42, 256)],
            )(shifts, sums, from_odd, from_even, axes, more[0], joints[step - 1])
        else:
            shift, sums, odd, even = call(
                functools.partial(shift_kernel, step), f"shift{step}", [VMEM] * 7,
                [table_shape, rows(24), rows(12), rows(12)], [*small, moments],
            )(shifts, sums, from_odd, from_even, axes, more[0], joints[step - 1])
    return out.reshape(velocity.shape), out_means.reshape(3, *occupancy.shape)


def solution(mesh):
    in_specs = (
        P(None, "gx", "gy", None, None),
        P("gx", "gy", None, None),
        P("gx", "gy", None),
        P(),
        P(None, "gx", "gy", None),
    )
    out_specs = (P(None, "gx", "gy", None, None), P(None, "gx", "gy", None))
    return jax.shard_map(
        on_device, mesh=mesh, in_specs=in_specs, out_specs=out_specs, check_vma=False
    )
```

```python
import functools
import math

import jax
import jax.numpy as jnp
import numpy as np
from jax import lax
from jax.experimental import pallas as pl
from jax.experimental.pallas import tpu as pltpu
from jax.sharding import PartitionSpec as P

SUBDIV = 8
NAXES = 32
ITERS = 4
GOLDEN = 2.399963229728653
TURN_COS = math.cos(130.0 * math.pi / 180.0)
TURN_SIN = math.sin(130.0 * math.pi / 180.0)
ALONG = (1.0 - TURN_COS) / (TURN_SIN * TURN_SIN)

F32 = jnp.float32
CHUNK = 32
WIDE = 48
WIDE_STEP = 2


def axis_table():
    ordinal = np.arange(NAXES, dtype=np.float64)
    height = 1.0 - (2.0 * ordinal + 1.0) / NAXES
    radius = np.sqrt(1.0 - height * height)
    phases = ordinal * GOLDEN
    return TURN_SIN * np.stack([radius * np.cos(phases), radius * np.sin(phases), height])


AXES = axis_table()


def is_odd(axis):
    return lax.rem(lax.axis_index(axis), 2) == 1


def hop_limits(shifts_ref, step):
    return [(SUBDIV - shifts_ref[step, dim]) * SUBDIV ** (2 - dim) for dim in range(3)]


def hop_masks(code, limits):
    hop_x = code >= limits[0]
    hop_y = (code & (SUBDIV * SUBDIV - 1)) >= limits[1]
    hop_z = (code & (SUBDIV - 1)) >= limits[2]
    return hop_x, hop_y, hop_z


def slot_sums(values, count, col, lanes, code_ref, shifts_ref, step, mom_ref):
    def body(i, acc):
        rows = pl.ds(pl.multiple_of(i * 8, 8), 8)
        code = code_ref[col, rows, lanes]
        hop_x, hop_y, hop_z = hop_masks(code, hop_limits(shifts_ref, step))
        out = list(acc)
        for comp, value in enumerate(values(rows, code)):
            with_x = jnp.where(hop_x, value, 0.0)
            with_y = jnp.where(hop_y, value, 0.0)
            with_xy = jnp.where(hop_y, with_x, 0.0)
            for pair, base in ((0, value), (2, with_y), (4, with_x), (6, with_xy)):
                at = comp * 8 + pair
                out[at] = out[at] + base
                out[at + 1] = out[at + 1] + jnp.where(hop_z, base, 0.0)
        return tuple(out)

    zero = jnp.zeros((8, 128), F32)
    acc = lax.fori_loop(0, 16, body, (zero,) * (8 * count), unroll=16)
    for comp in range(count):
        for moment in range(8):
            row = (col * 8 + moment) * 8 + comp
            mom_ref[row : row + 1, lanes] = jnp.sum(acc[comp * 8 + moment], axis=0, keepdims=True)


def blocks(cols=(0, 1)):
    for col in cols:
        for half in range(2):
            yield col, slice(half * 128, half * 128 + 128)


def deposit(vel_ref, code_ref, shifts_ref, step, mom_ref, counted, cols=(0, 1)):
    for col, lanes in blocks(cols):

        def values(rows, code):
            parts = [vel_ref[comp * 2 + col, rows, lanes] for comp in range(3)]
            return parts + ([jnp.where(code >= 0, 1.0, 0.0)] if counted else [])

        slot_sums(values, 4 if counted else 3, col, lanes, code_ref, shifts_ref, step, mom_ref)


def cell_sums(moment_of, sums_ref):
    pieces = {}
    for col in range(2):
        quads = {}
        for moment in (0, 2, 4, 6):
            up = moment_of(col, moment + 1)
            quads[moment] = moment_of(col, moment) - up + pltpu.roll(up, 1, 1)
        pieces[col, 1, 1] = quads[6]
        pieces[col, 1, 0] = quads[4] - quads[6]
        pieces[col, 0, 1] = quads[2] - quads[6]
        pieces[col, 0, 0] = quads[0] - quads[2] - quads[4] + quads[6]
    for hop in range(2):
        columns = (pieces[0, hop, 0], pieces[0, hop, 1] + pieces[1, hop, 0], pieces[1, hop, 1])
        for at, piece in enumerate(columns):
            row = (hop * 3 + at) * 4
            sums_ref[row : row + 4, :] = piece[0:4, :]


def stored_moment(mom_ref):
    def moment_of(col, moment):
        row = (col * 8 + moment) * 8
        return mom_ref[row : row + 8, :]

    return moment_of


def fill_messages_y(sums_ref, odd_ref, even_ref, columns=1, first=0):
    odd = is_odd("gy")
    size = columns * 4
    for hop in range(2):
        left = sums_ref[hop * 12 : hop * 12 + size, :]
        right = sums_ref[hop * 12 + 12 - size : hop * 12 + 12, :]
        rows = slice(first + hop * size, first + hop * size + size)
        odd_ref[rows, :] = jnp.where(odd, right, left)
        even_ref[rows, :] = jnp.where(odd, left, right)


def fill_messages_x(out_ref, size, odd_ref, even_ref):
    odd = is_odd("gx")
    low, high = out_ref[0:size, :], out_ref[size : 2 * size, :]
    odd_ref[0:size, :] = jnp.where(odd, high, low)
    even_ref[0:size, :] = jnp.where(odd, low, high)


def from_sides(axis, from_odd, from_even):
    odd = is_odd(axis)
    return jnp.where(odd, from_even, from_odd), jnp.where(odd, from_odd, from_even)


def start_kernel(shifts_hbm, vel_hbm, code_hbm, occ_hbm, ids_hbm, vel_ref, code_ref, sums_ref, odd_ref, even_ref, mom_ref, vel_in_ref, code_in_ref, occ_ref, ids_ref, shifts_ref, sems):
    fetch_shifts = pltpu.make_async_copy(shifts_hbm, shifts_ref, sems.at[10])
    fetch_occ = pltpu.make_async_copy(occ_hbm, occ_ref, sems.at[8])
    fetch_ids = pltpu.make_async_copy(ids_hbm, ids_ref, sems.at[9])
    fetch_shifts.start()
    fetch_occ.start()
    copies = []
    for col in range(2):
        copies.append(pltpu.make_async_copy(code_hbm.at[col], code_in_ref.at[col], sems.at[col]))
        copies.append(pltpu.make_async_copy(vel_hbm.at[:, col], vel_in_ref.at[:, col], sems.at[2 + col]))
    for copy in copies:
        copy.start()
    fetch_ids.start()
    mom_ref[...] = jnp.zeros_like(mom_ref)
    slot = lax.broadcasted_iota(jnp.int32, (128, 256), 0)
    fetch_occ.wait()
    fetch_shifts.wait()
    for col in range(2):
        filled = slot < occ_ref[col : col + 1, :]
        copies[2 * col].wait()
        code_ref[col] = jnp.where(filled, code_in_ref[col].T, -1)
        copies[2 * col + 1].wait()
        for comp in range(3):
            vel_ref[comp * 2 + col] = jnp.where(filled, vel_in_ref[comp, col].astype(F32).T, 0.0)
        deposit(vel_ref, code_ref, shifts_ref, 0, mom_ref, True, (col,))
    fetch_ids.wait()
    for step in range(ITERS):
        ids = ids_ref[step].astype(F32)
        rows = slice(12 + step * 2, 14 + step * 2)
        odd_ref[rows, :] = ids
        even_ref[rows, :] = ids
    cell_sums(stored_moment(mom_ref), sums_ref)
    fill_messages_x(sums_ref, 12, odd_ref, even_ref)


def add_x(sums_ref, from_odd_ref, from_even_ref, out_ref):
    by_low, by_high = from_sides("gx", from_odd_ref[0:12, :], from_even_ref[0:12, :])
    out_ref[0:12, :] = sums_ref[0:12, :] + by_low
    out_ref[12:24, :] = sums_ref[12:24, :] + by_high


def add_y(sums_ref, by_left_ref, by_right_ref, out_ref):
    for hop in range(2):
        at, own, rows = hop * 20, hop * 12, slice(hop * 8, hop * 8 + 8)
        out_ref[at : at + 8, :] = by_left_ref[rows, :]
        out_ref[at + 12 : at + 20, :] = by_right_ref[rows, :]
        out_ref[at + 8 : at + 12, :] = sums_ref[own + 4 : own + 8, :]
        out_ref[at + 4 : at + 8, :] = out_ref[at + 4 : at + 8, :] + sums_ref[own : own + 4, :]
        out_ref[at + 12 : at + 16, :] = out_ref[at + 12 : at + 16, :] + sums_ref[own + 8 : own + 12, :]


def first_middle_kernel(sums_ref, from_odd_ref, from_even_ref, ids_ref, ghost_odd_ref, ghost_even_ref, out_ref, both_ref, odd_ref, even_ref):
    add_x(sums_ref, from_odd_ref, from_even_ref, out_ref)
    fill_messages_y(out_ref, odd_ref, even_ref, 2)
    for step in range(ITERS):
        both_ref[step * 2 : step * 2 + 2, :] = ids_ref[step].astype(F32)
    _, by_high = from_sides("gx", from_odd_ref[12:20, :], from_even_ref[12:20, :])
    both_ref[8:16, :] = by_high
    for ref in (odd_ref, even_ref):
        for x in range(2):
            for step in range(ITERS):
                ref[16 + x * 4 + step : 17 + x * 4 + step, :] = both_ref[x * 8 + step * 2 : x * 8 + step * 2 + 1, :]
            for k, step in enumerate((0, WIDE_STEP)):
                ref[24 + x * 2 + k : 25 + x * 2 + k, :] = both_ref[x * 8 + step * 2 + 1 : x * 8 + step * 2 + 2, :]
    odd_ref[28:100, :] = ghost_odd_ref[...]
    even_ref[28:100, :] = ghost_even_ref[...]


def wide_middle_kernel(sums_ref, from_odd_ref, from_even_ref, turned_ref, joint_odd_ref, joint_even_ref, out_ref, odd_ref, even_ref):
    add_x(sums_ref, from_odd_ref, from_even_ref, out_ref)
    fill_messages_y(out_ref, odd_ref, even_ref, 2)
    fill_messages_y(turned_ref, odd_ref, even_ref, 1, 16)
    odd_ref[24:42, :] = joint_odd_ref[...]
    even_ref[24:42, :] = joint_even_ref[...]


def cell_means(work_ref, tot_ref, cells=6):
    tot_ref[...] = jnp.zeros_like(tot_ref)
    for cell in range(cells):
        for comp in range(4):
            tot_ref[comp, cell : cell + 1, :] = work_ref[cell * 4 + comp : cell * 4 + comp + 1, :]
    count = jnp.maximum(tot_ref[3], 1.0)
    return [tot_ref[comp] / count for comp in range(3)]


def cell_axes(ids):
    axes = [jnp.zeros(ids.shape, F32) for _ in range(3)]
    for k in range(NAXES):
        match = ids == float(k)
        axes = [jnp.where(match, float(AXES[comp, k]), axes[comp]) for comp in range(3)]
    return axes


def turned(axis, vec):
    along = (axis[0] * vec[0] + axis[1] * vec[1] + axis[2] * vec[2]) * ALONG
    out = []
    for comp in range(3):
        b, c = (comp + 1) % 3, (comp + 2) % 3
        out.append(TURN_COS * vec[comp] + (axis[b] * vec[c] - axis[c] * vec[b]) + along * axis[comp])
    return out


def next_z(value):
    return pltpu.roll(value, 255, 1)


def store_cells(table_ref, parts, cells=6):
    for cell in range(cells):
        for comp, part in enumerate(parts):
            table_ref[0, cell * 8 + comp : cell * 8 + comp + 1, :] = part[cell : cell + 1, :]
    table_ref[1] = next_z(table_ref[0])


def pick(table_ref, comp, col, lanes, masks):
    hop_x, hop_y, hop_z = masks
    by_x = []
    for step_x in range(2):
        by_y = []
        for step_y in range(2):
            row = (step_x * 3 + col + step_y) * 8 + comp
            by_y.append(jnp.where(hop_z, table_ref[1, row : row + 1, lanes], table_ref[0, row : row + 1, lanes]))
        by_x.append(jnp.where(hop_y, by_y[1], by_y[0]))
    return jnp.where(hop_x, by_x[1], by_x[0])


def over_slots(body):
    def run(i, carry):
        body(pl.ds(pl.multiple_of(i * CHUNK, CHUNK), CHUNK))
        return carry

    lax.fori_loop(0, 128 // CHUNK, run, 0, unroll=128 // CHUNK)


def first_kernel(shifts_ref, sums_ref, from_odd_ref, from_even_ref, both_ref, joint_ref, _, ids_ref, far_ids_ref, shift_ref, new_ref, odd_ref, even_ref, next_ref, work_ref, tot_ref, far_ref, turn_ref, left_ref, right_ref):
    by_left, by_right = from_sides("gy", from_odd_ref[...], from_even_ref[...])
    left_ref[...] = by_left
    right_ref[...] = by_right
    ids_ref[...] = jnp.zeros_like(ids_ref)
    for x in range(2):
        for t in range(ITERS):
            row = t * 8 + x * 3
            ids_ref[row : row + 2, :] = both_ref[x * 8 + t * 2 : x * 8 + t * 2 + 2, :]
            ids_ref[row + 2 : row + 3, :] = right_ref[16 + x * 4 + t : 17 + x * 4 + t, :]
    far_ids_ref[...] = jnp.zeros_like(far_ids_ref)
    for k, t in enumerate((0, WIDE_STEP)):
        for x in range(2):
            row, outer = k * 16 + x * 5, slice(24 + x * 2 + k, 25 + x * 2 + k)
            far_ids_ref[row : row + 1, :] = left_ref[outer, :]
            far_ids_ref[row + 1 : row + 4, :] = ids_ref[t * 8 + x * 3 : t * 8 + x * 3 + 3, :]
            far_ids_ref[row + 4 : row + 5, :] = right_ref[outer, :]
    add_y(sums_ref, left_ref, right_ref, work_ref)
    means = cell_means(work_ref, tot_ref, 10)
    axes = cell_axes(far_ids_ref[0:16, :])
    far_ref[...] = jnp.zeros_like(far_ref)
    store_cells(far_ref, shifts_of(means, axes), 10)
    own_cells(far_ref, shift_ref)
    turn_ref[...] = jnp.zeros_like(turn_ref)
    zero = jnp.zeros((16, 256), F32)
    for k in range(3):
        unit = [zero + (1.0 if comp == k else 0.0) for comp in range(3)]
        store_cells(turn_ref.at[k], turned(axes, unit), 10)
    nested = nested_hops(0, shifts_ref)

    def sources_of(cells, first, size):
        tables = [far_ref] + [turn_ref.at[k] for k in range(3)]
        return [(first + at * size, corner_differences(table, cells)) for at, table in enumerate(tables)]

    for col in range(2):
        sources = sources_of(((col + 1, col + 2), (col + 6, col + 7)), col * 27, 54)
        for later in range(8):
            row = (col * 8 + later) * 8
            next_ref[row : row + 8, :] = joint_moment(joint_ref, sources, later, nested, (9, 3, 1))
    cell_sums(stored_moment(next_ref), new_ref)
    for side, came_ref in enumerate((left_ref, right_ref)):
        add_side(new_ref, side, came_ref, sources_of(side_cells(side), 28, 18), nested)
    fill_messages_x(new_ref, 12, odd_ref, even_ref)


def joint_sums(vel_ref, code_ref, shifts_ref, t, out_ref):
    def classes(value, now, later):
        out = []
        for by_x in (value, jnp.where(now[0], value, 0), jnp.where(later[0], value, 0)):
            out += [by_x, jnp.where(now[1], by_x, 0), jnp.where(later[1], by_x, 0)]
        return out

    now_limits, later_limits = hop_limits(shifts_ref, t), hop_limits(shifts_ref, t + 1)

    def body(col, lanes, comp, counts, i, acc):
        rows = pl.ds(pl.multiple_of(i * 8, 8), 8)
        code = code_ref[col, rows, lanes]
        now, later = hop_masks(code, now_limits), hop_masks(code, later_limits)
        out = []
        if comp is not None:
            for value in classes(vel_ref[comp * 2 + col, rows, lanes], now, later):
                out += [value, jnp.where(now[2], value, 0.0), jnp.where(later[2], value, 0.0)]
        if counts:
            word = jnp.where(now[2], 1 + 256, 1) + jnp.where(later[2], 65536, 0)
            out += classes(jnp.where(code >= 0, word, 0), now, later)
        return tuple(a + b for a, b in zip(acc, out))

    zero, none = (jnp.zeros((8, 128), F32),) * 27, (jnp.zeros((8, 128), jnp.int32),) * 9
    for col, lanes in blocks():
        for comp, counts in ((None, True),) if vel_ref is None else ((0, False), (1, False), (2, True)):
            start = (() if comp is None else zero) + (none if counts else ())
            acc = lax.fori_loop(0, 16, functools.partial(body, col, lanes, comp, counts), start, unroll=8)
            if comp is not None:
                for at in range(27):
                    row = 54 + comp * 54 + col * 27 + at
                    out_ref[row : row + 1, lanes] = jnp.sum(acc[at], axis=0, keepdims=True)
            if counts:
                for at, word in enumerate(acc[-9:]):
                    for z in range(3):
                        part = lax.shift_right_logical(word, 8 * z) & 255
                        row = col * 27 + at * 3 + z
                        out_ref[row : row + 1, lanes] = jnp.sum(part.astype(F32), axis=0, keepdims=True)


def boundary_sums(joint_ref, kinds, nested, odd_ref, even_ref):
    odd = is_odd("gy")
    for kind in range(kinds):
        for x in range(3):
            for y in range(2):
                for z in range(3):
                    first = kind * 54 + x * 9 + z
                    hopped = (nested[1] if y else 2) * 3
                    left = joint_ref[first + y * 3 : first + y * 3 + 1, :] - joint_ref[pl.ds(first + hopped, 1), :]
                    right = joint_ref[pl.ds(27 + first + hopped, 1), :]
                    row = kind * 18 + x * 6 + y * 3 + z
                    odd_ref[row : row + 1, :] = jnp.where(odd, right, left)
                    even_ref[row : row + 1, :] = jnp.where(odd, left, right)


def class_kernel(shifts_ref, vel_ref, code_ref, out_ref, odd_ref, even_ref):
    joint_sums(vel_ref, code_ref, shifts_ref, 0, out_ref)
    boundary_sums(out_ref, 4, nested_hops(0, shifts_ref), odd_ref, even_ref)


def joint_kernel(shifts_ref, code_ref, first_ref, second_ref, odd_ref, even_ref):
    joint_sums(None, code_ref, shifts_ref, 1, first_ref)
    joint_sums(None, code_ref, shifts_ref, 2, second_ref)
    boundary_sums(second_ref, 1, nested_hops(WIDE_STEP, shifts_ref), odd_ref, even_ref)


def turn_kernel(step, *refs):
    shifts_ref, code_ref, ids_ref, vel_ref, last_ref, *refs = refs
    if step == 1:
        *refs, before_ref = refs
        before_ref[...] = jnp.zeros_like(before_ref)
        store_cells(before_ref, cell_axes(ids_ref[0:8, :]))
    if step == WIDE_STEP:
        far_ids_ref, out_ref, axes_ref, sums_ref, table_ref, mom_ref = refs
        for comp, axis in enumerate(cell_axes(far_ids_ref[16:32, :])):
            axes_ref[comp] = axis
    elif step < ITERS - 1:
        out_ref, axes_ref, mom_ref, table_ref = refs
    else:
        out_ref, axes_ref, table_ref = refs
    axes = cell_axes(ids_ref[step * 8 : step * 8 + 8, :])
    if step != WIDE_STEP:
        for comp in range(3):
            axes_ref[comp] = axes[comp]
    table_ref[...] = jnp.zeros_like(table_ref)
    store_cells(table_ref, axes)
    for col, lanes in blocks():

        def body(rows):
            code = code_ref[col, rows, lanes]
            vel = [vel_ref[comp * 2 + col, rows, lanes] for comp in range(3)]
            masks = hop_masks(code, hop_limits(shifts_ref, step - 1))
            if step == 1:
                vel = turned([pick(before_ref, comp, col, lanes, masks) for comp in range(3)], vel)
            filled = code >= 0
            vel = [jnp.where(filled, vel[comp] + pick(last_ref, comp, col, lanes, masks), 0.0) for comp in range(3)]
            masks = hop_masks(code, hop_limits(shifts_ref, step))
            turn = turned([pick(table_ref, comp, col, lanes, masks) for comp in range(3)], vel)
            for comp in range(3):
                out_ref[comp * 2 + col, rows, lanes] = turn[comp]

        over_slots(body)
    if step < ITERS - 1:
        mom_ref[...] = jnp.zeros_like(mom_ref)
        deposit(out_ref, code_ref, shifts_ref, step + 1, mom_ref, False)
    if step == WIDE_STEP:
        cell_sums(stored_moment(mom_ref), sums_ref)


def nested_hops(step, shifts_ref):
    return [jnp.where(shifts_ref[step, dim] <= shifts_ref[step + 1, dim], 1, 2) for dim in range(3)]


def corner_differences(shift_ref, cells):
    parts = {}
    for corner in range(8):
        cell = cells[corner >> 2][corner >> 1 & 1]
        parts[corner] = shift_ref[corner & 1, cell * 8 : cell * 8 + 8, :]
    for bit in (1, 2, 4):
        for corner in range(8):
            if corner & bit:
                parts[corner] = parts[corner] - parts[corner ^ bit]
    return parts


def joint_moment(joint_ref, sources, later, nested, weights):
    total = None
    for now in range(8):
        at = 0
        for dim, (bit, weight) in enumerate(zip((4, 2, 1), weights)):
            if now & bit and later & bit:
                at = at + nested[dim] * weight
            elif now & bit:
                at = at + weight
            elif later & bit:
                at = at + 2 * weight
        for first, parts in sources:
            term = joint_ref[pl.ds(first + at, 1), :] * parts[now]
            total = term if total is None else total + term
    return total


def shifts_of(means, axes):
    turn = turned(axes, means)
    return [means[comp] - turn[comp] for comp in range(3)] + [jnp.ones_like(means[0])]


def own_cells(far_ref, out_ref):
    for hop in range(2):
        for side in range(2):
            out_ref[side, hop * 24 : hop * 24 + 24, :] = far_ref[side, hop * 40 + 8 : hop * 40 + 32, :]


def side_cells(side):
    first = side * 3
    return ((first, first + 1), (first + 5, first + 6))


def add_side(new_ref, side, came_ref, sources, nested):
    def moment_of(later):
        return joint_moment(came_ref, sources, later, nested, (6, 3, 1))

    quads = []
    for moment in (0, 4):
        up = moment_of(moment + 1)
        quads.append(moment_of(moment) - up + pltpu.roll(up, 1, 1))
    for hop, piece in enumerate((quads[0] - quads[1], quads[1])):
        rows = slice(hop * 12 + side * 8, hop * 12 + side * 8 + 4)
        new_ref[rows, :] = new_ref[rows, :] + piece[0:4, :]


def shift_kernel(step, shifts_ref, sums_ref, from_odd_ref, from_even_ref, axes_ref, mom_ref, joint_ref, shift_ref, new_ref, odd_ref, even_ref, work_ref, tot_ref, next_ref):
    add_x(sums_ref, from_odd_ref, from_even_ref, work_ref)
    means = cell_means(work_ref, tot_ref)
    shift_ref[...] = jnp.zeros_like(shift_ref)
    store_cells(shift_ref, shifts_of(means, [axes_ref[comp] for comp in range(3)]))
    nested = nested_hops(step, shifts_ref)
    for col in range(2):
        parts = corner_differences(shift_ref, ((col, col + 1), (3 + col, 4 + col)))
        for later in range(8):
            row = (col * 8 + later) * 8
            next_ref[row : row + 8, :] = mom_ref[row : row + 8, :] + joint_moment(joint_ref, [(col * 27, parts)], later, nested, (9, 3, 1))
    cell_sums(stored_moment(next_ref), new_ref)
    fill_messages_x(new_ref, 12, odd_ref, even_ref)


def wide_shift_kernel(step, shifts_ref, sums_ref, from_odd_ref, from_even_ref, axes_ref, turned_ref, joint_ref, shift_ref, new_ref, odd_ref, even_ref, work_ref, tot_ref, next_ref, far_ref, left_ref, right_ref):
    by_left, by_right = from_sides("gy", from_odd_ref[...], from_even_ref[...])
    left_ref[...] = by_left
    right_ref[...] = by_right
    add_y(sums_ref, left_ref, right_ref, work_ref)
    means = cell_means(work_ref, tot_ref, 10)
    far_ref[...] = jnp.zeros_like(far_ref)
    store_cells(far_ref, shifts_of(means, [axes_ref[comp] for comp in range(3)]), 10)
    own_cells(far_ref, shift_ref)
    nested = nested_hops(step, shifts_ref)
    for col in range(2):
        parts = corner_differences(far_ref, ((col + 1, col + 2), (col + 6, col + 7)))
        for later in range(8):
            row = (col * 8 + later) * 8
            next_ref[row : row + 8, :] = joint_moment(joint_ref, [(col * 27, parts)], later, nested, (9, 3, 1))
    cell_sums(stored_moment(next_ref), new_ref)
    new_ref[...] = new_ref[...] + turned_ref[...]
    for side, came_ref in enumerate((left_ref, right_ref)):
        for hop in range(2):
            rows = slice(hop * 12 + side * 8, hop * 12 + side * 8 + 4)
            new_ref[rows, :] = new_ref[rows, :] + came_ref[16 + hop * 4 : 20 + hop * 4, :]
        add_side(new_ref, side, came_ref, [(24, corner_differences(far_ref, side_cells(side)))], nested)
    fill_messages_x(new_ref, 12, odd_ref, even_ref)


def last_kernel(shifts_ref, code_ref, vel_ref, sums_ref, from_odd_ref, from_even_ref, axes_ref, out_hbm, means_hbm, work_ref, tot_ref, table_ref, end_ref, out_ref, means_ref, sems):
    add_x(sums_ref, from_odd_ref, from_even_ref, work_ref)
    means = cell_means(work_ref, tot_ref)
    turn = turned([axes_ref[comp] for comp in range(3)], means)
    table_ref[...] = jnp.zeros_like(table_ref)
    store_cells(table_ref, [means[comp] - turn[comp] for comp in range(3)])
    for comp in range(3):
        means_ref[comp] = means[comp][0:2, :]
    saves = [pltpu.make_async_copy(means_ref, means_hbm, sems.at[6])]
    saves[0].start()
    limits = hop_limits(shifts_ref, ITERS - 1)
    for col in range(2):
        for _, lanes in blocks((col,)):

            def body(rows):
                code = code_ref[col, rows, lanes]
                masks = hop_masks(code, limits)
                filled = code >= 0
                for comp in range(3):
                    value = vel_ref[comp * 2 + col, rows, lanes] + pick(table_ref, comp, col, lanes, masks)
                    end_ref[comp * 2 + col, rows, lanes] = jnp.where(filled, value, 0.0)

            over_slots(body)
        for comp in range(3):
            at = comp * 2 + col
            out_ref[at] = end_ref[at].T.astype(jnp.bfloat16)
            saves.append(pltpu.make_async_copy(out_ref.at[at], out_hbm.at[at], sems.at[at]))
            saves[-1].start()
    for save in saves:
        save.wait()


VMEM = pl.BlockSpec(memory_space=pltpu.VMEM)
HBM = pl.BlockSpec(memory_space=pltpu.HBM)
BYTES = 8_000_000


def call(kernel, name, in_specs, shapes, scratch, cost=0, out_specs=None):
    return pl.pallas_call(
        kernel,
        out_shape=[jax.ShapeDtypeStruct(s, d) for s, d in shapes],
        in_specs=in_specs,
        out_specs=out_specs or [VMEM] * len(shapes),
        scratch_shapes=scratch,
        compiler_params=pltpu.CompilerParams(vmem_limit_bytes=16 * 1024 * 1024),
        cost_estimate=pl.CostEstimate(flops=0, bytes_accessed=cost, transcendentals=0) if cost else None,
        name=name,
    )


def swap(odd, even, axis):
    count = lax.axis_size(axis)
    evens = [(s, s ^ 1) for s in range(count)]
    odds = [(s, (((s - 1) % count ^ 1) + 1) % count) for s in range(count)]
    from_even = lax.ppermute(even, axis, evens)
    from_odd = lax.ppermute(odd, axis, odds)
    return from_odd, from_even


def on_device(velocity, position_code, occupancy, shifts, axis_ids):
    vel_in = velocity.reshape(3, 2, 256, 128)
    code_in = position_code.reshape(2, 256, 128)
    occ = occupancy.reshape(2, 256)
    ids_in = axis_ids.reshape(ITERS, 2, 256)

    def rows(count):
        return ((count, 256), F32)

    def room(*shape):
        return pltpu.VMEM(shape, F32)

    vel_shape, code_shape = ((6, 128, 256), F32), ((2, 128, 256), jnp.int32)
    table_shape, axes_shape = ((2, WIDE, 256), F32), ((3, 8, 256), F32)
    moments, table = room(128, 256), room(2, WIDE, 256)
    small = [room(24, 256), room(4, 8, 256)]
    wide_small, far = [room(40, 256), room(4, 16, 256)], room(2, 80, 256)

    vel, code, sums, odd, even = call(
        start_kernel, "start", [HBM] * 5, [vel_shape, code_shape, rows(24), rows(20), rows(20)],
        [moments, pltpu.VMEM((3, 2, 256, 128), jnp.bfloat16), pltpu.VMEM((2, 256, 128), jnp.int32), pltpu.VMEM((2, 256), jnp.int32), pltpu.VMEM((ITERS, 2, 256), jnp.int32), pltpu.SMEM((ITERS, 3), jnp.int32), pltpu.SemaphoreType.DMA((11,))],
    )(*(pltpu.with_memory_space_constraint(x, pltpu.HBM) for x in (shifts, vel_in, code_in, occ, ids_in)))

    from_odd, from_even = swap(odd, even, "gx")
    classes, class_odd, class_even = call(
        class_kernel, "classes", [VMEM] * 3, [rows(216), rows(72), rows(72)], [], BYTES
    )(shifts, vel, code)
    sums, both, odd, even = call(
        first_middle_kernel, "middle0", [VMEM] * 6, [rows(24), rows(16), rows(100), rows(100)], [],
    )(sums, from_odd, from_even, ids_in, class_odd, class_even)
    from_odd, from_even = swap(odd, even, "gy")
    *joints, joint_odd, joint_even = call(
        joint_kernel, "joint", [VMEM] * 2, [rows(54), rows(54), rows(18), rows(18)], [], BYTES
    )(shifts, code)
    ids, far_ids, shift, sums, odd, even = call(
        first_kernel, "first", [VMEM] * 7, [rows(32), rows(32), table_shape, rows(24), rows(12), rows(12)],
        [moments, *wide_small, far, room(3, 2, 80, 256), room(100, 256), room(100, 256)],
    )(shifts, sums, from_odd, from_even, both, classes, joints[0])

    for step in range(1, ITERS):
        last, wide = step == ITERS - 1, step == WIDE_STEP
        from_odd, from_even = swap(odd, even, "gx")
        args = [shifts, code, ids, vel, shift]
        shapes, scratch = [vel_shape, axes_shape], [table] * (2 if step == 1 else 1)
        if wide:
            args.append(far_ids)
            shapes = [vel_shape, ((3, 16, 256), F32), rows(24)]
            scratch = [table, moments]
        elif not last:
            shapes.append(rows(128))
        vel, axes, *more = call(
            functools.partial(turn_kernel, step), f"turn{step}", [VMEM] * len(args), shapes, scratch, BYTES,
        )(*args)
        if last:
            out, out_means = call(
                last_kernel, "last", [VMEM] * 7, [((6, 256, 128), jnp.bfloat16), ((3, 2, 256), F32)],
                [*small, table, room(6, 128, 256), pltpu.VMEM((6, 256, 128), jnp.bfloat16), room(3, 2, 256), pltpu.SemaphoreType.DMA((7,))],
                out_specs=[HBM, HBM],
            )(shifts, code, vel, sums, from_odd, from_even, axes)
        elif wide:
            sums, odd, even = call(
                wide_middle_kernel, f"middle{step}", [VMEM] * 6, [rows(24), rows(42), rows(42)], [],
            )(sums, from_odd, from_even, more[0], joint_odd, joint_even)
            from_odd, from_even = swap(odd, even, "gy")
            shift, sums, odd, even = call(
                functools.partial(wide_shift_kernel, step), f"shift{step}", [VMEM] * 7,
                [table_shape, rows(24), rows(12), rows(12)], [*wide_small, moments, far, room(42, 256), room(42, 256)],
            )(shifts, sums, from_odd, from_even, axes, more[0], joints[step - 1])
        else:
            shift, sums, odd, even = call(
                functools.partial(shift_kernel, step), f"shift{step}", [VMEM] * 7,
                [table_shape, rows(24), rows(12), rows(12)], [*small, moments],
            )(shifts, sums, from_odd, from_even, axes, more[0], joints[step - 1])
    return out.reshape(velocity.shape), out_means.reshape(3, *occupancy.shape)


def solution(mesh):
    in_specs = (
        P(None, "gx", "gy", None, None),
        P("gx", "gy", None, None),
        P("gx", "gy", None),
        P(),
        P(None, "gx", "gy", None),
    )
    out_specs = (P(None, "gx", "gy", None, None), P(None, "gx", "gy", None))
    return jax.shard_map(
        on_device, mesh=mesh, in_specs=in_specs, out_specs=out_specs, check_vma=False
    )
```

```python
import functools
import math

import jax
import jax.numpy as jnp
import numpy as np
from jax import lax
from jax.experimental import pallas as pl
from jax.experimental.pallas import tpu as pltpu
from jax.sharding import PartitionSpec as P

SUBDIV = 8
NAXES = 32
ITERS = 4
GOLDEN = 2.399963229728653
TURN_COS = math.cos(130.0 * math.pi / 180.0)
TURN_SIN = math.sin(130.0 * math.pi / 180.0)
ALONG = (1.0 - TURN_COS) / (TURN_SIN * TURN_SIN)

F32 = jnp.float32
CHUNK = 32
WIDE = 48
WIDE_STEP = 2


def axis_table():
    ordinal = np.arange(NAXES, dtype=np.float64)
    height = 1.0 - (2.0 * ordinal + 1.0) / NAXES
    radius = np.sqrt(1.0 - height * height)
    phases = ordinal * GOLDEN
    return TURN_SIN * np.stack([radius * np.cos(phases), radius * np.sin(phases), height])


AXES = axis_table()


def is_odd(axis):
    return lax.rem(lax.axis_index(axis), 2) == 1


def hop_limits(shifts_ref, step):
    return [(SUBDIV - shifts_ref[step, dim]) * SUBDIV ** (2 - dim) for dim in range(3)]


def hop_masks(code, limits):
    hop_x = code >= limits[0]
    hop_y = (code & (SUBDIV * SUBDIV - 1)) >= limits[1]
    hop_z = (code & (SUBDIV - 1)) >= limits[2]
    return hop_x, hop_y, hop_z


def slot_sums(values, count, col, lanes, code_ref, shifts_ref, step, mom_ref):
    def body(i, acc):
        rows = pl.ds(pl.multiple_of(i * 8, 8), 8)
        code = code_ref[col, rows, lanes]
        hop_x, hop_y, hop_z = hop_masks(code, hop_limits(shifts_ref, step))
        out = list(acc)
        for comp, value in enumerate(values(rows, code)):
            with_x = jnp.where(hop_x, value, 0.0)
            with_y = jnp.where(hop_y, value, 0.0)
            with_xy = jnp.where(hop_y, with_x, 0.0)
            for pair, base in ((0, value), (2, with_y), (4, with_x), (6, with_xy)):
                at = comp * 8 + pair
                out[at] = out[at] + base
                out[at + 1] = out[at + 1] + jnp.where(hop_z, base, 0.0)
        return tuple(out)

    zero = jnp.zeros((8, 128), F32)
    acc = lax.fori_loop(0, 16, body, (zero,) * (8 * count), unroll=16)
    for comp in range(count):
        for moment in range(8):
            row = (col * 8 + moment) * 8 + comp
            mom_ref[row : row + 1, lanes] = jnp.sum(acc[comp * 8 + moment], axis=0, keepdims=True)


def blocks(cols=(0, 1)):
    for col in cols:
        for half in range(2):
            yield col, slice(half * 128, half * 128 + 128)


def deposit(vel_ref, code_ref, shifts_ref, step, mom_ref, counted, cols=(0, 1)):
    for col, lanes in blocks(cols):

        def values(rows, code):
            parts = [vel_ref[comp * 2 + col, rows, lanes] for comp in range(3)]
            return parts + ([jnp.where(code >= 0, 1.0, 0.0)] if counted else [])

        slot_sums(values, 4 if counted else 3, col, lanes, code_ref, shifts_ref, step, mom_ref)


def cell_sums(moment_of, sums_ref):
    pieces = {}
    for col in range(2):
        quads = {}
        for moment in (0, 2, 4, 6):
            up = moment_of(col, moment + 1)
            quads[moment] = moment_of(col, moment) - up + pltpu.roll(up, 1, 1)
        pieces[col, 1, 1] = quads[6]
        pieces[col, 1, 0] = quads[4] - quads[6]
        pieces[col, 0, 1] = quads[2] - quads[6]
        pieces[col, 0, 0] = quads[0] - quads[2] - quads[4] + quads[6]
    for hop in range(2):
        columns = (pieces[0, hop, 0], pieces[0, hop, 1] + pieces[1, hop, 0], pieces[1, hop, 1])
        for at, piece in enumerate(columns):
            row = (hop * 3 + at) * 4
            sums_ref[row : row + 4, :] = piece[0:4, :]


def stored_moment(mom_ref):
    def moment_of(col, moment):
        row = (col * 8 + moment) * 8
        return mom_ref[row : row + 8, :]

    return moment_of


def fill_messages_y(sums_ref, odd_ref, even_ref, columns=1, first=0):
    odd = is_odd("gy")
    size = columns * 4
    for hop in range(2):
        left = sums_ref[hop * 12 : hop * 12 + size, :]
        right = sums_ref[hop * 12 + 12 - size : hop * 12 + 12, :]
        rows = slice(first + hop * size, first + hop * size + size)
        odd_ref[rows, :] = jnp.where(odd, right, left)
        even_ref[rows, :] = jnp.where(odd, left, right)


def fill_messages_x(out_ref, size, odd_ref, even_ref):
    odd = is_odd("gx")
    low, high = out_ref[0:size, :], out_ref[size : 2 * size, :]
    odd_ref[0:size, :] = jnp.where(odd, high, low)
    even_ref[0:size, :] = jnp.where(odd, low, high)


def from_sides(axis, from_odd, from_even):
    odd = is_odd(axis)
    return jnp.where(odd, from_even, from_odd), jnp.where(odd, from_odd, from_even)


def start_kernel(shifts_hbm, vel_hbm, code_hbm, occ_hbm, ids_hbm, vel_ref, code_ref, sums_ref, odd_ref, even_ref, mom_ref, vel_in_ref, code_in_ref, occ_ref, ids_ref, shifts_ref, sems):
    fetch_shifts = pltpu.make_async_copy(shifts_hbm, shifts_ref, sems.at[10])
    fetch_occ = pltpu.make_async_copy(occ_hbm, occ_ref, sems.at[8])
    fetch_ids = pltpu.make_async_copy(ids_hbm, ids_ref, sems.at[9])
    fetch_shifts.start()
    fetch_occ.start()
    copies = []
    for col in range(2):
        copies.append(pltpu.make_async_copy(code_hbm.at[col], code_in_ref.at[col], sems.at[col]))
        copies.append(pltpu.make_async_copy(vel_hbm.at[:, col], vel_in_ref.at[:, col], sems.at[2 + col]))
    for copy in copies:
        copy.start()
    fetch_ids.start()
    mom_ref[...] = jnp.zeros_like(mom_ref)
    slot = lax.broadcasted_iota(jnp.int32, (128, 256), 0)
    fetch_occ.wait()
    fetch_shifts.wait()
    for col in range(2):
        filled = slot < occ_ref[col : col + 1, :]
        copies[2 * col].wait()
        code_ref[col] = jnp.where(filled, code_in_ref[col].T, -1)
        copies[2 * col + 1].wait()
        for comp in range(3):
            vel_ref[comp * 2 + col] = jnp.where(filled, vel_in_ref[comp, col].astype(F32).T, 0.0)
        deposit(vel_ref, code_ref, shifts_ref, 0, mom_ref, True, (col,))
    fetch_ids.wait()
    for step in range(ITERS):
        ids = ids_ref[step].astype(F32)
        rows = slice(12 + step * 2, 14 + step * 2)
        odd_ref[rows, :] = ids
        even_ref[rows, :] = ids
    cell_sums(stored_moment(mom_ref), sums_ref)
    fill_messages_x(sums_ref, 12, odd_ref, even_ref)


def add_x(sums_ref, from_odd_ref, from_even_ref, out_ref):
    by_low, by_high = from_sides("gx", from_odd_ref[0:12, :], from_even_ref[0:12, :])
    out_ref[0:12, :] = sums_ref[0:12, :] + by_low
    out_ref[12:24, :] = sums_ref[12:24, :] + by_high


def add_y(sums_ref, by_left_ref, by_right_ref, out_ref):
    for hop in range(2):
        at, own, rows = hop * 20, hop * 12, slice(hop * 8, hop * 8 + 8)
        out_ref[at : at + 8, :] = by_left_ref[rows, :]
        out_ref[at + 12 : at + 20, :] = by_right_ref[rows, :]
        out_ref[at + 8 : at + 12, :] = sums_ref[own + 4 : own + 8, :]
        out_ref[at + 4 : at + 8, :] = out_ref[at + 4 : at + 8, :] + sums_ref[own : own + 4, :]
        out_ref[at + 12 : at + 16, :] = out_ref[at + 12 : at + 16, :] + sums_ref[own + 8 : own + 12, :]


def first_middle_kernel(sums_ref, from_odd_ref, from_even_ref, ids_ref, ghost_odd_ref, ghost_even_ref, out_ref, both_ref, odd_ref, even_ref):
    add_x(sums_ref, from_odd_ref, from_even_ref, out_ref)
    fill_messages_y(out_ref, odd_ref, even_ref, 2)
    for step in range(ITERS):
        both_ref[step * 2 : step * 2 + 2, :] = ids_ref[step].astype(F32)
    _, by_high = from_sides("gx", from_odd_ref[12:20, :], from_even_ref[12:20, :])
    both_ref[8:16, :] = by_high
    for ref in (odd_ref, even_ref):
        for x in range(2):
            for step in range(ITERS):
                ref[16 + x * 4 + step : 17 + x * 4 + step, :] = both_ref[x * 8 + step * 2 : x * 8 + step * 2 + 1, :]
            for k, step in enumerate((0, WIDE_STEP)):
                ref[24 + x * 2 + k : 25 + x * 2 + k, :] = both_ref[x * 8 + step * 2 + 1 : x * 8 + step * 2 + 2, :]
    odd_ref[28:100, :] = ghost_odd_ref[...]
    even_ref[28:100, :] = ghost_even_ref[...]


def wide_middle_kernel(sums_ref, from_odd_ref, from_even_ref, turned_ref, joint_odd_ref, joint_even_ref, out_ref, odd_ref, even_ref):
    add_x(sums_ref, from_odd_ref, from_even_ref, out_ref)
    fill_messages_y(out_ref, odd_ref, even_ref, 2)
    fill_messages_y(turned_ref, odd_ref, even_ref, 1, 16)
    odd_ref[24:42, :] = joint_odd_ref[...]
    even_ref[24:42, :] = joint_even_ref[...]


def cell_means(work_ref, tot_ref, cells=6):
    tot_ref[...] = jnp.zeros_like(tot_ref)
    for cell in range(cells):
        for comp in range(4):
            tot_ref[comp, cell : cell + 1, :] = work_ref[cell * 4 + comp : cell * 4 + comp + 1, :]
    count = jnp.maximum(tot_ref[3], 1.0)
    return [tot_ref[comp] / count for comp in range(3)]


def cell_axes(ids):
    axes = [jnp.zeros(ids.shape, F32) for _ in range(3)]
    for k in range(NAXES):
        match = ids == float(k)
        axes = [jnp.where(match, float(AXES[comp, k]), axes[comp]) for comp in range(3)]
    return axes


def turned(axis, vec):
    along = (axis[0] * vec[0] + axis[1] * vec[1] + axis[2] * vec[2]) * ALONG
    out = []
    for comp in range(3):
        b, c = (comp + 1) % 3, (comp + 2) % 3
        out.append(TURN_COS * vec[comp] + (axis[b] * vec[c] - axis[c] * vec[b]) + along * axis[comp])
    return out


def next_z(value):
    return pltpu.roll(value, 255, 1)


def store_cells(table_ref, parts, cells=6):
    for cell in range(cells):
        for comp, part in enumerate(parts):
            table_ref[0, cell * 8 + comp : cell * 8 + comp + 1, :] = part[cell : cell + 1, :]
    table_ref[1] = next_z(table_ref[0])


def pick(table_ref, comp, col, lanes, masks):
    hop_x, hop_y, hop_z = masks
    by_x = []
    for step_x in range(2):
        by_y = []
        for step_y in range(2):
            row = (step_x * 3 + col + step_y) * 8 + comp
            by_y.append(jnp.where(hop_z, table_ref[1, row : row + 1, lanes], table_ref[0, row : row + 1, lanes]))
        by_x.append(jnp.where(hop_y, by_y[1], by_y[0]))
    return jnp.where(hop_x, by_x[1], by_x[0])


def over_slots(body):
    def run(i, carry):
        body(pl.ds(pl.multiple_of(i * CHUNK, CHUNK), CHUNK))
        return carry

    lax.fori_loop(0, 128 // CHUNK, run, 0, unroll=128 // CHUNK)


def first_kernel(shifts_ref, sums_ref, from_odd_ref, from_even_ref, both_ref, joint_ref, _, ids_ref, far_ids_ref, shift_ref, new_ref, odd_ref, even_ref, next_ref, work_ref, tot_ref, far_ref, turn_ref, left_ref, right_ref):
    by_left, by_right = from_sides("gy", from_odd_ref[...], from_even_ref[...])
    left_ref[...] = by_left
    right_ref[...] = by_right
    ids_ref[...] = jnp.zeros_like(ids_ref)
    for x in range(2):
        for t in range(ITERS):
            row = t * 8 + x * 3
            ids_ref[row : row + 2, :] = both_ref[x * 8 + t * 2 : x * 8 + t * 2 + 2, :]
            ids_ref[row + 2 : row + 3, :] = right_ref[16 + x * 4 + t : 17 + x * 4 + t, :]
    far_ids_ref[...] = jnp.zeros_like(far_ids_ref)
    for k, t in enumerate((0, WIDE_STEP)):
        for x in range(2):
            row, outer = k * 16 + x * 5, slice(24 + x * 2 + k, 25 + x * 2 + k)
            far_ids_ref[row : row + 1, :] = left_ref[outer, :]
            far_ids_ref[row + 1 : row + 4, :] = ids_ref[t * 8 + x * 3 : t * 8 + x * 3 + 3, :]
            far_ids_ref[row + 4 : row + 5, :] = right_ref[outer, :]
    add_y(sums_ref, left_ref, right_ref, work_ref)
    means = cell_means(work_ref, tot_ref, 10)
    axes = cell_axes(far_ids_ref[0:16, :])
    far_ref[...] = jnp.zeros_like(far_ref)
    store_cells(far_ref, shifts_of(means, axes), 10)
    own_cells(far_ref, shift_ref)
    turn_ref[...] = jnp.zeros_like(turn_ref)
    zero = jnp.zeros((16, 256), F32)
    for k in range(3):
        unit = [zero + (1.0 if comp == k else 0.0) for comp in range(3)]
        store_cells(turn_ref.at[k], turned(axes, unit), 10)
    nested = nested_hops(0, shifts_ref)

    def sources_of(cells, first, size):
        tables = [far_ref] + [turn_ref.at[k] for k in range(3)]
        return [(first + at * size, corner_differences(table, cells)) for at, table in enumerate(tables)]

    for col in range(2):
        sources = sources_of(((col + 1, col + 2), (col + 6, col + 7)), col * 27, 54)
        for later in range(8):
            row = (col * 8 + later) * 8
            next_ref[row : row + 8, :] = joint_moment(joint_ref, sources, later, nested, (9, 3, 1))
    cell_sums(stored_moment(next_ref), new_ref)
    for side, came_ref in enumerate((left_ref, right_ref)):
        add_side(new_ref, side, came_ref, sources_of(side_cells(side), 28, 18), nested)
    fill_messages_x(new_ref, 12, odd_ref, even_ref)


def joint_sums(vel_ref, code_ref, shifts_ref, t, out_ref):
    def classes(value, now, later):
        out = []
        for by_x in (value, jnp.where(now[0], value, 0), jnp.where(later[0], value, 0)):
            out += [by_x, jnp.where(now[1], by_x, 0), jnp.where(later[1], by_x, 0)]
        return out

    now_limits, later_limits = hop_limits(shifts_ref, t), hop_limits(shifts_ref, t + 1)

    def body(col, lanes, comp, counts, i, acc):
        rows = pl.ds(pl.multiple_of(i * 8, 8), 8)
        code = code_ref[col, rows, lanes]
        now, later = hop_masks(code, now_limits), hop_masks(code, later_limits)
        out = []
        if comp is not None:
            for value in classes(vel_ref[comp * 2 + col, rows, lanes], now, later):
                out += [value, jnp.where(now[2], value, 0.0), jnp.where(later[2], value, 0.0)]
        if counts:
            word = jnp.where(now[2], 1 + 256, 1) + jnp.where(later[2], 65536, 0)
            out += classes(jnp.where(code >= 0, word, 0), now, later)
        return tuple(a + b for a, b in zip(acc, out))

    zero, none = (jnp.zeros((8, 128), F32),) * 27, (jnp.zeros((8, 128), jnp.int32),) * 9
    for col, lanes in blocks():
        for comp, counts in ((None, True),) if vel_ref is None else ((0, False), (1, False), (2, True)):
            start = (() if comp is None else zero) + (none if counts else ())
            acc = lax.fori_loop(0, 16, functools.partial(body, col, lanes, comp, counts), start, unroll=8)
            if comp is not None:
                for at in range(27):
                    row = 54 + comp * 54 + col * 27 + at
                    out_ref[row : row + 1, lanes] = jnp.sum(acc[at], axis=0, keepdims=True)
            if counts:
                for at, word in enumerate(acc[-9:]):
                    for z in range(3):
                        part = lax.shift_right_logical(word, 8 * z) & 255
                        row = col * 27 + at * 3 + z
                        out_ref[row : row + 1, lanes] = jnp.sum(part.astype(F32), axis=0, keepdims=True)


def boundary_sums(joint_ref, kinds, nested, odd_ref, even_ref):
    odd = is_odd("gy")
    for kind in range(kinds):
        for x in range(3):
            for y in range(2):
                for z in range(3):
                    first = kind * 54 + x * 9 + z
                    hopped = (nested[1] if y else 2) * 3
                    left = joint_ref[first + y * 3 : first + y * 3 + 1, :] - joint_ref[pl.ds(first + hopped, 1), :]
                    right = joint_ref[pl.ds(27 + first + hopped, 1), :]
                    row = kind * 18 + x * 6 + y * 3 + z
                    odd_ref[row : row + 1, :] = jnp.where(odd, right, left)
                    even_ref[row : row + 1, :] = jnp.where(odd, left, right)


def class_kernel(shifts_ref, vel_ref, code_ref, out_ref, odd_ref, even_ref):
    joint_sums(vel_ref, code_ref, shifts_ref, 0, out_ref)
    boundary_sums(out_ref, 4, nested_hops(0, shifts_ref), odd_ref, even_ref)


def joint_kernel(shifts_ref, code_ref, first_ref, second_ref, odd_ref, even_ref):
    joint_sums(None, code_ref, shifts_ref, 1, first_ref)
    joint_sums(None, code_ref, shifts_ref, 2, second_ref)
    boundary_sums(second_ref, 1, nested_hops(WIDE_STEP, shifts_ref), odd_ref, even_ref)


def turn_kernel(step, *refs):
    shifts_ref, code_ref, ids_ref, vel_ref, last_ref, *refs = refs
    if step == 1:
        *refs, before_ref = refs
        before_ref[...] = jnp.zeros_like(before_ref)
        store_cells(before_ref, cell_axes(ids_ref[0:8, :]))
    if step == WIDE_STEP:
        far_ids_ref, out_ref, axes_ref, sums_ref, table_ref, mom_ref = refs
        for comp, axis in enumerate(cell_axes(far_ids_ref[16:32, :])):
            axes_ref[comp] = axis
    elif step < ITERS - 1:
        out_ref, axes_ref, mom_ref, table_ref = refs
    else:
        out_ref, axes_ref, table_ref = refs
    axes = cell_axes(ids_ref[step * 8 : step * 8 + 8, :])
    if step != WIDE_STEP:
        for comp in range(3):
            axes_ref[comp] = axes[comp]
    table_ref[...] = jnp.zeros_like(table_ref)
    store_cells(table_ref, axes)
    for col, lanes in blocks():

        def body(rows):
            code = code_ref[col, rows, lanes]
            vel = [vel_ref[comp * 2 + col, rows, lanes] for comp in range(3)]
            masks = hop_masks(code, hop_limits(shifts_ref, step - 1))
            if step == 1:
                vel = turned([pick(before_ref, comp, col, lanes, masks) for comp in range(3)], vel)
            filled = code >= 0
            vel = [jnp.where(filled, vel[comp] + pick(last_ref, comp, col, lanes, masks), 0.0) for comp in range(3)]
            masks = hop_masks(code, hop_limits(shifts_ref, step))
            turn = turned([pick(table_ref, comp, col, lanes, masks) for comp in range(3)], vel)
            for comp in range(3):
                out_ref[comp * 2 + col, rows, lanes] = turn[comp]

        over_slots(body)
    if step < ITERS - 1:
        mom_ref[...] = jnp.zeros_like(mom_ref)
        deposit(out_ref, code_ref, shifts_ref, step + 1, mom_ref, False)
    if step == WIDE_STEP:
        cell_sums(stored_moment(mom_ref), sums_ref)


def nested_hops(step, shifts_ref):
    return [jnp.where(shifts_ref[step, dim] <= shifts_ref[step + 1, dim], 1, 2) for dim in range(3)]


def corner_differences(shift_ref, cells):
    parts = {}
    for corner in range(8):
        cell = cells[corner >> 2][corner >> 1 & 1]
        parts[corner] = shift_ref[corner & 1, cell * 8 : cell * 8 + 8, :]
    for bit in (1, 2, 4):
        for corner in range(8):
            if corner & bit:
                parts[corner] = parts[corner] - parts[corner ^ bit]
    return parts


def joint_moment(joint_ref, sources, later, nested, weights):
    total = None
    for now in range(8):
        at = 0
        for dim, (bit, weight) in enumerate(zip((4, 2, 1), weights)):
            if now & bit and later & bit:
                at = at + nested[dim] * weight
            elif now & bit:
                at = at + weight
            elif later & bit:
                at = at + 2 * weight
        for first, parts in sources:
            term = joint_ref[pl.ds(first + at, 1), :] * parts[now]
            total = term if total is None else total + term
    return total


def shifts_of(means, axes):
    turn = turned(axes, means)
    return [means[comp] - turn[comp] for comp in range(3)] + [jnp.ones_like(means[0])]


def own_cells(far_ref, out_ref):
    for hop in range(2):
        for side in range(2):
            out_ref[side, hop * 24 : hop * 24 + 24, :] = far_ref[side, hop * 40 + 8 : hop * 40 + 32, :]


def side_cells(side):
    first = side * 3
    return ((first, first + 1), (first + 5, first + 6))


def add_side(new_ref, side, came_ref, sources, nested):
    def moment_of(later):
        return joint_moment(came_ref, sources, later, nested, (6, 3, 1))

    quads = []
    for moment in (0, 4):
        up = moment_of(moment + 1)
        quads.append(moment_of(moment) - up + pltpu.roll(up, 1, 1))
    for hop, piece in enumerate((quads[0] - quads[1], quads[1])):
        rows = slice(hop * 12 + side * 8, hop * 12 + side * 8 + 4)
        new_ref[rows, :] = new_ref[rows, :] + piece[0:4, :]


def shift_kernel(step, shifts_ref, sums_ref, from_odd_ref, from_even_ref, axes_ref, mom_ref, joint_ref, shift_ref, new_ref, odd_ref, even_ref, work_ref, tot_ref, next_ref):
    add_x(sums_ref, from_odd_ref, from_even_ref, work_ref)
    means = cell_means(work_ref, tot_ref)
    shift_ref[...] = jnp.zeros_like(shift_ref)
    store_cells(shift_ref, shifts_of(means, [axes_ref[comp] for comp in range(3)]))
    nested = nested_hops(step, shifts_ref)
    for col in range(2):
        parts = corner_differences(shift_ref, ((col, col + 1), (3 + col, 4 + col)))
        for later in range(8):
            row = (col * 8 + later) * 8
            next_ref[row : row + 8, :] = mom_ref[row : row + 8, :] + joint_moment(joint_ref, [(col * 27, parts)], later, nested, (9, 3, 1))
    cell_sums(stored_moment(next_ref), new_ref)
    fill_messages_x(new_ref, 12, odd_ref, even_ref)


def wide_shift_kernel(step, shifts_ref, sums_ref, from_odd_ref, from_even_ref, axes_ref, turned_ref, joint_ref, shift_ref, new_ref, odd_ref, even_ref, work_ref, tot_ref, next_ref, far_ref, left_ref, right_ref):
    by_left, by_right = from_sides("gy", from_odd_ref[...], from_even_ref[...])
    left_ref[...] = by_left
    right_ref[...] = by_right
    add_y(sums_ref, left_ref, right_ref, work_ref)
    means = cell_means(work_ref, tot_ref, 10)
    far_ref[...] = jnp.zeros_like(far_ref)
    store_cells(far_ref, shifts_of(means, [axes_ref[comp] for comp in range(3)]), 10)
    own_cells(far_ref, shift_ref)
    nested = nested_hops(step, shifts_ref)
    for col in range(2):
        parts = corner_differences(far_ref, ((col + 1, col + 2), (col + 6, col + 7)))
        for later in range(8):
            row = (col * 8 + later) * 8
            next_ref[row : row + 8, :] = joint_moment(joint_ref, [(col * 27, parts)], later, nested, (9, 3, 1))
    cell_sums(stored_moment(next_ref), new_ref)
    new_ref[...] = new_ref[...] + turned_ref[...]
    for side, came_ref in enumerate((left_ref, right_ref)):
        for hop in range(2):
            rows = slice(hop * 12 + side * 8, hop * 12 + side * 8 + 4)
            new_ref[rows, :] = new_ref[rows, :] + came_ref[16 + hop * 4 : 20 + hop * 4, :]
        add_side(new_ref, side, came_ref, [(24, corner_differences(far_ref, side_cells(side)))], nested)
    fill_messages_x(new_ref, 12, odd_ref, even_ref)


def last_kernel(shifts_ref, code_ref, vel_ref, sums_ref, from_odd_ref, from_even_ref, axes_ref, out_hbm, means_hbm, work_ref, tot_ref, table_ref, end_ref, out_ref, means_ref, sems):
    add_x(sums_ref, from_odd_ref, from_even_ref, work_ref)
    means = cell_means(work_ref, tot_ref)
    turn = turned([axes_ref[comp] for comp in range(3)], means)
    table_ref[...] = jnp.zeros_like(table_ref)
    store_cells(table_ref, [means[comp] - turn[comp] for comp in range(3)])
    for comp in range(3):
        means_ref[comp] = means[comp][0:2, :]
    saves = [pltpu.make_async_copy(means_ref, means_hbm, sems.at[2])]
    saves[0].start()
    limits = hop_limits(shifts_ref, ITERS - 1)
    for col in range(2):
        for _, lanes in blocks((col,)):

            def body(rows):
                code = code_ref[col, rows, lanes]
                masks = hop_masks(code, limits)
                filled = code >= 0
                for comp in range(3):
                    value = vel_ref[comp * 2 + col, rows, lanes] + pick(table_ref, comp, col, lanes, masks)
                    end_ref[comp * 2 + col, rows, lanes] = jnp.where(filled, value, 0.0)

            over_slots(body)
        for comp in range(3):
            out_ref[comp, col] = end_ref[comp * 2 + col].T.astype(jnp.bfloat16)
        saves.append(pltpu.make_async_copy(out_ref.at[:, col], out_hbm.at[:, col], sems.at[col]))
        saves[-1].start()
    for save in saves:
        save.wait()


VMEM = pl.BlockSpec(memory_space=pltpu.VMEM)
HBM = pl.BlockSpec(memory_space=pltpu.HBM)
BYTES = 8_000_000


def call(kernel, name, in_specs, shapes, scratch, cost=0, out_specs=None):
    return pl.pallas_call(
        kernel,
        out_shape=[jax.ShapeDtypeStruct(s, d) for s, d in shapes],
        in_specs=in_specs,
        out_specs=out_specs or [VMEM] * len(shapes),
        scratch_shapes=scratch,
        compiler_params=pltpu.CompilerParams(vmem_limit_bytes=16 * 1024 * 1024),
        cost_estimate=pl.CostEstimate(flops=0, bytes_accessed=cost, transcendentals=0) if cost else None,
        name=name,
    )


def swap(odd, even, axis):
    count = lax.axis_size(axis)
    evens = [(s, s ^ 1) for s in range(count)]
    odds = [(s, (((s - 1) % count ^ 1) + 1) % count) for s in range(count)]
    from_even = lax.ppermute(even, axis, evens)
    from_odd = lax.ppermute(odd, axis, odds)
    return from_odd, from_even


def on_device(velocity, position_code, occupancy, shifts, axis_ids):
    vel_in = velocity.reshape(3, 2, 256, 128)
    code_in = position_code.reshape(2, 256, 128)
    occ = occupancy.reshape(2, 256)
    ids_in = axis_ids.reshape(ITERS, 2, 256)

    def rows(count):
        return ((count, 256), F32)

    def room(*shape):
        return pltpu.VMEM(shape, F32)

    vel_shape, code_shape = ((6, 128, 256), F32), ((2, 128, 256), jnp.int32)
    table_shape, axes_shape = ((2, WIDE, 256), F32), ((3, 8, 256), F32)
    moments, table = room(128, 256), room(2, WIDE, 256)
    small = [room(24, 256), room(4, 8, 256)]
    wide_small, far = [room(40, 256), room(4, 16, 256)], room(2, 80, 256)

    vel, code, sums, odd, even = call(
        start_kernel, "start", [HBM] * 5, [vel_shape, code_shape, rows(24), rows(20), rows(20)],
        [moments, pltpu.VMEM((3, 2, 256, 128), jnp.bfloat16), pltpu.VMEM((2, 256, 128), jnp.int32), pltpu.VMEM((2, 256), jnp.int32), pltpu.VMEM((ITERS, 2, 256), jnp.int32), pltpu.SMEM((ITERS, 3), jnp.int32), pltpu.SemaphoreType.DMA((11,))],
    )(*(pltpu.with_memory_space_constraint(x, pltpu.HBM) for x in (shifts, vel_in, code_in, occ, ids_in)))

    from_odd, from_even = swap(odd, even, "gx")
    classes, class_odd, class_even = call(
        class_kernel, "classes", [VMEM] * 3, [rows(216), rows(72), rows(72)], [], BYTES
    )(shifts, vel, code)
    sums, both, odd, even = call(
        first_middle_kernel, "middle0", [VMEM] * 6, [rows(24), rows(16), rows(100), rows(100)], [],
    )(sums, from_odd, from_even, ids_in, class_odd, class_even)
    from_odd, from_even = swap(odd, even, "gy")
    *joints, joint_odd, joint_even = call(
        joint_kernel, "joint", [VMEM] * 2, [rows(54), rows(54), rows(18), rows(18)], [], BYTES
    )(shifts, code)
    ids, far_ids, shift, sums, odd, even = call(
        first_kernel, "first", [VMEM] * 7, [rows(32), rows(32), table_shape, rows(24), rows(12), rows(12)],
        [moments, *wide_small, far, room(3, 2, 80, 256), room(100, 256), room(100, 256)],
    )(shifts, sums, from_odd, from_even, both, classes, joints[0])

    for step in range(1, ITERS):
        last, wide = step == ITERS - 1, step == WIDE_STEP
        from_odd, from_even = swap(odd, even, "gx")
        args = [shifts, code, ids, vel, shift]
        shapes, scratch = [vel_shape, axes_shape], [table] * (2 if step == 1 else 1)
        if wide:
            args.append(far_ids)
            shapes = [vel_shape, ((3, 16, 256), F32), rows(24)]
            scratch = [table, moments]
        elif not last:
            shapes.append(rows(128))
        vel, axes, *more = call(
            functools.partial(turn_kernel, step), f"turn{step}", [VMEM] * len(args), shapes, scratch, BYTES,
        )(*args)
        if last:
            out, out_means = call(
                last_kernel, "last", [VMEM] * 7, [((3, 2, 256, 128), jnp.bfloat16), ((3, 2, 256), F32)],
                [*small, table, room(6, 128, 256), pltpu.VMEM((3, 2, 256, 128), jnp.bfloat16), room(3, 2, 256), pltpu.SemaphoreType.DMA((3,))],
                out_specs=[HBM, HBM],
            )(shifts, code, vel, sums, from_odd, from_even, axes)
        elif wide:
            sums, odd, even = call(
                wide_middle_kernel, f"middle{step}", [VMEM] * 6, [rows(24), rows(42), rows(42)], [],
            )(sums, from_odd, from_even, more[0], joint_odd, joint_even)
            from_odd, from_even = swap(odd, even, "gy")
            shift, sums, odd, even = call(
                functools.partial(wide_shift_kernel, step), f"shift{step}", [VMEM] * 7,
                [table_shape, rows(24), rows(12), rows(12)], [*wide_small, moments, far, room(42, 256), room(42, 256)],
            )(shifts, sums, from_odd, from_even, axes, more[0], joints[step - 1])
        else:
            shift, sums, odd, even = call(
                functools.partial(shift_kernel, step), f"shift{step}", [VMEM] * 7,
                [table_shape, rows(24), rows(12), rows(12)], [*small, moments],
            )(shifts, sums, from_odd, from_even, axes, more[0], joints[step - 1])
    return out.reshape(velocity.shape), out_means.reshape(3, *occupancy.shape)


def solution(mesh):
    in_specs = (
        P(None, "gx", "gy", None, None),
        P("gx", "gy", None, None),
        P("gx", "gy", None),
        P(),
        P(None, "gx", "gy", None),
    )
    out_specs = (P(None, "gx", "gy", None, None), P(None, "gx", "gy", None))
    return jax.shard_map(
        on_device, mesh=mesh, in_specs=in_specs, out_specs=out_specs, check_vma=False
    )
```
